32 devices in a mesh: fsdp: 4 (over x, core), ctx: 8 (over z, y).
Axes of the slice: x: 2, y: 2, z: 4, core: 2. Of those that a mesh axis runs over, the one named last changes fastest.
Arguments:
- tokens: bfloat16 [8, 1024, 2048], P('fsdp', 'ctx'), may hold values from -6 to 6
- lengths: int32 [8], P('fsdp'), may hold values from 256 to 1024, as said below
- cotangent: bfloat16 [8, 1024, 2048], P('fsdp', 'ctx'), may hold values from -6 to 6
- attn_gain: bfloat16 [2048], P(('fsdp', 'ctx')), may hold values from 0.5 to 1.5
- w_query: bfloat16 [2048, 2048], P(('fsdp', 'ctx')), may hold values from -0.1875 to 0.1875
- w_key: bfloat16 [2048, 512], P(('fsdp', 'ctx')), may hold values from -0.1875 to 0.1875
- w_value: bfloat16 [2048, 512], P(('fsdp', 'ctx')), may hold values from -0.125 to 0.125
- w_out: bfloat16 [2048, 2048], P(('fsdp', 'ctx')), may hold values from -1 to 1
- mlp_gain: bfloat16 [2048], P(('fsdp', 'ctx')), may hold values from 0.5 to 1.5
- w_gate: bfloat16 [2048, 8192], P(('fsdp', 'ctx')), may hold values from -0.125 to 0.125
- w_up: bfloat16 [2048, 8192], P(('fsdp', 'ctx')), may hold values from -0.125 to 0.125
- w_down: bfloat16 [8192, 2048], P(('fsdp', 'ctx')), may hold values from -0.0625 to 0.0625
Outputs:
- layer_out: bfloat16 [8, 1024, 2048], P('fsdp', 'ctx')
- grad_tokens: bfloat16 [8, 1024, 2048], P('fsdp', 'ctx')
- grad_attn_gain: float32 [2048], P(('fsdp', 'ctx'))
- grad_w_query: float32 [2048, 2048], P(('fsdp', 'ctx'))
- grad_w_key: float32 [2048, 512], P(('fsdp', 'ctx'))
- grad_w_value: float32 [2048, 512], P(('fsdp', 'ctx'))
- grad_w_out: float32 [2048, 2048], P(('fsdp', 'ctx'))
- grad_mlp_gain: float32 [2048], P(('fsdp', 'ctx'))
- grad_w_gate: float32 [2048, 8192], P(('fsdp', 'ctx'))
- grad_w_up: float32 [2048, 8192], P(('fsdp', 'ctx'))
- grad_w_down: float32 [8192, 2048], P(('fsdp', 'ctx'))
The draws below stay inside these ranges and needn't reach their ends.
Inputs may be any that keep to these rules, and one draw needn't show every extreme that they name: `lengths`: valid tokens of each sequence, counted from its start; among the 2 sequences on one index of fsdp one has all 1024.
All inputs are finite; a program needn't handle non-finite values.
Results may differ from the reference program's by a relative error of at most 0.018.
Values may be sent and summed in bfloat16 or wider, within the bound.
A program may use at most 512 MiB of HBM per device.

```python
import jax
import jax.numpy as jnp
from jax import lax

D = 2048
HEADS = 32
KVH = 8
HD = 64
FF = 8192
SEQ_DEV = 2
LENGTH = 1024
SEQS = 8


def draw_lengths(key, part):
    key = jax.random.fold_in(key, 7)
    base_key, pick_key = jax.random.split(key)
    groups = SEQS // SEQ_DEV
    drawn_lengths = jax.random.randint(base_key, (SEQS,), LENGTH // 4, LENGTH + 1)
    chosen = jax.random.randint(pick_key, (groups,), 0, SEQ_DEV)
    member = jnp.arange(SEQS, dtype=jnp.int32) % SEQ_DEV
    full_one = member == jnp.repeat(chosen, SEQ_DEV)
    return jnp.where(full_one, LENGTH, drawn_lengths).astype(jnp.int32)


def strengthened(values, stream_key, source, target, shards_of, factor):
    owner, partner = [(jnp.arange(values.shape[position]) // (values.shape[position] // shards_of)).reshape([-1 if axis == position else 1 for axis in range(values.ndim)]) for position in (source, target)]
    chosen = jax.random.permutation(stream_key, shards_of)[partner]
    strong = (owner == chosen) | (owner == (partner + shards_of // 2) % shards_of)
    return jnp.where(strong, factor * values, values)


def block_levels(key, dims, cuts, smallest, largest):
    factor_of = 1.0
    for axis_at, parts in cuts:
        steps = jax.random.uniform(jax.random.fold_in(jax.random.fold_in(key, 6), axis_at), (parts,), jnp.float32, smallest / len(cuts), largest / len(cuts))
        factor_of = factor_of * jnp.repeat(jnp.exp(steps), dims[axis_at] // parts).reshape((-1,) + (1,) * (len(dims) - 1 - axis_at))
    return factor_of


def noise(stream_key, dims, width, most, cuts=(), held_as=jnp.bfloat16):
    gain = block_levels(stream_key, dims, cuts, -0.22, 0.18) if cuts else 1.0
    drawn = jax.random.normal(stream_key, dims, jnp.float32) * width * gain
    return jnp.minimum(jnp.maximum(drawn, -most), most).astype(held_as)


def gaussian_with(stream_key, shape, spread, reach, shards, heavy, held_as=jnp.bfloat16):
    values = spread * jax.random.normal(stream_key, shape, jnp.float32)
    if shards:
        values = values * block_levels(stream_key, shape, shards, -0.22, 0.18)
    return jnp.clip(strengthened(values, jax.random.fold_in(stream_key, 3), *heavy), -reach, reach).astype(held_as)


def setup_inputs(seed: int = 0) -> dict:
    splits = jax.random.split(jax.random.key(seed), 13)
    return {
        "tokens": noise(splits[0], (SEQS, LENGTH, D), 1.0, 6.0, ((0, 4), (1, 8))),
        "lengths": draw_lengths(jax.random.fold_in(splits[12], 71), 0),
        "cotangent": gaussian_with(splits[2], (SEQS, LENGTH, D), 1.0, 6.0, ((0, 4), (1, 8)), (1, 2, 8, 2.0)),
        "attn_gain": jnp.clip(1.0 + 0.1 * jax.random.normal(splits[3], (D,), jnp.float32), 0.5, 1.5).astype(jnp.bfloat16),
        "w_query": noise(splits[4], (D, D), (D // 2) ** -0.5, 0.1875, ((0, 32),)),
        "w_key": noise(splits[5], (D, KVH * HD), (D // 2) ** -0.5, 0.1875, ((0, 32),)),
        "w_value": noise(splits[6], (D, KVH * HD), D ** -0.5, 0.125, ((0, 32),)),
        "w_out": noise(splits[7], (D, D), (D // 64) ** -0.5, 1.0, ((0, 32),)),
        "mlp_gain": jnp.clip(1.0 + 0.1 * jax.random.normal(splits[8], (D,), jnp.float32), 0.5, 1.5).astype(jnp.bfloat16),
        "w_gate": noise(splits[9], (D, FF), D ** -0.5, 0.125, ((0, 32),)),
        "w_up": noise(splits[10], (D, FF), D ** -0.5, 0.125, ((0, 32),)),
        "w_down": noise(splits[11], (FF, D), FF ** -0.5, 0.0625, ((0, 32),)),
    }


EPSILON = 1e-05
NEGATIVE = -1e+30
HIGHEST = lax.Precision.HIGHEST

@jax.custom_vjp
def low(v):
    return lax.optimization_barrier(v.astype(jnp.bfloat16)).astype(jnp.float32)

@jax.custom_vjp
def low_back(v):
    return v

def low_keep(v):
    return (low(v), None)

def low_pass(kept, grad):
    return (grad,)

def back_keep(v):
    return (v, None)

def back_low(kept, grad):
    return (low(grad),)
low.defvjp(low_keep, low_pass)
low_back.defvjp(back_keep, back_low)

def rope_tables(positions, head_width):
    half_width = head_width // 2
    frequency = 500000.0 ** (-jnp.arange(half_width, dtype=jnp.float32) * 2.0 / head_width)
    angles = positions.astype(jnp.float32)[:, None] * frequency[None, :]
    return (jnp.cos(angles)[:, None, :], jnp.sin(angles)[:, None, :])

def rotate(field, cos_table, sin_table):
    half_width = field.shape[-1] // 2
    first_half = field[..., :half_width]
    second_half = field[..., half_width:]
    return jnp.concatenate([first_half * cos_table - second_half * sin_table, second_half * cos_table + first_half * sin_table], -1)

def matmul(left_side, right_side):
    return jnp.dot(left_side, right_side, precision=HIGHEST)

def rms_normed(field):
    return field * lax.rsqrt(lax.optimization_barrier(jnp.mean(field * field, -1, keepdims=True)) + EPSILON)

def attention(queries, keys, values, seq_len):
    row_count = queries.shape[0]
    block_rows = min(512, row_count)
    group_size = HEADS // KVH
    key_pos = jnp.arange(row_count, dtype=jnp.int32)

    def one_block(item):
        query_part, block_start = item
        grouped = query_part.reshape(block_rows, KVH, group_size, HD)
        raw_scores = jnp.einsum('qkgd,nkd->kgqn', grouped, keys, precision=HIGHEST)
        scores = low_back(raw_scores) * HD ** (-0.5)
        query_pos = block_start + jnp.arange(block_rows, dtype=jnp.int32)
        allowed = (key_pos[None, :] <= query_pos[:, None]) & (key_pos[None, :] < seq_len)
        masked = jnp.where(allowed[None, None], scores, NEGATIVE)
        row_top = lax.optimization_barrier(jnp.max(masked, -1, keepdims=True))
        log_total = row_top + jnp.log(lax.optimization_barrier(jnp.sum(jnp.exp(masked - row_top), -1, keepdims=True)))
        soft_low = low(jnp.exp(masked - log_total))
        result = jnp.einsum('kgqn,nkd->qkgd', soft_low, values, precision=HIGHEST)
        return result.reshape(block_rows, HEADS * HD)
    pieces = queries.reshape(row_count // block_rows, block_rows, HEADS, HD)
    starts = jnp.arange(row_count // block_rows, dtype=jnp.int32) * block_rows
    outputs = lax.map(jax.checkpoint(one_block), (pieces, starts))
    return outputs.reshape(row_count, HEADS * HD)

def layer(params, resid_in, seq_len):
    gain_one, query_w, key_w, value_w, out_w, gain_two, gate_w, up_w, down_w = params
    row_count = resid_in.shape[0]
    cos_table, sin_table = rope_tables(jnp.arange(row_count, dtype=jnp.int32), HD)
    hidden_one = low(rms_normed(resid_in) * gain_one)
    queries = low(rotate(low_back(matmul(hidden_one, query_w)).reshape(row_count, HEADS, HD), cos_table, sin_table))
    keys = low(rotate(low_back(matmul(hidden_one, key_w)).reshape(row_count, KVH, HD), cos_table, sin_table))
    values = low(low_back(matmul(hidden_one, value_w))).reshape(row_count, KVH, HD)
    attended = low(low_back(attention(queries, keys, values, seq_len)))
    resid_mid = resid_in + low_back(matmul(attended, out_w))
    hidden_two = low(rms_normed(resid_mid) * gain_two)
    gate_pre = low_back(matmul(hidden_two, gate_w))
    up_pre = low_back(matmul(hidden_two, up_w))
    mlp_inner = low(low_back(jax.nn.silu(gate_pre) * up_pre))
    return resid_mid + low_back(matmul(mlp_inner, down_w))

def reference(tokens, lengths, cotangent, attn_gain, w_query, w_key, w_value, w_out, mlp_gain, w_gate, w_up, w_down):
    params = (attn_gain.astype(jnp.float32), w_query.astype(jnp.float32), w_key.astype(jnp.float32), w_value.astype(jnp.float32), w_out.astype(jnp.float32), mlp_gain.astype(jnp.float32), w_gate.astype(jnp.float32), w_up.astype(jnp.float32), w_down.astype(jnp.float32))
    positions = jnp.arange(LENGTH, dtype=jnp.int32)

    def one_sequence(totals, item):
        seq_tokens, seq_len, seq_grad = item

        def forward(weights_in, field):
            return layer(weights_in, field, seq_len)
        result, pull = jax.vjp(forward, params, seq_tokens.astype(jnp.float32))
        valid = (positions < seq_len).astype(jnp.float32)
        weight_grads, input_grad = pull(seq_grad.astype(jnp.float32) * valid[:, None])
        totals = jax.tree.map(jnp.add, totals, weight_grads)
        return (totals, (result.astype(jnp.bfloat16), input_grad.astype(jnp.bfloat16)))
    zeros = jax.tree.map(jnp.zeros_like, params)
    totals, (outputs, input_grads) = lax.scan(one_sequence, zeros, (tokens, lengths, cotangent))
    return (outputs, input_grads, totals[0], totals[1], totals[2], totals[3], totals[4], totals[5], totals[6], totals[7], totals[8])
```

```python
import jax
import jax.numpy as jnp
from jax import lax
from jax.sharding import Mesh
from jax.sharding import PartitionSpec as P

HEADS = 32
KVH = 8
HD = 64
EPSILON = 1e-05
NEGATIVE = -1e30
BF = jnp.bfloat16
F32 = jnp.float32
GROUP = ("a", "core", "cl")


def rope_tables(positions, head_width):
    half_width = head_width // 2
    frequency = 500000.0 ** (-jnp.arange(half_width, dtype=F32) * 2.0 / head_width)
    angles = positions.astype(F32)[:, None] * frequency[None, :]
    return jnp.cos(angles), jnp.sin(angles)


def rotate(field, cos, sin):
    half = field.shape[-1] // 2
    u1, u2 = field[..., :half], field[..., half:]
    return jnp.concatenate([u1 * cos - u2 * sin, u2 * cos + u1 * sin], -1)


def rotate_back(field, cos, sin):
    return rotate(field, cos, -sin)


def rms_scale(field):
    return lax.rsqrt(jnp.mean(field * field, -1, keepdims=True) + EPSILON)


def norm_back(grad_normed, normed, scale_rows):
    return scale_rows * (grad_normed - normed * jnp.mean(grad_normed * normed, -1, keepdims=True))


def mm(a, b):
    return jnp.dot(a, b, preferred_element_type=F32)


def mm_tn(a, b):
    return jnp.einsum("rd,re->de", a, b, preferred_element_type=F32)


def mm_nt(a, b):
    return jnp.einsum("re,de->rd", a, b, preferred_element_type=F32)


def gather_group(x):
    return lax.all_gather(x, GROUP, axis=0, tiled=True)


def sum_group(x):
    return lax.psum_scatter(x.astype(BF), GROUP, scatter_dimension=0, tiled=True).astype(F32)


def swap_group(x):
    return lax.all_to_all(x, GROUP, 0, 0, tiled=True)


def rows_of(x):
    nz = lax.axis_size("cm")
    x = lax.all_gather(x, "cm", axis=0)
    _, _, r, c = x.shape
    return x.reshape(nz, 4, 2, r, c).transpose(1, 0, 2, 3, 4).reshape(nz * 8 * r, c)


def rows_to(g):
    nz = lax.axis_size("cm")
    rows, c = g.shape
    r = rows // (8 * nz)
    g = g.astype(BF).reshape(4, nz, 2, r, c).transpose(1, 0, 2, 3, 4).reshape(nz * 8, r, c)
    g = lax.psum_scatter(g, "cm", scatter_dimension=0, tiled=True)
    return swap_group(g)


def on_device(
    tokens, lengths, cotangent, attn_gain, w_query, w_key, w_value, w_out, mlp_gain, w_gate, w_up, w_down
):
    seqs, block, width = tokens.shape
    nz = lax.axis_size("cm")
    rows = seqs * block
    r = w_query.shape[0]
    fb = w_down.shape[0]
    nseq = 4 * seqs
    slots = 2 * block
    length = slots * nz
    qh = HEADS // 8
    scale = HD ** (-0.5)
    cm = lax.axis_index("cm")
    cl = lax.axis_index("cl")

    gains = jnp.stack([attn_gain, mlp_gain], -1)
    gains = jnp.pad(gains, ((0, 0), (0, 126)))
    pack = jnp.concatenate(
        [
            w_query.reshape(r, 8, qh * HD),
            w_key.reshape(r, 8, HD),
            w_value.reshape(r, 8, HD),
            jnp.broadcast_to(gains[:, None], (r, 8, 128)),
        ],
        -1,
    ).transpose(1, 0, 2)
    pack = rows_of(swap_group(pack))
    wqkv = pack[:, : qh * HD + 2 * HD]
    gain_one = pack[:, qh * HD + 2 * HD].astype(F32)
    gain_two = pack[:, qh * HD + 2 * HD + 1].astype(F32)
    perm = [(c, (c % nz) * 2 + c // nz) for c in range(2 * nz)]
    wo = lax.all_gather(lax.ppermute(w_out, ("cm", "cl"), perm), "cm", axis=0, tiled=True)

    def ff_cols(w):
        w = w.reshape(r, 4, nz, 2, fb).transpose(1, 3, 0, 2, 4).reshape(8, r, nz * fb)
        return rows_of(swap_group(w))

    wg = ff_cols(w_gate)
    wu = ff_cols(w_up)
    wd = lax.all_gather(w_down, "cm", axis=0, tiled=True)
    lens = lax.all_gather(lengths, ("a", "core"), axis=0, tiled=True)

    own = tokens.reshape(rows, width)
    resid_in = own.astype(F32)
    tok_all = gather_group(own)
    tok_f = tok_all.astype(F32)
    hidden_one = (tok_f * rms_scale(tok_f) * gain_one).astype(BF)

    def by_seq(x):
        e = x.shape[-1]
        return x.reshape(4, 2, seqs, block, e).transpose(0, 2, 1, 3, 4).reshape(nseq, slots, e)

    def by_row(x):
        e = x.shape[-1]
        return x.reshape(4, seqs, 2, block, e).transpose(0, 2, 1, 3, 4).reshape(8 * rows, e)

    pos = cm * slots + jnp.arange(slots, dtype=jnp.int32)
    cos, sin = rope_tables(pos, HD)
    qkv = by_seq(mm(hidden_one, wqkv))
    q = qkv[..., : qh * HD].reshape(nseq, slots, qh, HD).transpose(0, 2, 1, 3)
    q = rotate(q, cos, sin).astype(BF)
    k = rotate(qkv[..., qh * HD : qh * HD + HD], cos, sin).astype(BF)
    v = qkv[..., qh * HD + HD :].astype(BF)
    kv = lax.all_gather(jnp.concatenate([k, v], -1), "cm", axis=1, tiled=True)
    keys, values = kv[..., :HD], kv[..., HD:]
    key_pos = jnp.arange(length, dtype=jnp.int32)
    allowed = (key_pos[None, None, :] <= pos[None, :, None]) & (key_pos[None, None, :] < lens[:, None, None])
    scores = jnp.einsum("shqd,snd->shqn", q, keys, preferred_element_type=F32) * scale
    scores = jnp.where(allowed[:, None], scores, NEGATIVE)
    top = jnp.max(scores, -1, keepdims=True)
    log_total = top + jnp.log(jnp.sum(jnp.exp(scores - top), -1, keepdims=True))
    soft = jnp.exp(scores - log_total)
    probs = soft.astype(BF)
    attended = jnp.einsum("shqn,snd->shqd", probs, values, preferred_element_type=F32)
    attended_low = by_row(attended.astype(BF).transpose(0, 2, 1, 3).reshape(nseq, slots, qh * HD))

    resid_mid = resid_in + sum_group(mm(attended_low, wo))
    scale_two = rms_scale(resid_mid)
    normed_two = resid_mid * scale_two
    hidden_two = gather_group((normed_two * gain_two).astype(BF))
    gate_pre = mm(hidden_two, wg)
    up_pre = mm(hidden_two, wu)
    sig = jax.nn.sigmoid(gate_pre)
    act = gate_pre * sig
    inner = (act * up_pre).astype(BF)
    layer_out = (resid_mid + sum_group(mm(inner, wd))).astype(BF)

    own_pos = cm * slots + cl * block + jnp.arange(block, dtype=jnp.int32)
    valid = (own_pos[None, :] < lengths[:, None]).astype(F32)
    grad_out = (cotangent.astype(F32) * valid[..., None]).reshape(rows, width)
    grad_low = gather_group(grad_out.astype(BF))
    grad_wd = lax.psum_scatter(mm_tn(inner, grad_low).astype(BF), "cm", scatter_dimension=0, tiled=True)
    grad_inner = mm_nt(grad_low, wd).astype(BF).astype(F32)
    grad_gate = (grad_inner * up_pre * (sig * (1.0 + gate_pre * (1.0 - sig)))).astype(BF)
    grad_up = (grad_inner * act).astype(BF)

    def ff_back(g):
        g = rows_to(g)
        return g.reshape(4, 2, r, nz, fb).transpose(2, 0, 3, 1, 4).reshape(r, 8 * nz * fb).astype(F32)

    grad_wg = ff_back(mm_tn(hidden_two, grad_gate))
    grad_wu = ff_back(mm_tn(hidden_two, grad_up))
    grad_hidden_two = sum_group(mm_nt(grad_gate, wg) + mm_nt(grad_up, wu))
    gain_grad_two = jnp.sum(grad_wg * w_gate.astype(F32) + grad_wu * w_up.astype(F32), -1) / mlp_gain.astype(F32)
    grad_mid = grad_out + norm_back(grad_hidden_two * gain_two, normed_two, scale_two)
    grad_attn = gather_group(grad_mid.astype(BF))
    grad_wo = lax.psum_scatter(mm_tn(attended_low, grad_attn).astype(BF), "cm", scatter_dimension=0, tiled=True)
    grad_wo = lax.ppermute(grad_wo, ("cm", "cl"), [(t, s) for s, t in perm]).astype(F32)
    grad_heads = by_seq(mm_nt(grad_attn, wo).astype(BF)).reshape(nseq, slots, qh, HD).transpose(0, 2, 1, 3)
    delta = jnp.sum(grad_heads.astype(F32) * attended, -1, keepdims=True)
    grad_soft = jnp.einsum("shqd,snd->shqn", grad_heads, values, preferred_element_type=F32)
    grad_scores = (scale * soft * (grad_soft - delta)).astype(BF)
    grad_q = jnp.einsum("shqn,snd->shqd", grad_scores, keys, preferred_element_type=F32)
    grad_k = jnp.einsum("shqn,shqd->snd", grad_scores, q, preferred_element_type=F32)
    grad_v = jnp.einsum("shqn,shqd->snd", probs, grad_heads, preferred_element_type=F32)
    grad_kv = jnp.concatenate([grad_k, grad_v], -1).astype(BF)
    grad_kv = lax.psum_scatter(grad_kv, "cm", scatter_dimension=1, tiled=True).astype(F32)
    grad_rows = by_row(
        jnp.concatenate(
            [
                rotate_back(grad_q, cos, sin).transpose(0, 2, 1, 3).reshape(nseq, slots, qh * HD).astype(BF),
                rotate_back(grad_kv[..., :HD], cos, sin).astype(BF),
                grad_kv[..., HD:].astype(BF),
            ],
            -1,
        )
    )
    back = rows_to(mm_tn(hidden_one, grad_rows))
    back = back.transpose(1, 0, 2).astype(F32)
    grad_wq = back[..., : qh * HD].reshape(r, HEADS * HD)
    grad_wk = back[..., qh * HD : qh * HD + HD].reshape(r, KVH * HD)
    grad_wv = back[..., qh * HD + HD :].reshape(r, KVH * HD)
    gain_grad_one = (
        jnp.sum(grad_wq * w_query.astype(F32), -1)
        + jnp.sum(grad_wk * w_key.astype(F32), -1)
        + jnp.sum(grad_wv * w_value.astype(F32), -1)
    ) / attn_gain.astype(F32)
    grad_hidden_one = sum_group(mm_nt(grad_rows, wqkv))
    scale_one = rms_scale(resid_in)
    grad_tokens = grad_mid + norm_back(grad_hidden_one * gain_one, resid_in * scale_one, scale_one)
    return (
        layer_out.reshape(seqs, block, width),
        grad_tokens.reshape(seqs, block, width).astype(BF),
        gain_grad_one,
        grad_wq,
        grad_wk,
        grad_wv,
        grad_wo,
        gain_grad_two,
        grad_wg,
        grad_wu,
        grad_wd.astype(F32),
    )


def solution(mesh):
    fsdp, ctx = mesh.devices.shape
    fine = Mesh(mesh.devices.reshape(fsdp // 2, 2, ctx // 2, 2), ("a", "core", "cm", "cl"))
    token = P(("a", "core"), ("cm", "cl"), None)
    vector = P(("a", "core", "cm", "cl"))
    matrix = P(("a", "core", "cm", "cl"), None)
    return jax.shard_map(
        on_device,
        mesh=fine,
        in_specs=(
            token,
            P(("a", "core")),
            token,
            vector,
            matrix,
            matrix,
            matrix,
            matrix,
            vector,
            matrix,
            matrix,
            matrix,
        ),
        out_specs=(token, token, vector, matrix, matrix, matrix, matrix, vector, matrix, matrix, matrix),
        check_vma=False,
    )
```

```python
import functools

import jax
import jax.numpy as jnp
from jax import lax
from jax.experimental import pallas as pl
from jax.experimental.pallas import tpu as pltpu
from jax.sharding import Mesh
from jax.sharding import PartitionSpec as P

HEADS = 32
KVH = 8
HD = 64
EPSILON = 1e-05
NEGATIVE = -1e30
BF = jnp.bfloat16
F32 = jnp.float32
GROUP = ("a", "core", "cl")


TILE = 32
MESH = pl.DeviceIdType.MESH

def places():
    a, core, cl = (lax.axis_index(n) for n in ("a", "core", "cl"))
    return a, core, cl

def index_of(a, core, cl):
    return (a * 2 + core) * 2 + cl

def meet(names):
    barrier = pltpu.get_barrier_semaphore()
    for name in names:
        pl.semaphore_signal(barrier, inc=1, device_id={name: 1 - lax.axis_index(name)}, device_id_type=MESH)
    pl.semaphore_wait(barrier, len(names))

def remote(src, dst, send, recv, name):
    return pltpu.make_async_remote_copy(
        src_ref=src, dst_ref=dst, send_sem=send, recv_sem=recv,
        device_id={name: 1 - lax.axis_index(name)}, device_id_type=MESH)

def gather_kernel(x_ref, *refs):
    o_ref, local, ss, rs = refs[-4:]
    a, core, cl = places()
    half = x_ref.shape[0] // 2
    lo, hi = pl.ds(0, half), pl.ds(half, half)
    me = index_of(a, core, cl)
    sx = index_of(1 - a, core, cl)
    sy = index_of(a, core, 1 - cl)
    sd = index_of(1 - a, core, 1 - cl)
    meet(("a", "core", "cl"))
    mine = pltpu.make_async_copy(x_ref, o_ref.at[me], local)
    def put(i, slot, part, name, src=None):
        src = o_ref.at[slot, part] if src is None else src
        return remote(src, o_ref.at[slot, part], ss.at[i], rs.at[i], name)
    x0 = put(0, me, lo, "a", x_ref.at[lo])
    y0 = put(1, me, hi, "cl", x_ref.at[hi])
    x1 = put(2, me, hi, "a", x_ref.at[hi])
    y1 = put(3, me, lo, "cl", x_ref.at[lo])
    c0 = put(4, me, pl.ds(0, 2 * half), "core", x_ref)
    for c in (x0, y0, x1, y1, c0, mine):
        c.start()
    def got(i, slot, part, name):
        return put(i, slot, part, name)
    fx0 = got(0, sx, lo, "a")
    fx0.wait_recv()
    y2 = put(5, sx, lo, "cl")
    y2.start()
    k0 = put(6, sx, lo, "core")
    k0.start()
    fy0 = got(1, sy, hi, "cl")
    fy0.wait_recv()
    x2 = put(7, sy, hi, "a")
    x2.start()
    k1 = put(8, sy, hi, "core")
    k1.start()
    got(2, sx, hi, "a").wait_recv()
    k2 = put(9, sx, hi, "core")
    k2.start()
    got(3, sy, lo, "cl").wait_recv()
    k3 = put(10, sy, lo, "core")
    k3.start()
    got(5, sd, lo, "cl").wait_recv()
    k4 = put(11, sd, lo, "core")
    k4.start()
    got(7, sd, hi, "a").wait_recv()
    k5 = put(12, sd, hi, "core")
    k5.start()
    def other(slot):
        return slot + 2 - 4 * core
    got(4, other(me), pl.ds(0, 2 * half), "core").wait_recv()
    for i, slot, part in ((6, sx, lo), (8, sy, hi), (9, sx, hi), (10, sy, lo), (11, sd, lo), (12, sd, hi)):
        got(i, other(slot), part, "core").wait_recv()
    for c in (x0, y0, x1, y1, c0, y2, k0, x2, k1, k2, k3, k4, k5):
        c.wait_send()
    mine.wait()

def plane_gather(x, cid, deps=()):
    rows, cols = x.shape
    out = pl.pallas_call(
        gather_kernel,
        out_shape=jax.ShapeDtypeStruct((8, rows, cols), x.dtype),
        in_specs=[pl.BlockSpec(memory_space=pl.ANY)] * (1 + len(deps)),
        out_specs=pl.BlockSpec(memory_space=pl.ANY),
        scratch_shapes=[pltpu.SemaphoreType.DMA, pltpu.SemaphoreType.DMA((13,)), pltpu.SemaphoreType.DMA((13,))],
        compiler_params=pltpu.CompilerParams(collective_id=cid, has_side_effects=True),
        name=f"gather{cid}",
    )(x, *deps)
    return out.reshape(8 * rows, cols)


def sum_kernel(x_ref, *refs):
    o_ref, mine, theirs, first, last, osem, lsem, cs, cr, ss, rs = refs[-11:]
    a, core, cl = places()
    rows = x_ref.shape[1]
    half = rows // 2
    lo, hi = pl.ds(0, half), pl.ds(half, half)
    chips = ((a, cl), (1 - a, cl), (a, 1 - cl), (1 - a, 1 - cl))
    meet(("a", "core", "cl"))
    order = (3, 1, 2, 0)
    out, loc = {}, {}
    for p in order:
        ca, cc = chips[p]
        out[p] = remote(x_ref.at[index_of(ca, 1 - core, cc)], theirs.at[p], cs.at[p], cr.at[p], "core")
        out[p].start()
        loc[p] = pltpu.make_async_copy(x_ref.at[index_of(ca, core, cc)], mine.at[p], lsem.at[p])
        loc[p].start()

    def add(dst, src_list, n):
        @pl.loop(0, n // TILE)
        def _(i):
            part = pl.ds(pl.multiple_of(i * TILE, TILE), TILE)
            total = src_list[0][part, :].astype(F32)
            for s in src_list[1:]:
                total = total + s[part, :].astype(F32)
            dst[part, :] = total.astype(dst.dtype)

    def chip_sum(p):
        out[p].wait_recv()
        loc[p].wait()
        add(mine.at[p], (mine.at[p], theirs.at[p]), rows)

    chip_sum(3)
    xd = remote(mine.at[3, lo], first.at[0], ss.at[0], rs.at[0], "a")
    yd = remote(mine.at[3, hi], first.at[1], ss.at[1], rs.at[1], "cl")
    xd.start()
    yd.start()
    chip_sum(1)
    xo = remote(mine.at[1, lo], first.at[2], ss.at[2], rs.at[2], "a")
    xo.start()
    chip_sum(2)
    yo = remote(mine.at[2, hi], first.at[3], ss.at[3], rs.at[3], "cl")
    yo.start()
    chip_sum(0)
    xd.wait_recv()
    add(mine.at[2, lo], (mine.at[2, lo], first.at[0]), half)
    y2 = remote(mine.at[2, lo], last.at[0], ss.at[4], rs.at[4], "cl")
    y2.start()
    yd.wait_recv()
    add(mine.at[1, hi], (mine.at[1, hi], first.at[1]), half)
    x2 = remote(mine.at[1, hi], last.at[1], ss.at[5], rs.at[5], "a")
    x2.start()
    xo.wait_recv()
    add(mine.at[0, lo], (mine.at[0, lo], first.at[2]), half)
    yo.wait_recv()
    add(mine.at[0, hi], (mine.at[0, hi], first.at[3]), half)
    y2.wait_recv()
    add(mine.at[0, lo], (mine.at[0, lo], last.at[0]), half)
    x2.wait_recv()
    add(mine.at[0, hi], (mine.at[0, hi], last.at[1]), half)
    done = pltpu.make_async_copy(mine.at[0], o_ref, osem)
    done.start()
    for c in (*out.values(), xd, yd, xo, yo, y2, x2):
        c.wait_send()
    done.wait()

def plane_sum(x, cid, deps=()):
    total, cols = x.shape
    rows = total // 8
    half = rows // 2
    return pl.pallas_call(
        sum_kernel,
        out_shape=jax.ShapeDtypeStruct((rows, cols), x.dtype),
        in_specs=[pl.BlockSpec(memory_space=pl.ANY)] * (1 + len(deps)),
        out_specs=pl.BlockSpec(memory_space=pl.ANY),
        scratch_shapes=[
            pltpu.VMEM((4, rows, cols), x.dtype),
            pltpu.VMEM((4, rows, cols), x.dtype),
            pltpu.VMEM((4, half, cols), x.dtype),
            pltpu.VMEM((2, half, cols), x.dtype),
            pltpu.SemaphoreType.DMA,
            pltpu.SemaphoreType.DMA((4,)),
            pltpu.SemaphoreType.DMA((4,)),
            pltpu.SemaphoreType.DMA((4,)),
            pltpu.SemaphoreType.DMA((6,)),
            pltpu.SemaphoreType.DMA((6,)),
        ],
        compiler_params=pltpu.CompilerParams(collective_id=cid, has_side_effects=True, vmem_limit_bytes=40 * 2**20),
        name=f"sum{cid}",
    )(x.reshape(8, rows, cols), *deps)


def partners():
    a, core, cl = places()
    out = []
    for t in range(1, 8):
        at = (a ^ (t >> 2), core ^ ((t >> 1) & 1), cl ^ (t & 1))
        out.append((dict(zip(GROUP, at)), index_of(*at)))
    return out


def columns(ref, i, width):
    return ref.at[:, pl.ds(pl.multiple_of(i * width, width), width)]


def moved_to(c, nz):
    return lax.rem(c, nz), c // nz


def moved_from(c, nz):
    block = lax.rem(c, 2) * nz + c // 2
    return block // 2, lax.rem(block, 2)


def swap_kernel(kinds, nz, *refs):
    n = len(kinds)
    ins, outs, (lsem, ss, rs) = refs[:n], refs[-3 - n : -3], refs[-3:]
    me = index_of(*places())
    others = partners()
    moving = [k for k, (kind, _) in enumerate(kinds) if kind in ("move", "home")]
    barrier = pltpu.get_barrier_semaphore()
    for device, _ in others:
        pl.semaphore_signal(barrier, inc=1, device_id=device, device_id_type=MESH)
    if moving:
        here = lax.axis_index("cm") * 2 + lax.axis_index("cl")
        pair = [dict(zip(("cm", "cl"), f(here, nz))) for f in (moved_to, moved_from)]
        if kinds[moving[0]][0] == "home":
            pair.reverse()
        stays = pair[0]["cm"] * 2 + pair[0]["cl"] == here

        @pl.when(jnp.logical_not(stays))
        def _():
            for device in pair:
                pl.semaphore_signal(barrier, inc=1, device_id=device, device_id_type=MESH)
            pl.semaphore_wait(barrier, len(others) + 2)

        @pl.when(stays)
        def _():
            pl.semaphore_wait(barrier, len(others))

    else:
        pl.semaphore_wait(barrier, len(others))
    copies = []
    for k, (kind, pieces) in enumerate(kinds):
        if kind in ("move", "home"):
            mine = pltpu.make_async_copy(ins[k], outs[k], lsem.at[k, 0])
            away = pltpu.make_async_remote_copy(
                src_ref=ins[k],
                dst_ref=outs[k],
                send_sem=ss.at[k, 0, 0],
                recv_sem=rs.at[k, 0, 0],
                device_id=pair[0],
                device_id_type=MESH,
            )
            pl.when(stays)(mine.start)
            pl.when(jnp.logical_not(stays))(away.start)
            continue
        for p in range(pieces):

            def block(f, k=k, kind=kind, pieces=pieces, p=p):
                i = ((f // 2) * pieces + p) * 2 + lax.rem(f, 2) if pieces > 1 else f
                return i

            width = (outs[k] if kind == "cols" else ins[k]).shape[-1] // pieces

            def part(ref, i, p=p, width=width, pieces=pieces):
                return ref.at[i] if pieces == 1 else ref.at[i, :, pl.ds(p * width, width)]

            def source(f):
                return columns(ins[k], block(f), width) if kind == "cols" else part(ins[k], f)

            target = columns(outs[k], block(me), width) if kind == "back" else part(outs[k], me)
            for t, (device, index) in enumerate(others):
                copy = pltpu.make_async_remote_copy(
                    src_ref=source(index),
                    dst_ref=target,
                    send_sem=ss.at[k, p, t],
                    recv_sem=rs.at[k, p, t],
                    device_id=device,
                    device_id_type=MESH,
                )
                copy.start()
                copies.append(copy)
            mine = pltpu.make_async_copy(source(me), target, lsem.at[k, p])
            mine.start()
            copies.append(mine)
    for copy in copies:
        copy.wait()
    for k in moving:
        mine = pltpu.make_async_copy(ins[k], outs[k], lsem.at[k, 0])
        away = pltpu.make_async_remote_copy(
            src_ref=ins[k],
            dst_ref=outs[k],
            send_sem=ss.at[k, 0, 0],
            recv_sem=rs.at[k, 0, 0],
            device_id=pair[0],
            device_id_type=MESH,
        )
        pl.when(stays)(mine.wait)
        pl.when(jnp.logical_not(stays))(away.wait)


def after(x, deps):
    return pl.pallas_call(
        lambda *refs: None,
        out_shape=jax.ShapeDtypeStruct(x.shape, x.dtype),
        in_specs=[pl.BlockSpec(memory_space=pl.ANY)] * (1 + len(deps)),
        out_specs=pl.BlockSpec(memory_space=pl.ANY),
        input_output_aliases={0: 0},
    )(x, *deps)


def plane_swap(kinds, arrays, cid, deps=()):
    shapes = []
    most = max(pieces for _, pieces in kinds)
    for (kind, _), x in zip(kinds, arrays):
        if kind == "cols":
            shape = (8, x.shape[0], x.shape[1] // 8)
        elif kind == "back":
            shape = (x.shape[1], 8 * x.shape[2])
        else:
            shape = x.shape
        shapes.append(jax.ShapeDtypeStruct(shape, x.dtype))
    n = len(kinds)
    return pl.pallas_call(
        functools.partial(swap_kernel, kinds, lax.axis_size("cm")),
        out_shape=shapes,
        in_specs=[pl.BlockSpec(memory_space=pl.ANY)] * (n + len(deps)),
        out_specs=[pl.BlockSpec(memory_space=pl.ANY)] * n,
        scratch_shapes=[
            pltpu.SemaphoreType.DMA((n, most)),
            pltpu.SemaphoreType.DMA((n, most, 7)),
            pltpu.SemaphoreType.DMA((n, most, 7)),
        ],
        compiler_params=pltpu.CompilerParams(collective_id=cid, has_side_effects=True),
        name=f"swap{cid}",
    )(*arrays, *deps)


def rope_tables(positions, head_width):
    half_width = head_width // 2
    frequency = 500000.0 ** (-jnp.arange(half_width, dtype=F32) * 2.0 / head_width)
    angles = positions.astype(F32)[:, None] * frequency[None, :]
    return jnp.cos(angles), jnp.sin(angles)


def rotate(field, cos, sin):
    half = field.shape[-1] // 2
    u1, u2 = field[..., :half], field[..., half:]
    return jnp.concatenate([u1 * cos - u2 * sin, u2 * cos + u1 * sin], -1)


def rotate_back(field, cos, sin):
    return rotate(field, cos, -sin)


def rms_scale(field):
    return lax.rsqrt(jnp.mean(field * field, -1, keepdims=True) + EPSILON)


def norm_back(grad_normed, normed, scale_rows):
    return scale_rows * (grad_normed - normed * jnp.mean(grad_normed * normed, -1, keepdims=True))


def mm(a, b):
    return jnp.dot(a, b, preferred_element_type=F32)


def mm_tn(a, b):
    return jnp.einsum("rd,re->de", a, b, preferred_element_type=F32)


def mm_nt(a, b):
    return jnp.einsum("re,de->rd", a, b, preferred_element_type=F32)


def rows_of(x):
    nz = lax.axis_size("cm")
    x = lax.all_gather(x, "cm", axis=0)
    _, _, r, c = x.shape
    return x.reshape(nz, 4, 2, r, c).transpose(1, 0, 2, 3, 4).reshape(nz * 8 * r, c)


def sum_planes(g):
    return lax.psum_scatter(g, "cm", scatter_dimension=0, tiled=True)


def rows_first(g):
    nz = lax.axis_size("cm")
    rows, c = g.shape
    r = rows // (8 * nz)
    return g.astype(BF).reshape(4, nz, 2, r, c).transpose(1, 0, 2, 3, 4).reshape(nz * 8, r, c)


def on_device(
    tokens, lengths, cotangent, attn_gain, w_query, w_key, w_value, w_out, mlp_gain, w_gate, w_up, w_down
):
    seqs, block, width = tokens.shape
    nz = lax.axis_size("cm")
    rows = seqs * block
    r = w_query.shape[0]
    nseq = 4 * seqs
    slots = 2 * block
    length = slots * nz
    qh = HEADS // 8
    scale = HD ** (-0.5)
    cm = lax.axis_index("cm")
    cl = lax.axis_index("cl")

    gains = jnp.stack([attn_gain, mlp_gain], -1)
    gains = jnp.pad(gains, ((0, 0), (0, 126)))
    pack = jnp.concatenate(
        [
            w_query.reshape(r, 8, qh * HD),
            w_key.reshape(r, 8, HD),
            w_value.reshape(r, 8, HD),
            jnp.broadcast_to(gains[:, None], (r, 8, 128)),
        ],
        -1,
    ).transpose(1, 0, 2)
    (pack,) = plane_swap((("slab", 1),), (pack,), 9)
    pack = rows_of(pack)
    wqkv = pack[:, : qh * HD + 2 * HD]
    gain_one = pack[:, qh * HD + 2 * HD].astype(F32)
    gain_two = pack[:, qh * HD + 2 * HD + 1].astype(F32)
    pieces = nz if w_down.shape[0] % 128 == 0 else 1
    perm = [(c, (c % nz) * 2 + c // nz) for c in range(2 * nz)]
    home = [(t, s) for s, t in perm]
    wd_home = w_down if pieces > 1 else lax.ppermute(w_down, ("cm", "cl"), perm)
    wg, wo_home = plane_swap((("cols", pieces), ("move", 1)), (w_gate, w_out), 10)
    wg = rows_of(wg)
    lens = lax.all_gather(lengths, ("a", "core"), axis=0, tiled=True)

    own = tokens.reshape(rows, width)
    resid_in = own.astype(F32)
    tok_all = plane_gather(own, 1)
    tok_f = tok_all.astype(F32)
    hidden_one = (tok_f * rms_scale(tok_f) * gain_one).astype(BF)

    def by_seq(x):
        e = x.shape[-1]
        return x.reshape(4, 2, seqs, block, e).transpose(0, 2, 1, 3, 4).reshape(nseq, slots, e)

    def by_row(x):
        e = x.shape[-1]
        return x.reshape(4, seqs, 2, block, e).transpose(0, 2, 1, 3, 4).reshape(8 * rows, e)

    pos = cm * slots + jnp.arange(slots, dtype=jnp.int32)
    cos, sin = rope_tables(pos, HD)
    qkv = by_seq(mm(hidden_one, wqkv))
    q = qkv[..., : qh * HD].reshape(nseq, slots, qh, HD).transpose(0, 2, 1, 3)
    q = rotate(q, cos, sin).astype(BF)
    k = rotate(qkv[..., qh * HD : qh * HD + HD], cos, sin).astype(BF)
    v = qkv[..., qh * HD + HD :].astype(BF)
    kv = lax.all_gather(jnp.concatenate([k, v], -1), "cm", axis=1, tiled=True)
    keys, values = kv[..., :HD], kv[..., HD:]
    (wu,) = plane_swap((("cols", pieces),), (w_up,), 13, (k, v))
    wo = lax.all_gather(wo_home, "cm", axis=0, tiled=True)
    wu = rows_of(wu)
    wd = lax.all_gather(wd_home, "cm", axis=0, tiled=True)
    key_pos = jnp.arange(length, dtype=jnp.int32)
    allowed = (key_pos[None, None, :] <= pos[None, :, None]) & (key_pos[None, None, :] < lens[:, None, None])
    scores = jnp.einsum("shqd,snd->shqn", q, keys, preferred_element_type=F32) * scale
    scores = jnp.where(allowed[:, None], scores, NEGATIVE)
    top = jnp.max(scores, -1, keepdims=True)
    log_total = top + jnp.log(jnp.sum(jnp.exp(scores - top), -1, keepdims=True))
    soft = jnp.exp(scores - log_total)
    probs = soft.astype(BF)
    attended = jnp.einsum("shqn,snd->shqd", probs, values, preferred_element_type=F32)
    attended_low = by_row(attended.astype(BF).transpose(0, 2, 1, 3).reshape(nseq, slots, qh * HD))

    resid_mid = resid_in + plane_sum(mm(attended_low, wo).astype(BF), 5).astype(F32)
    scale_two = rms_scale(resid_mid)
    normed_two = resid_mid * scale_two
    hidden_two = plane_gather((normed_two * gain_two).astype(BF), 2)
    gate_pre = mm(hidden_two, wg)
    up_pre = mm(hidden_two, wu)
    sig = jax.nn.sigmoid(gate_pre)
    act = gate_pre * sig
    inner = (act * up_pre).astype(BF)
    layer_out = (resid_mid + plane_sum(mm(inner, wd).astype(BF), 6).astype(F32)).astype(BF)

    own_pos = cm * slots + cl * block + jnp.arange(block, dtype=jnp.int32)
    valid = (own_pos[None, :] < lengths[:, None]).astype(F32)
    grad_out = (cotangent.astype(F32) * valid[..., None]).reshape(rows, width)
    grad_low = plane_gather(grad_out.astype(BF), 3, (k, v))
    grad_wd = mm_tn(inner, grad_low).astype(BF)
    grad_inner = mm_nt(grad_low, wd).astype(BF).astype(F32)
    grad_gate = (grad_inner * up_pre * (sig * (1.0 + gate_pre * (1.0 - sig)))).astype(BF)
    grad_up = (grad_inner * act).astype(BF)

    grad_wg = rows_first(mm_tn(hidden_two, grad_gate))
    grad_wu = rows_first(mm_tn(hidden_two, grad_up))
    grad_hidden_two = plane_sum(
        (mm_nt(grad_gate, wg) + mm_nt(grad_up, wu)).astype(BF), 7, (grad_wd, grad_wg, grad_wu)
    ).astype(F32)
    grad_wd, grad_wu, grad_wg = sum_planes(grad_wd), sum_planes(grad_wu), sum_planes(grad_wg)
    ff_sums = (grad_wd, grad_wu, grad_wg)
    if pieces == 1:
        grad_wd = lax.ppermute(grad_wd, ("cm", "cl"), home)
    grad_wg, grad_wu = plane_swap((("back", pieces),) * 2, (grad_wg, grad_wu), 11)
    grad_wg, grad_wu = grad_wg.astype(F32), grad_wu.astype(F32)
    gain_grad_two = jnp.sum(grad_wg * w_gate.astype(F32) + grad_wu * w_up.astype(F32), -1) / mlp_gain.astype(F32)
    grad_mid = grad_out + norm_back(grad_hidden_two * gain_two, normed_two, scale_two)
    grad_attn = plane_gather(grad_mid.astype(BF), 4)
    grad_wo = mm_tn(attended_low, grad_attn).astype(BF)
    grad_heads = by_seq(mm_nt(grad_attn, wo).astype(BF)).reshape(nseq, slots, qh, HD).transpose(0, 2, 1, 3)
    delta = jnp.sum(grad_heads.astype(F32) * attended, -1, keepdims=True)
    grad_soft = jnp.einsum("shqd,snd->shqn", grad_heads, values, preferred_element_type=F32)
    grad_scores = (scale * soft * (grad_soft - delta)).astype(BF)
    grad_q = jnp.einsum("shqn,snd->shqd", grad_scores, keys, preferred_element_type=F32)
    grad_k = jnp.einsum("shqn,shqd->snd", grad_scores, q, preferred_element_type=F32)
    grad_v = jnp.einsum("shqn,shqd->snd", probs, grad_heads, preferred_element_type=F32)
    grad_kv = jnp.concatenate([grad_k, grad_v], -1).astype(BF)
    grad_kv = lax.psum_scatter(after(grad_kv, ff_sums), "cm", scatter_dimension=1, tiled=True)
    grad_wo = sum_planes(after(grad_wo, (grad_kv,)))
    grad_kv = grad_kv.astype(F32)
    grad_rows = by_row(
        jnp.concatenate(
            [
                rotate_back(grad_q, cos, sin).transpose(0, 2, 1, 3).reshape(nseq, slots, qh * HD).astype(BF),
                rotate_back(grad_kv[..., :HD], cos, sin).astype(BF),
                grad_kv[..., HD:].astype(BF),
            ],
            -1,
        )
    )
    back = sum_planes(rows_first(mm_tn(hidden_one, grad_rows)))
    back, grad_wo = plane_swap((("slab", 1), ("home", 1)), (back, grad_wo), 12)
    back = back.transpose(1, 0, 2).astype(F32)
    grad_wq = back[..., : qh * HD].reshape(r, HEADS * HD)
    grad_wk = back[..., qh * HD : qh * HD + HD].reshape(r, KVH * HD)
    grad_wv = back[..., qh * HD + HD :].reshape(r, KVH * HD)
    gain_grad_one = (
        jnp.sum(grad_wq * w_query.astype(F32), -1)
        + jnp.sum(grad_wk * w_key.astype(F32), -1)
        + jnp.sum(grad_wv * w_value.astype(F32), -1)
    ) / attn_gain.astype(F32)
    grad_hidden_one = plane_sum(mm_nt(grad_rows, wqkv).astype(BF), 8).astype(F32)
    scale_one = rms_scale(resid_in)
    grad_tokens = grad_mid + norm_back(grad_hidden_one * gain_one, resid_in * scale_one, scale_one)
    return (
        layer_out.reshape(seqs, block, width),
        grad_tokens.reshape(seqs, block, width).astype(BF),
        gain_grad_one,
        grad_wq,
        grad_wk,
        grad_wv,
        grad_wo.astype(F32),
        gain_grad_two,
        grad_wg,
        grad_wu,
        grad_wd.astype(F32),
    )


def solution(mesh):
    fsdp, ctx = mesh.devices.shape
    fine = Mesh(mesh.devices.reshape(fsdp // 2, 2, ctx // 2, 2), ("a", "core", "cm", "cl"))
    token = P(("a", "core"), ("cm", "cl"), None)
    vector = P(("a", "core", "cm", "cl"))
    matrix = P(("a", "core", "cm", "cl"), None)
    return jax.shard_map(
        on_device,
        mesh=fine,
        in_specs=(
            token,
            P(("a", "core")),
            token,
            vector,
            matrix,
            matrix,
            matrix,
            matrix,
            vector,
            matrix,
            matrix,
            matrix,
        ),
        out_specs=(token, token, vector, matrix, matrix, matrix, matrix, vector, matrix, matrix, matrix),
        check_vma=False,
    )
```

```python
import functools

import jax
import jax.numpy as jnp
from jax import lax
from jax.experimental import pallas as pl
from jax.experimental.pallas import tpu as pltpu
from jax.sharding import Mesh
from jax.sharding import PartitionSpec as P

HEADS = 32
KVH = 8
HD = 64
EPSILON = 1e-05
NEGATIVE = -1e30
BF = jnp.bfloat16
F32 = jnp.float32
GROUP = ("a", "core", "cl")
MESH = pl.DeviceIdType.MESH
ANY = pl.BlockSpec(memory_space=pl.ANY)
TILE = 32
MIB = 2**20


def dma(*shape):
    return pltpu.SemaphoreType.DMA(shape)


def places():
    return tuple(lax.axis_index(n) for n in GROUP)


def index_of(a, core, cl):
    return (a * 2 + core) * 2 + cl


def partners():
    a, core, cl = places()
    out = []
    for t in range(1, 8):
        at = (a ^ (t >> 2), core ^ ((t >> 1) & 1), cl ^ (t & 1))
        out.append((dict(zip(GROUP, at)), index_of(*at)))
    return out


def moved_to(c, nz):
    return lax.rem(c, nz), c // nz


def moved_from(c, nz):
    block = lax.rem(c, 2) * nz + c // 2
    return block // 2, lax.rem(block, 2)


def move_pair(nz, back):
    here = lax.axis_index("cm") * 2 + lax.axis_index("cl")
    pair = [dict(zip(("cm", "cl"), f(here, nz))) for f in (moved_to, moved_from)]
    if back:
        pair.reverse()
    return pair, pair[0]["cm"] * 2 + pair[0]["cl"] == here


def greet(whole, line, move, nz):
    barrier = pltpu.get_barrier_semaphore()

    def signal(device):
        pl.semaphore_signal(barrier, inc=1, device_id=device, device_id_type=MESH)

    if whole:
        base = [device for device, _ in partners()]
    else:
        base = [{n: 1 - lax.axis_index(n)} for n in GROUP]
    for device in base:
        signal(device)
    n = len(base)
    if line:
        z = lax.axis_index("cm")
        pl.when(z > 0)(lambda: signal({"cm": z - 1}))
        pl.when(z < nz - 1)(lambda: signal({"cm": z + 1}))
        edge = jnp.logical_or(z == 0, z == nz - 1)
        pl.when(edge)(lambda: pl.semaphore_wait(barrier, n + 1))
        pl.when(jnp.logical_not(edge))(lambda: pl.semaphore_wait(barrier, n + 2))
    elif move is not None:
        pair, stays = move_pair(nz, move)

        @pl.when(jnp.logical_not(stays))
        def _():
            for device in pair:
                signal(device)
            pl.semaphore_wait(barrier, n + 2)

        @pl.when(stays)
        def _():
            pl.semaphore_wait(barrier, n)

    else:
        pl.semaphore_wait(barrier, n)


def remote(src, dst, send, recv, device):
    if isinstance(device, str):
        device = {device: 1 - lax.axis_index(device)}
    return pltpu.make_async_remote_copy(
        src_ref=src, dst_ref=dst, send_sem=send, recv_sem=recv, device_id=device, device_id_type=MESH
    )


def gather_steps(x_ref, o_ref, local, ss, rs):
    a, core, cl = places()
    half = x_ref.shape[0] // 2
    lo, hi = pl.ds(0, half), pl.ds(half, half)
    me = index_of(a, core, cl)
    sx = index_of(1 - a, core, cl)
    sy = index_of(a, core, 1 - cl)
    sd = index_of(1 - a, core, 1 - cl)
    mine = pltpu.make_async_copy(x_ref, o_ref.at[me], local.at[0])

    def put(i, slot, part, name, src=None):
        src = o_ref.at[slot, part] if src is None else src
        return remote(src, o_ref.at[slot, part], ss.at[i], rs.at[i], name)

    sent = [
        put(0, me, lo, "a", x_ref.at[lo]),
        put(1, me, hi, "cl", x_ref.at[hi]),
        put(2, me, hi, "a", x_ref.at[hi]),
        put(3, me, lo, "cl", x_ref.at[lo]),
        put(4, me, pl.ds(0, 2 * half), "core", x_ref),
    ]
    for c in sent:
        c.start()
    mine.start()
    yield

    def on(i, slot, part, name):
        c = put(i, slot, part, name)
        c.start()
        sent.append(c)

    put(0, sx, lo, "a").wait_recv()
    on(5, sx, lo, "cl")
    on(6, sx, lo, "core")
    put(1, sy, hi, "cl").wait_recv()
    on(7, sy, hi, "a")
    on(8, sy, hi, "core")
    yield
    put(2, sx, hi, "a").wait_recv()
    on(9, sx, hi, "core")
    put(3, sy, lo, "cl").wait_recv()
    on(10, sy, lo, "core")
    yield
    put(5, sd, lo, "cl").wait_recv()
    on(11, sd, lo, "core")
    put(7, sd, hi, "a").wait_recv()
    on(12, sd, hi, "core")
    yield
    other = 2 - 4 * core
    put(4, me + other, pl.ds(0, 2 * half), "core").wait_recv()
    for i, slot, part in ((6, sx, lo), (8, sy, hi), (9, sx, hi), (10, sy, lo), (11, sd, lo), (12, sd, hi)):
        put(i, slot + other, part, "core").wait_recv()
    for c in sent:
        c.wait_send()
    mine.wait()


def add_rows(dst, sources, n):
    @pl.loop(0, n // TILE)
    def _(i):
        part = pl.ds(pl.multiple_of(i * TILE, TILE), TILE)
        total = sources[0][part, :].astype(F32)
        for s in sources[1:]:
            total = total + s[part, :].astype(F32)
        dst[part, :] = total.astype(dst.dtype)


def plane_chips():
    a, _, cl = places()
    return (a, cl), (1 - a, cl), (a, 1 - cl), (1 - a, 1 - cl)


def sum_steps(x_ref, o_ref, mine, theirs, first, last, lsem, cs, cr, ss, rs):
    core = lax.axis_index("core")
    out, loc = {}, {}
    for p in (3, 1, 2, 0):
        ca, cc = plane_chips()[p]
        out[p] = remote(x_ref.at[index_of(ca, 1 - core, cc)], theirs.at[p], cs.at[p], cr.at[p], "core")
        out[p].start()
        loc[p] = pltpu.make_async_copy(x_ref.at[index_of(ca, core, cc)], mine.at[p], lsem.at[p])
        loc[p].start()
    yield
    yield from sum_rest(o_ref, mine, theirs, first, last, lsem, out, loc, ss, rs)


def sum_rest(o_ref, mine, theirs, first, last, lsem, out, loc, ss, rs):
    rows = mine.shape[1]
    half = rows // 2
    lo, hi = pl.ds(0, half), pl.ds(half, half)

    def chip_sum(p):
        out[p].wait_recv()
        if p in loc:
            loc[p].wait()
        add_rows(mine.at[p], (mine.at[p], theirs.at[p]), rows)

    chip_sum(3)
    xd = remote(mine.at[3, lo], first.at[0], ss.at[0], rs.at[0], "a")
    yd = remote(mine.at[3, hi], first.at[1], ss.at[1], rs.at[1], "cl")
    xd.start()
    yd.start()
    chip_sum(1)
    xo = remote(mine.at[1, lo], first.at[2], ss.at[2], rs.at[2], "a")
    xo.start()
    chip_sum(2)
    yo = remote(mine.at[2, hi], first.at[3], ss.at[3], rs.at[3], "cl")
    yo.start()
    chip_sum(0)
    yield
    xd.wait_recv()
    add_rows(mine.at[2, lo], (mine.at[2, lo], first.at[0]), half)
    y2 = remote(mine.at[2, lo], last.at[0], ss.at[4], rs.at[4], "cl")
    y2.start()
    yd.wait_recv()
    add_rows(mine.at[1, hi], (mine.at[1, hi], first.at[1]), half)
    x2 = remote(mine.at[1, hi], last.at[1], ss.at[5], rs.at[5], "a")
    x2.start()
    yield
    xo.wait_recv()
    add_rows(mine.at[0, lo], (mine.at[0, lo], first.at[2]), half)
    yo.wait_recv()
    add_rows(mine.at[0, hi], (mine.at[0, hi], first.at[3]), half)
    yield
    y2.wait_recv()
    add_rows(mine.at[0, lo], (mine.at[0, lo], last.at[0]), half)
    x2.wait_recv()
    add_rows(mine.at[0, hi], (mine.at[0, hi], last.at[1]), half)
    done = pltpu.make_async_copy(mine.at[0], o_ref, lsem.at[4])
    done.start()
    for c in (*out.values(), xd, yd, xo, yo, y2, x2):
        c.wait_send()
    done.wait()


def swap_steps(kind, pieces, src, dst, lsem, ss, rs):
    me = index_of(*places())
    copies = []
    for p in range(pieces):

        def block(f, p=p):
            return ((f // 2) * pieces + p) * 2 + lax.rem(f, 2) if pieces > 1 else f

        width = (dst if kind == "cols" else src).shape[-1] // pieces

        def cut(ref, i, width=width):
            return ref.at[:, pl.ds(pl.multiple_of(i * width, width), width)]

        def part(ref, i, p=p, width=width):
            return ref.at[i] if pieces == 1 else ref.at[i, :, pl.ds(p * width, width)]

        def source(f, block=block, cut=cut, part=part):
            return cut(src, block(f)) if kind == "cols" else part(src, f)

        target = cut(dst, block(me)) if kind == "back" else part(dst, me)
        for t, (device, index) in enumerate(partners()):
            copies.append(remote(source(index), target, ss.at[p, t], rs.at[p, t], device))
            copies[-1].start()
        copies.append(pltpu.make_async_copy(source(me), target, lsem.at[p]))
        copies[-1].start()
    yield
    yield
    yield
    yield
    for copy in copies:
        copy.wait()


def move_steps(nz, back, src, dst, lsem, ss, rs):
    pair, stays = move_pair(nz, back)
    mine = pltpu.make_async_copy(src, dst, lsem.at[0])
    away = remote(src, dst, ss.at[0], rs.at[0], pair[0])
    pl.when(stays)(mine.start)
    pl.when(jnp.logical_not(stays))(away.start)
    yield
    yield
    yield
    yield
    pl.when(stays)(mine.wait)
    pl.when(jnp.logical_not(stays))(away.wait)


def up_steps(nz, x_ref, o_ref, lsem, ss, rs):
    z = lax.axis_index("cm")
    mine = pltpu.make_async_copy(x_ref, o_ref.at[z], lsem.at[0])
    mine.start()

    def send(j, src):
        return remote(src, o_ref.at[j], ss.at[j], rs.at[j], {"cm": jnp.minimum(z + 1, nz - 1)})

    @pl.when(z < nz - 1)
    def _():
        send(z, x_ref).start()

    yield
    for i in range(1, nz):

        @pl.when(z >= i)
        def _(i=i):
            j = z - i
            send(j, o_ref.at[j]).wait_recv()

            @pl.when(z < nz - 1)
            def _():
                send(j, o_ref.at[j]).start()

        yield
    for i in range(nz):

        @pl.when(jnp.logical_and(z >= i, z < nz - 1))
        def _(i=i):
            send(z - i, x_ref).wait_send()

    mine.wait()


def pass_steps(src, dst, lsem):
    copy = pltpu.make_async_copy(src, dst, lsem.at[0])
    copy.start()
    yield
    yield
    yield
    copy.wait()


def down_steps(nz, x_ref, o_ref, mine, came, lsem, ss, rs):
    z = lax.axis_index("cm")
    rows = x_ref.shape[1]

    def load(j):
        return pltpu.make_async_copy(x_ref.at[j], mine.at[j], lsem.at[j])

    def send(j):
        return remote(mine.at[j], came.at[j], ss.at[j], rs.at[j], {"cm": jnp.maximum(z - 1, 0)})

    for j in range(nz):
        pl.when(z >= j)(lambda j=j: load(j).start())
    yield
    for j in range(nz):

        @pl.when(z >= j)
        def _(j=j):
            load(j).wait()

            @pl.when(z < nz - 1)
            def _():
                send(j).wait_recv()
                add_rows(mine.at[j], (mine.at[j], came.at[j]), rows)

            @pl.when(z > j)
            def _():
                send(j).start()

        yield
    done = pltpu.make_async_copy(mine.at[z], o_ref, lsem.at[nz])
    done.start()
    for j in range(nz):
        pl.when(z > j)(lambda j=j: send(j).wait_send())
    done.wait()


def back_steps(nz, r, hid_ref, one_ref, two_ref, wone_ref, wtwo_ref, o_ref, out_one, out_two, *scratch):
    hid, g, w, out, stage, theirs, first, last, gsem, osem, lsem, cs, cr, ss, rs = scratch
    tiles, _, wide = hid.shape
    run = 2 * r
    per = wide // run
    core = lax.axis_index("core")
    rows, width = theirs.shape[1:]
    loads = [
        pltpu.make_async_copy(src, dst, gsem.at[n])
        for n, (src, dst) in enumerate(
            [(wone_ref, w.at[0]), (one_ref, g.at[0]), (wtwo_ref, w.at[1]), (two_ref, g.at[1])]
            + [(hid_ref.at[:, pl.ds(i * wide, wide)], hid.at[i]) for i in range(tiles)]
        )
    ]
    for c in loads:
        c.start()
    for c in loads[:4]:
        c.wait()

    @pl.loop(0, 8)
    def _(n):
        to = jnp.where(n < 4, 1 - core, core)
        turn = lax.rem(n, 4)
        a, _, cl = places()
        far_a = jnp.where(jnp.logical_or(turn == 0, turn == 1), 1 - a, a)
        far_cl = jnp.where(jnp.logical_or(turn == 0, turn == 2), 1 - cl, cl)
        p = jnp.where(turn == 0, 3, jnp.where(turn == 3, 0, turn))
        first_row = pl.multiple_of(index_of(far_a, to, far_cl) * rows, rows)
        for c in range(0, width, width // 2):
            part = pl.ds(c, width // 2)
            e = dot(g[0, pl.ds(first_row, rows), :], w[0, part, :], 1, 1)
            e += dot(g[1, pl.ds(first_row, rows), :], w[1, part, :], 1, 1)
            stage[n // 4, p, :, part] = e.astype(BF)

        @pl.when(n < 4)
        def _():
            remote(stage.at[0, p], theirs.at[p], cs.at[p], cr.at[p], "core").start()

    out_core = {p: remote(stage.at[0, p], theirs.at[p], cs.at[p], cr.at[p], "core") for p in range(4)}
    for c in loads[4:]:
        c.wait()

    def store(k, i, p):
        chunk = i * per + p
        at = (lax.rem(chunk, nz) * 4 + chunk // nz) * run
        target = (out_one, out_two)[k]
        return pltpu.make_async_copy(
            out.at[k, i, pl.ds(p * run, run)], target.at[pl.ds(pl.multiple_of(at, run), run)], osem.at[k, i, p]
        )

    def products(k, lo, hi):
        @pl.loop(lo, hi)
        def _(i):
            out[k, i] = dot(hid[i], g[k], 0, 0).astype(BF)
            for p in range(per):
                store(k, i, p).start()

    summing = sum_rest(o_ref, stage.at[1], theirs, first, last, lsem, out_core, {}, ss, rs)
    half = tiles // 2
    for k, lo, hi in ((1, 0, half), (1, half, tiles), (0, 0, half), (0, half, tiles)):
        next(summing, None)
        products(k, lo, hi)
    for _ in summing:
        pass
    for k in range(2):

        @pl.loop(0, tiles)
        def _(i, k=k):
            for p in range(per):
                store(k, i, p).wait()

    yield


def product_steps(a_ref, b_ref, o_ref, a, b, out, lsem, osem):
    tiles, rows, _ = out.shape
    loads = [pltpu.make_async_copy(a_ref, a, lsem.at[0]), pltpu.make_async_copy(b_ref, b, lsem.at[1])]
    for c in loads:
        c.start()
    for c in loads:
        c.wait()

    def store(i):
        return pltpu.make_async_copy(out.at[i], o_ref.at[pl.ds(pl.multiple_of(i * rows, rows), rows)], osem.at[i])

    half = b.shape[1] // 2
    for lo, hi in ((0, tiles // 2), (tiles // 2, tiles)):

        @pl.loop(lo, hi)
        def _(i):
            left = a[pl.ds(pl.multiple_of(i * rows, rows), rows), :]
            for c in (0, half):
                out[i, :, c : c + half] = dot(left, b[:, c : c + half]).astype(BF)
            store(i).start()

        yield

    @pl.loop(0, tiles)
    def _(i):
        store(i).wait()


def heads_steps(x_ref, wo_ref, low_ref, heads_ref, g_ref, buf, wo, low, heads, total, g, lsem, local, ss, rs):
    loads = [pltpu.make_async_copy(wo_ref, wo, lsem.at[0]), pltpu.make_async_copy(low_ref, low, lsem.at[1])]
    for c in loads:
        c.start()
    yield from gather_steps(x_ref, buf, local, ss, rs)
    for c in loads:
        c.wait()
    total[...] = jnp.zeros_like(total)
    rows = buf.shape[1]

    @pl.loop(0, 8)
    def _(i):
        block = buf[i]
        part = pl.ds(pl.multiple_of(i * rows, rows), rows)
        heads[part, :] = dot(block, wo[...], 1, 1).astype(BF)
        total[...] += dot(low[part, :], block, 0, 0)

    g[...] = total[...].astype(BF)
    stores = [pltpu.make_async_copy(heads, heads_ref, lsem.at[2]), pltpu.make_async_copy(g, g_ref, lsem.at[3])]
    for c in stores:
        c.start()
    for c in stores:
        c.wait()


def part(kind, *xs, **how):
    nz = lax.axis_size("cm")
    x = xs[0]
    like = lambda *shape: jax.ShapeDtypeStruct(shape, x.dtype)
    vmem = lambda *shape: pltpu.VMEM(shape, x.dtype)
    if kind == "gather":
        rows, cols = x.shape
        return kind, gather_steps, xs, [like(8, rows, cols)], [dma(1), dma(13), dma(13)]
    if kind == "sum":
        rows, cols = x.shape[0] // 8, x.shape[1]
        scratch = [vmem(n, m, cols) for n, m in ((4, rows), (4, rows), (4, rows // 2), (2, rows // 2))]
        scratch += [dma(5), dma(4), dma(4), dma(6), dma(6)]
        return kind, sum_steps, [x.reshape(8, rows, cols)], [like(rows, cols)], scratch
    if kind == "up":
        return kind, functools.partial(up_steps, nz), xs, [like(nz, *x.shape)], [dma(1), dma(nz), dma(nz)]
    if kind == "pass":
        return kind, pass_steps, xs, [like(*x.shape)], [dma(1)]
    if kind == "down":
        scratch = [vmem(*x.shape)] * 2 + [dma(nz + 1), dma(nz), dma(nz)]
        return kind, functools.partial(down_steps, nz), xs, [like(*x.shape[1:])], scratch
    if kind in ("move", "home"):
        return kind, functools.partial(move_steps, nz, kind == "home"), xs, [like(*x.shape)], [dma(1), dma(1), dma(1)]
    if kind == "mlp":
        rows, width = x.shape
        cols = xs[1].shape[1]
        r = width // (8 * nz)
        wide = 256
        tiles = width // wide
        block = rows // 8
        scratch = [vmem(tiles, rows, wide), vmem(2, rows, cols), vmem(2, width, cols), vmem(2, tiles, wide, cols)]
        scratch += [vmem(2, 4, block, width), vmem(4, block, width), vmem(4, block // 2, width)]
        scratch += [vmem(2, block // 2, width), dma(4 + tiles), dma(2, tiles, wide // (2 * r))]
        scratch += [dma(5), dma(4), dma(4), dma(6), dma(6)]
        outs = [like(block, width), like(width, cols), like(width, cols)]
        return kind, functools.partial(back_steps, nz, r), xs, outs, scratch
    if kind == "product":
        rows, cols = x.shape[0], xs[1].shape[1]
        scratch = [vmem(*x.shape), vmem(*xs[1].shape), vmem(8, rows // 8, cols), dma(2), dma(8)]
        return kind, product_steps, xs, [like(rows, cols)], scratch
    if kind == "heads":
        rows, cols = x.shape
        wide = xs[1].shape[0]
        scratch = [vmem(8, rows, cols), vmem(wide, cols), vmem(8 * rows, wide), vmem(8 * rows, wide)]
        scratch += [pltpu.VMEM((wide, cols), F32), vmem(wide, cols), dma(4), dma(1), dma(13), dma(13)]
        return kind, heads_steps, xs, [like(8 * rows, wide), like(wide, cols)], scratch
    pieces = how.get("pieces", 1)
    shape = x.shape
    if kind == "cols":
        shape = (8, x.shape[0], x.shape[1] // 8)
    elif kind == "back":
        shape = (x.shape[1], 8 * x.shape[2])
    scratch = [dma(pieces), dma(pieces, 7), dma(pieces, 7)]
    return kind, functools.partial(swap_steps, kind, pieces), xs, [like(*shape)], scratch


def transfer(cid, parts, deps=()):
    nz = lax.axis_size("cm")
    kinds = [p[0] for p in parts]
    operands = [x for p in parts for x in p[2]]
    results = [o for p in parts for o in p[3]]
    moves = [k == "home" for k in kinds if k in ("move", "home")]
    whole = any(k in ("slab", "cols", "back") for k in kinds)
    line = any(k in ("up", "down") for k in kinds)

    def kernel(*refs):
        ins = list(refs[: len(operands)])
        rest = list(refs[len(operands) + len(deps) :])
        outs, scratch = rest[: len(results)], rest[len(results) :]

        def take(refs, n):
            out = refs[:n]
            del refs[:n]
            return out

        greet(whole, line, moves[0] if moves else None, nz)
        running = []
        for _, steps, xs, shapes, own in parts:
            running.append(steps(*take(ins, len(xs)), *take(outs, len(shapes)), *take(scratch, len(own))))
        while running:
            still = []
            for steps in running:
                try:
                    next(steps)
                except StopIteration:
                    continue
                still.append(steps)
            running = still

    return pl.pallas_call(
        kernel,
        out_shape=results,
        in_specs=[ANY] * (len(operands) + len(deps)),
        out_specs=[ANY] * len(results),
        scratch_shapes=[s for p in parts for s in p[4]],
        compiler_params=pltpu.CompilerParams(
            collective_id=cid, has_side_effects=True, vmem_limit_bytes=56 * MIB
        ),
        name="_".join(kinds) + str(cid),
    )(*operands, *deps)


def after(x, deps):
    return pl.pallas_call(
        lambda *refs: None,
        out_shape=jax.ShapeDtypeStruct(x.shape, x.dtype),
        in_specs=[ANY] * (1 + len(deps)),
        out_specs=ANY,
        input_output_aliases={0: 0},
        name="after",
    )(x, *deps)


def sum_planes(g):
    return lax.psum_scatter(g, "cm", scatter_dimension=0, tiled=True)


def gather_planes(x):
    return lax.all_gather(x, "cm", axis=0, tiled=True)


def dot(a, b, left=1, right=0):
    return lax.dot_general(a, b, (((left,), (right,)), ((), ())), preferred_element_type=F32)


def rope(u, cos, sin):
    width = u.shape[-1]
    lane = lax.broadcasted_iota(jnp.int32, u.shape, 1)
    other = jnp.where(lane % HD < HD // 2, pltpu.roll(u, width - HD // 2, 1), pltpu.roll(u, HD // 2, 1))
    return u * cos + other * sin


def tables(positions):
    lane = jnp.arange(2 * HD)
    frequency = 500000.0 ** (-(lane % (HD // 2)).astype(F32) * 2.0 / HD)
    angles = positions.astype(F32)[..., None] * frequency
    return jnp.cos(angles), jnp.where(lane % HD < HD // 2, -1.0, 1.0) * jnp.sin(angles)


def project_kernel(x_ref, gain_ref, w_ref, cos_ref, sin_ref, hid_ref, q_ref, kv_ref):
    x = x_ref[...].astype(F32)
    hid = (x * lax.rsqrt(jnp.mean(x * x, -1, keepdims=True) + EPSILON) * gain_ref[...]).astype(BF)
    hid_ref[...] = hid
    u = dot(hid, w_ref[...])
    times = x.shape[0] // cos_ref.shape[1]
    cos = jnp.concatenate([cos_ref[0]] * times, 0)
    sin = jnp.concatenate([sin_ref[0]] * times, 0)
    wide = q_ref.shape[-1]
    copies = wide // (2 * HD)
    q_ref[...] = rope(u[:, :wide], jnp.concatenate([cos] * copies, 1), jnp.concatenate([sin] * copies, 1)).astype(BF)
    kv = u[:, wide:]
    lane = lax.broadcasted_iota(jnp.int32, kv.shape, 1)
    kv_ref[...] = jnp.where(lane < HD, rope(kv, cos, sin), kv).astype(BF)


def project(x, gain, w, wide, cos, sin):
    rows, width = x.shape
    step = rows // 8
    block = cos.shape[1]
    table = pl.BlockSpec((1, block, 2 * HD), lambda g: (g % 2, 0, 0))
    return pl.pallas_call(
        project_kernel,
        grid=(8,),
        out_shape=[jax.ShapeDtypeStruct((rows, c), BF) for c in (width, wide, 2 * HD)],
        in_specs=[
            pl.BlockSpec((step, width), lambda g: (g, 0)),
            pl.BlockSpec((1, width), lambda g: (0, 0)),
            pl.BlockSpec((width, wide + 2 * HD), lambda g: (0, 0)),
            table,
            table,
        ],
        out_specs=[pl.BlockSpec((step, c), lambda g: (g, 0)) for c in (width, wide, 2 * HD)],
        compiler_params=pltpu.CompilerParams(vmem_limit_bytes=48 * MIB),
        name="project",
    )(x, gain, w, cos, sin)


def project_back_kernel(dq_ref, dkv_ref, hid_ref, w_ref, cos_ref, sin_ref, e_ref, g_ref, total):
    step = pl.program_id(0)

    @pl.when(step == 0)
    def _():
        total[...] = jnp.zeros_like(total)

    dq = dq_ref[...]
    times = dq.shape[0] // cos_ref.shape[1]
    cos = jnp.concatenate([cos_ref[0]] * times, 0)
    sin = -jnp.concatenate([sin_ref[0]] * times, 0)
    copies = dq.shape[1] // (2 * HD)
    dq = rope(dq, jnp.concatenate([cos] * copies, 1), jnp.concatenate([sin] * copies, 1))
    dkv = dkv_ref[...].astype(F32)
    lane = lax.broadcasted_iota(jnp.int32, dkv.shape, 1)
    dkv = jnp.where(lane < HD, rope(dkv, cos, sin), dkv)
    rows = jnp.concatenate([dq.astype(BF), dkv.astype(BF)], 1)
    e_ref[...] = dot(rows, w_ref[...], 1, 1).astype(BF)
    total[...] += dot(hid_ref[...], rows, 0, 0)

    @pl.when(step == pl.num_programs(0) - 1)
    def _():
        g_ref[...] = total[...].astype(BF)


def project_back(dq, dkv, hid, w, cos, sin):
    rows, width = hid.shape
    step = rows // 8
    shape = (width, dq.shape[1] + 2 * HD)
    block = cos.shape[1]
    table = pl.BlockSpec((1, block, 2 * HD), lambda g: (g % 2, 0, 0))
    return pl.pallas_call(
        project_back_kernel,
        grid=(8,),
        out_shape=[jax.ShapeDtypeStruct((rows, width), BF), jax.ShapeDtypeStruct(shape, BF)],
        in_specs=[
            pl.BlockSpec((step, dq.shape[1]), lambda g: (g, 0)),
            pl.BlockSpec((step, 2 * HD), lambda g: (g, 0)),
            pl.BlockSpec((step, width), lambda g: (g, 0)),
            pl.BlockSpec(shape, lambda g: (0, 0)),
            table,
            table,
        ],
        out_specs=[pl.BlockSpec((step, width), lambda g: (g, 0)), pl.BlockSpec(shape, lambda g: (0, 0))],
        scratch_shapes=[pltpu.VMEM(shape, F32)],
        compiler_params=pltpu.CompilerParams(vmem_limit_bytes=48 * MIB),
        name="project_back",
    )(dq, dkv, hid, w, cos, sin)


def flat(ref):
    x = ref[...]
    return x.reshape(x.shape[-4] * x.shape[-2], x.shape[-1])


def heads_of(x):
    return [x[:, h * HD : (h + 1) * HD] for h in range(x.shape[1] // HD)]


def seen(n, j, z, slots):
    col = lax.broadcasted_iota(jnp.int32, (slots, slots), 0) + j * slots
    row = lax.broadcasted_iota(jnp.int32, (slots, slots), 1) + z * slots
    return jnp.logical_and(col <= row, col < n)


def attend_kernel(lens, q_ref, kv_ref, att_ref, low_ref, log_ref, scores, top, sums, acc):
    z = lax.axis_index("cm")
    n = lens[pl.program_id(0) * pl.num_programs(1) + pl.program_id(1)]
    q = flat(q_ref)
    slots = q.shape[0]
    qs = heads_of((q.astype(F32) * HD ** (-0.5)).astype(BF))
    top[...] = jnp.full_like(top, NEGATIVE)
    sums[...] = jnp.zeros_like(sums)
    acc[...] = jnp.zeros_like(acc)

    def score(j, _):
        k = flat(kv_ref.at[j])[:, :HD]
        mask = seen(n, j, z, slots)
        for h, qh in enumerate(qs):
            s = jnp.where(mask, dot(k, qh, 1, 1), NEGATIVE)
            scores[j, h] = s
            top[h : h + 1] = jnp.maximum(top[h : h + 1], jnp.max(s, 0, keepdims=True))
        return 0

    blocks = jnp.minimum(z + 1, (n + slots - 1) // slots)
    lax.fori_loop(0, blocks, score, 0)

    def weigh(j, _):
        v = flat(kv_ref.at[j])[:, HD:]
        for h in range(len(qs)):
            p = jnp.exp(scores[j, h] - top[h : h + 1])
            sums[h : h + 1] += jnp.sum(p, 0, keepdims=True)
            acc[h * HD : (h + 1) * HD] += dot(v, p.astype(BF), 0, 0)
        return 0

    lax.fori_loop(0, blocks, weigh, 0)
    out = jnp.concatenate([acc[h * HD : (h + 1) * HD] / sums[h : h + 1] for h in range(len(qs))], 0)
    att_ref[0, 0] = out
    low_ref[...] = out.T.astype(BF).reshape(low_ref.shape)
    log_ref[0, 0] = top[...] + jnp.log(sums[...])


def attend_back_kernel(lens, q_ref, kv_ref, do_ref, att_ref, log_ref, dq_ref, dkv_ref, acc):
    z = lax.axis_index("cm")
    n = lens[pl.program_id(0) * pl.num_programs(1) + pl.program_id(1)]
    q = flat(q_ref)
    slots = q.shape[0]
    qs = heads_of((q.astype(F32) * HD ** (-0.5)).astype(BF))
    do = flat(do_ref)
    dos = heads_of(do)
    both = do.astype(F32).T * att_ref[0, 0]
    deltas = [jnp.sum(both[h * HD : (h + 1) * HD], 0, keepdims=True) for h in range(len(qs))]
    acc[...] = jnp.zeros_like(acc)

    def step(j, _):
        kv = flat(kv_ref.at[j])
        k, v = kv[:, :HD], kv[:, HD:]
        mask = seen(n, j, z, slots)
        dk = jnp.zeros((slots, HD), F32)
        dv = jnp.zeros((slots, HD), F32)
        for h, qh in enumerate(qs):
            s = jnp.where(mask, dot(k, qh, 1, 1), NEGATIVE)
            p = jnp.exp(s - log_ref[0, 0, h : h + 1])
            ds = (p * (dot(v, dos[h], 1, 1) - deltas[h])).astype(BF)
            acc[h * HD : (h + 1) * HD] += dot(k, ds, 0, 0)
            dk += dot(ds, qh)
            dv += dot(p.astype(BF), dos[h])
        out = jnp.concatenate([dk, dv], 1).astype(BF)
        dkv_ref[j] = out.reshape(dkv_ref.shape[1:])
        return 0

    live = jnp.where(z * slots < n, z + 1, 0)
    lax.fori_loop(0, live, step, 0)

    def nothing(j, _):
        dkv_ref[j] = jnp.zeros(dkv_ref.shape[1:], BF)
        return 0

    lax.fori_loop(live, z + 1, nothing, 0)
    dq_ref[...] = (acc[...] * HD ** (-0.5)).T.reshape(dq_ref.shape)


def attention_specs(seqs, block, wide, nz):
    own = lambda c: pl.BlockSpec((1, 2, 1, block, c), lambda f, s: (f, 0, s, 0, 0))
    every = pl.BlockSpec((nz, 1, 2, 1, block, 2 * HD), lambda f, s: (0, f, 0, s, 0, 0))
    turned = lambda c: pl.BlockSpec((1, 1, c, 2 * block), lambda f, s: (f, s, 0, 0))
    return own(wide), every, turned(wide), turned(wide // HD)


def attend(lens, q, kv, seqs, block):
    nz, rows, _ = kv.shape
    wide = q.shape[1]
    heads = wide // HD
    own, every, turned, logs = attention_specs(seqs, block, wide, nz)
    view = (4, 2, seqs, block)
    att, low, log = pl.pallas_call(
        attend_kernel,
        grid=(4, seqs),
        out_shape=[
            jax.ShapeDtypeStruct((4, seqs, wide, 2 * block), F32),
            jax.ShapeDtypeStruct((*view, wide), BF),
            jax.ShapeDtypeStruct((4, seqs, heads, 2 * block), F32),
        ],
        in_specs=[pl.BlockSpec(memory_space=pltpu.SMEM), own, every],
        out_specs=[turned, own, logs],
        scratch_shapes=[
            pltpu.VMEM((nz, heads, 2 * block, 2 * block), F32),
            pltpu.VMEM((heads, 2 * block), F32),
            pltpu.VMEM((heads, 2 * block), F32),
            pltpu.VMEM((wide, 2 * block), F32),
        ],
        compiler_params=pltpu.CompilerParams(vmem_limit_bytes=48 * MIB),
        name="attend",
    )(lens, q.reshape(*view, wide), kv.reshape(nz, *view, 2 * HD))
    return att, low.reshape(rows, wide), log


def attend_back(lens, q, kv, do, att, log, seqs, block):
    nz, rows, _ = kv.shape
    wide = q.shape[1]
    own, every, turned, logs = attention_specs(seqs, block, wide, nz)
    view = (4, 2, seqs, block)
    dq, dkv = pl.pallas_call(
        attend_back_kernel,
        grid=(4, seqs),
        out_shape=[
            jax.ShapeDtypeStruct((*view, wide), F32),
            jax.ShapeDtypeStruct((nz, *view, 2 * HD), BF),
        ],
        in_specs=[pl.BlockSpec(memory_space=pltpu.SMEM), own, every, own, turned, logs],
        out_specs=[own, every],
        scratch_shapes=[pltpu.VMEM((wide, 2 * block), F32)],
        compiler_params=pltpu.CompilerParams(vmem_limit_bytes=48 * MIB),
        name="attend_back",
    )(lens, q.reshape(*view, wide), kv.reshape(nz, *view, 2 * HD), do.reshape(*view, wide), att, log)
    return dq.reshape(rows, wide), dkv.reshape(nz, rows, 2 * HD)


def rms_scale(field):
    return lax.rsqrt(jnp.mean(field * field, -1, keepdims=True) + EPSILON)


def norm_back(grad_normed, normed, scale_rows):
    return scale_rows * (grad_normed - normed * jnp.mean(grad_normed * normed, -1, keepdims=True))


def rows_of(x):
    nz = lax.axis_size("cm")
    _, r, c = x.shape
    x = gather_planes(x)
    return x.reshape(nz, 4, 2, r, c).transpose(1, 0, 2, 3, 4).reshape(nz * 8 * r, c)


def rows_first(g):
    nz = lax.axis_size("cm")
    rows, c = g.shape
    r = rows // (8 * nz)
    return g.astype(BF).reshape(4, nz, 2, r, c).transpose(1, 0, 2, 3, 4).reshape(nz * 8, r, c)


def on_device(
    tokens, lengths, cotangent, attn_gain, w_query, w_key, w_value, w_out, mlp_gain, w_gate, w_up, w_down
):
    seqs, block, width = tokens.shape
    nz = lax.axis_size("cm")
    rows = seqs * block
    r = w_query.shape[0]
    wide = HEADS // 8 * HD
    cm = lax.axis_index("cm")
    cl = lax.axis_index("cl")
    gain_two = mlp_gain.astype(F32)[:, None]
    pieces = nz if w_down.shape[0] % 128 == 0 else 1
    perm = [(c, (c % nz) * 2 + c // nz) for c in range(2 * nz)]
    home = [(t, s) for s, t in perm]

    def gained(w):
        return (w.astype(F32) * gain_two).astype(BF)

    pack = [w.reshape(r, 8, -1) for w in (w_query, w_key, w_value)]
    pack.append(jnp.broadcast_to(attn_gain[:, None, None], (r, 8, 2 * HD)))
    pack = jnp.concatenate(pack, -1).transpose(1, 0, 2)
    lens = jnp.broadcast_to(jnp.pad(lengths, (0, 128 - seqs))[None, None], (8, 8, 128))
    pack, lens = transfer(1, [part("slab", pack), part("slab", lens)])
    lens = lens[::2, 0, :seqs].reshape(-1)
    wg, wo = transfer(2, [part("cols", gained(w_gate), pieces=pieces), part("move", w_out)], (pack,))
    own = tokens.reshape(rows, width)
    tok_all, wu = transfer(3, [part("gather", own), part("cols", gained(w_up), pieces=pieces)], (wg,))
    pack = rows_of(pack)
    gain_row = pack[:, wide + 2 * HD].astype(F32)[None]
    wg = rows_of(wg)
    wo = gather_planes(wo)

    slot = cm * 2 * block + jnp.arange(2 * block, dtype=jnp.int32).reshape(2, block)
    cos, sin = tables(slot)
    hidden_one, q, kv = project(tok_all.reshape(8 * rows, width), gain_row, pack, wide, cos, sin)
    own_pos = cm * 2 * block + cl * block + jnp.arange(block, dtype=jnp.int32)
    valid = (own_pos[None, :] < lengths[:, None]).astype(F32)
    grad_out = (cotangent.astype(F32) * valid[..., None]).reshape(rows, width)
    grad_low, kv_all, down = transfer(
        4,
        [
            part("gather", grad_out.astype(BF)),
            part("up", kv),
            part("pass", w_down),
        ],
    )
    grad_low = grad_low.reshape(8 * rows, width)
    wu = rows_of(wu)
    att, att_low, log = attend(lens, q, kv_all, seqs, block)

    resid_in = own.astype(F32)
    (mid,) = transfer(5, [part("sum", dot(att_low, wo).astype(BF))], (wg,))
    wd = gather_planes(down if pieces > 1 else lax.ppermute(down, ("cm", "cl"), perm))
    resid_mid = resid_in + mid.astype(F32)
    scale_two = rms_scale(resid_mid)
    normed_two = resid_mid * scale_two
    (hidden_two,) = transfer(6, [part("gather", normed_two.astype(BF))], (wu,))
    hidden_two = hidden_two.reshape(8 * rows, width)
    gate_pre = dot(hidden_two, wg)
    up_pre = dot(hidden_two, wu)
    sig = jax.nn.sigmoid(gate_pre)
    act = gate_pre * sig
    inner = (act * up_pre).astype(BF)
    grad_wd = dot(inner, grad_low, 0, 0).astype(BF)
    wd = after(wd, (grad_wd,))
    grad_inner = dot(grad_low, wd, 1, 1).astype(BF).astype(F32)
    grad_gate = (grad_inner * up_pre * (sig * (1.0 + gate_pre * (1.0 - sig)))).astype(BF)
    grad_up = (grad_inner * act).astype(BF)
    e_two, grad_wg, grad_wu = transfer(7, [part("mlp", hidden_two, grad_gate, grad_up, wg, wu)])
    by_owner = lambda g: sum_planes(g.reshape(8 * nz, r, -1))
    grad_wd, grad_wu, grad_wg = sum_planes(grad_wd), by_owner(grad_wu), by_owner(grad_wg)
    grad_mid = grad_out + norm_back(e_two.astype(F32), normed_two, scale_two)
    grad_heads, grad_wo, out_part = transfer(
        8, [part("heads", grad_mid.astype(BF), wo, att_low), part("product", inner, wd)], (grad_wd,)
    )
    dq, dkv = attend_back(lens, q, kv_all, grad_heads, att, log, seqs, block)
    dkv, out_sum, grad_wu = transfer(
        9, [part("down", dkv), part("sum", out_part), part("back", grad_wu, pieces=pieces)]
    )
    layer_out = (resid_mid + out_sum.astype(F32)).astype(BF)
    e_one, grad_qkv = project_back(dq, dkv, hidden_one, pack, cos, sin)
    e_one, grad_wg = transfer(10, [part("sum", e_one), part("back", grad_wg, pieces=pieces)])
    grad_wo = sum_planes(grad_wo)
    grad_qkv = sum_planes(rows_first(grad_qkv))
    scale_one = rms_scale(resid_in)
    grad_tokens = grad_mid + norm_back(e_one.astype(F32) * gain_row, resid_in * scale_one, scale_one)
    grad_qkv, grad_wo = transfer(11, [part("slab", grad_qkv), part("home", grad_wo)], (e_one,))
    if pieces == 1:
        grad_wd = lax.ppermute(grad_wd, ("cm", "cl"), home)
    grad_qkv = grad_qkv.transpose(1, 0, 2).astype(F32)
    grad_wq = grad_qkv[..., :wide].reshape(r, 8 * wide)
    grad_wk = grad_qkv[..., wide : wide + HD].reshape(r, 8 * HD)
    grad_wv = grad_qkv[..., wide + HD :].reshape(r, 8 * HD)
    grad_wg, grad_wu = grad_wg.astype(F32), grad_wu.astype(F32)

    def gain_grad(pairs):
        return sum(jnp.sum(w.astype(F32) * g, -1) for w, g in pairs)

    gain_grad_one = gain_grad(((w_query, grad_wq), (w_key, grad_wk), (w_value, grad_wv))) / attn_gain.astype(F32)
    gain_grad_two = gain_grad(((w_gate, grad_wg), (w_up, grad_wu)))
    return (
        layer_out.reshape(seqs, block, width),
        grad_tokens.reshape(seqs, block, width).astype(BF),
        gain_grad_one,
        grad_wq,
        grad_wk,
        grad_wv,
        grad_wo.astype(F32),
        gain_grad_two,
        grad_wg * gain_two,
        grad_wu * gain_two,
        grad_wd.astype(F32),
    )


def solution(mesh):
    fsdp, ctx = mesh.devices.shape
    fine = Mesh(mesh.devices.reshape(fsdp // 2, 2, ctx // 2, 2), ("a", "core", "cm", "cl"))
    token = P(("a", "core"), ("cm", "cl"), None)
    vector = P(("a", "core", "cm", "cl"))
    matrix = P(("a", "core", "cm", "cl"), None)
    return jax.shard_map(
        on_device,
        mesh=fine,
        in_specs=(
            token,
            P(("a", "core")),
            token,
            vector,
            matrix,
            matrix,
            matrix,
            matrix,
            vector,
            matrix,
            matrix,
            matrix,
        ),
        out_specs=(token, token, vector, matrix, matrix, matrix, matrix, vector, matrix, matrix, matrix),
        check_vma=False,
    )
```

```python
import functools

import jax
import jax.numpy as jnp
from jax import lax
from jax.experimental import pallas as pl
from jax.experimental.pallas import tpu as pltpu
from jax.sharding import Mesh
from jax.sharding import PartitionSpec as P

HEADS = 32
KVH = 8
HD = 64
EPSILON = 1e-05
NEGATIVE = -1e30
BF = jnp.bfloat16
F32 = jnp.float32
GROUP = ("a", "core", "cl")
MESH = pl.DeviceIdType.MESH
ANY = pl.BlockSpec(memory_space=pl.ANY)
TILE = 32
MIB = 2**20


def dma(*shape):
    return pltpu.SemaphoreType.DMA(shape)


def places():
    return tuple(lax.axis_index(n) for n in GROUP)


def index_of(a, core, cl):
    return (a * 2 + core) * 2 + cl


def partners():
    a, core, cl = places()
    out = []
    for t in range(1, 8):
        at = (a ^ (t >> 2), core ^ ((t >> 1) & 1), cl ^ (t & 1))
        out.append((dict(zip(GROUP, at)), index_of(*at)))
    return out


def moved_to(c, nz):
    return lax.rem(c, nz), c // nz


def moved_from(c, nz):
    block = lax.rem(c, 2) * nz + c // 2
    return block // 2, lax.rem(block, 2)


def move_pair(nz, back):
    here = lax.axis_index("cm") * 2 + lax.axis_index("cl")
    pair = [dict(zip(("cm", "cl"), f(here, nz))) for f in (moved_to, moved_from)]
    if back:
        pair.reverse()
    return pair, pair[0]["cm"] * 2 + pair[0]["cl"] == here


def greet(whole, line, move, nz):
    barrier = pltpu.get_barrier_semaphore()

    def signal(device):
        pl.semaphore_signal(barrier, inc=1, device_id=device, device_id_type=MESH)

    if whole:
        base = [device for device, _ in partners()]
    else:
        base = [{n: 1 - lax.axis_index(n)} for n in GROUP]
    for device in base:
        signal(device)
    n = len(base)
    if line:
        z = lax.axis_index("cm")
        pl.when(z > 0)(lambda: signal({"cm": z - 1}))
        pl.when(z < nz - 1)(lambda: signal({"cm": z + 1}))
        edge = jnp.logical_or(z == 0, z == nz - 1)
        pl.when(edge)(lambda: pl.semaphore_wait(barrier, n + 1))
        pl.when(jnp.logical_not(edge))(lambda: pl.semaphore_wait(barrier, n + 2))
    elif move is not None:
        pair, stays = move_pair(nz, move)

        @pl.when(jnp.logical_not(stays))
        def _():
            for device in pair:
                signal(device)
            pl.semaphore_wait(barrier, n + 2)

        @pl.when(stays)
        def _():
            pl.semaphore_wait(barrier, n)

    else:
        pl.semaphore_wait(barrier, n)


def remote(src, dst, send, recv, device):
    if isinstance(device, str):
        device = {device: 1 - lax.axis_index(device)}
    return pltpu.make_async_remote_copy(
        src_ref=src, dst_ref=dst, send_sem=send, recv_sem=recv, device_id=device, device_id_type=MESH
    )


def gather_steps(x_ref, o_ref, local, ss, rs, ready=None):
    ready = ready or (lambda i: None)
    a, core, cl = places()
    half = x_ref.shape[0] // 2
    lo, hi, both = pl.ds(0, half), pl.ds(half, half), pl.ds(0, 2 * half)
    me = index_of(a, core, cl)
    sx = index_of(1 - a, core, cl)
    sy = index_of(a, core, 1 - cl)
    sd = index_of(1 - a, core, 1 - cl)
    other = 2 - 4 * core
    mine = pltpu.make_async_copy(x_ref, o_ref.at[me], local.at[0])

    def put(i, slot, part, name, src=None):
        src = o_ref.at[slot, part] if src is None else src
        return remote(src, o_ref.at[slot, part], ss.at[i], rs.at[i], name)

    sent = [
        put(0, me, lo, "a", x_ref.at[lo]),
        put(1, me, hi, "cl", x_ref.at[hi]),
        put(2, me, hi, "a", x_ref.at[hi]),
        put(3, me, lo, "cl", x_ref.at[lo]),
        put(4, me, both, "core", x_ref),
    ]
    for c in sent:
        c.start()
    mine.start()
    yield
    mine.wait()
    ready(me)

    def on(i, slot, part, name):
        c = put(i, slot, part, name)
        c.start()
        sent.append(c)

    put(0, sx, lo, "a").wait_recv()
    on(5, sx, lo, "cl")
    on(6, sx, lo, "core")
    put(1, sy, hi, "cl").wait_recv()
    on(7, sy, hi, "a")
    on(8, sy, hi, "core")
    put(4, me + other, both, "core").wait_recv()
    ready(me + other)
    yield
    put(2, sx, hi, "a").wait_recv()
    on(9, sx, hi, "core")
    put(3, sy, lo, "cl").wait_recv()
    on(10, sy, lo, "core")
    ready(sx)
    ready(sy)
    yield
    for i, slot, part in ((6, sx, lo), (9, sx, hi)):
        put(i, slot + other, part, "core").wait_recv()
    ready(sx + other)
    put(5, sd, lo, "cl").wait_recv()
    on(11, sd, lo, "core")
    put(7, sd, hi, "a").wait_recv()
    on(12, sd, hi, "core")
    yield
    for i, slot, part in ((8, sy, hi), (10, sy, lo)):
        put(i, slot + other, part, "core").wait_recv()
    ready(sy + other)
    ready(sd)
    for i, slot, part in ((11, sd, lo), (12, sd, hi)):
        put(i, slot + other, part, "core").wait_recv()
    ready(sd + other)
    for c in sent:
        c.wait_send()


def add_rows(dst, sources, n):
    @pl.loop(0, n // TILE)
    def _(i):
        part = pl.ds(pl.multiple_of(i * TILE, TILE), TILE)
        total = sources[0][part, :].astype(F32)
        for s in sources[1:]:
            total = total + s[part, :].astype(F32)
        dst[part, :] = total.astype(dst.dtype)


def plane_chips():
    a, _, cl = places()
    return (a, cl), (1 - a, cl), (a, 1 - cl), (1 - a, 1 - cl)


def sum_steps(x_ref, o_ref, mine, theirs, first, last, lsem, cs, cr, ss, rs):
    core = lax.axis_index("core")
    out, loc = {}, {}
    for p in (3, 1, 2, 0):
        ca, cc = plane_chips()[p]
        out[p] = remote(x_ref.at[index_of(ca, 1 - core, cc)], theirs.at[p], cs.at[p], cr.at[p], "core")
        out[p].start()
        loc[p] = pltpu.make_async_copy(x_ref.at[index_of(ca, core, cc)], mine.at[p], lsem.at[p])
        loc[p].start()
    yield
    yield from sum_rest(o_ref, mine, theirs, first, last, lsem, out, loc, ss, rs)


def sum_rest(o_ref, mine, theirs, first, last, lsem, out, loc, ss, rs):
    rows = mine.shape[1]
    half = rows // 2
    lo, hi = pl.ds(0, half), pl.ds(half, half)

    def chip_sum(p):
        out[p].wait_recv()
        if p in loc:
            loc[p].wait()
        add_rows(mine.at[p], (mine.at[p], theirs.at[p]), rows)

    chip_sum(3)
    xd = remote(mine.at[3, lo], first.at[0], ss.at[0], rs.at[0], "a")
    yd = remote(mine.at[3, hi], first.at[1], ss.at[1], rs.at[1], "cl")
    xd.start()
    yd.start()
    chip_sum(1)
    xo = remote(mine.at[1, lo], first.at[2], ss.at[2], rs.at[2], "a")
    xo.start()
    chip_sum(2)
    yo = remote(mine.at[2, hi], first.at[3], ss.at[3], rs.at[3], "cl")
    yo.start()
    chip_sum(0)
    yield
    xd.wait_recv()
    add_rows(mine.at[2, lo], (mine.at[2, lo], first.at[0]), half)
    y2 = remote(mine.at[2, lo], last.at[0], ss.at[4], rs.at[4], "cl")
    y2.start()
    yd.wait_recv()
    add_rows(mine.at[1, hi], (mine.at[1, hi], first.at[1]), half)
    x2 = remote(mine.at[1, hi], last.at[1], ss.at[5], rs.at[5], "a")
    x2.start()
    yield
    xo.wait_recv()
    add_rows(mine.at[0, lo], (mine.at[0, lo], first.at[2]), half)
    yo.wait_recv()
    add_rows(mine.at[0, hi], (mine.at[0, hi], first.at[3]), half)
    yield
    y2.wait_recv()
    add_rows(mine.at[0, lo], (mine.at[0, lo], last.at[0]), half)
    x2.wait_recv()
    add_rows(mine.at[0, hi], (mine.at[0, hi], last.at[1]), half)
    done = pltpu.make_async_copy(mine.at[0], o_ref, lsem.at[4])
    done.start()
    for c in (*out.values(), xd, yd, xo, yo, y2, x2):
        c.wait_send()
    done.wait()


def swap_steps(kind, pieces, src, dst, lsem, ss, rs):
    me = index_of(*places())
    copies = []
    for p in range(pieces):

        def block(f, p=p):
            return ((f // 2) * pieces + p) * 2 + lax.rem(f, 2) if pieces > 1 else f

        width = (dst if kind == "cols" else src).shape[-1] // pieces

        def cut(ref, i, width=width):
            return ref.at[:, pl.ds(pl.multiple_of(i * width, width), width)]

        def part(ref, i, p=p, width=width):
            return ref.at[i] if pieces == 1 else ref.at[i, :, pl.ds(p * width, width)]

        def source(f, block=block, cut=cut, part=part):
            return cut(src, block(f)) if kind == "cols" else part(src, f)

        target = cut(dst, block(me)) if kind == "back" else part(dst, me)
        for t, (device, index) in enumerate(partners()):
            copies.append(remote(source(index), target, ss.at[p, t], rs.at[p, t], device))
            copies[-1].start()
        copies.append(pltpu.make_async_copy(source(me), target, lsem.at[p]))
        copies[-1].start()
    yield
    yield
    yield
    yield
    for copy in copies:
        copy.wait()


def move_steps(nz, back, src, dst, lsem, ss, rs):
    pair, stays = move_pair(nz, back)
    mine = pltpu.make_async_copy(src, dst, lsem.at[0])
    away = remote(src, dst, ss.at[0], rs.at[0], pair[0])
    pl.when(stays)(mine.start)
    pl.when(jnp.logical_not(stays))(away.start)
    yield
    yield
    yield
    yield
    pl.when(stays)(mine.wait)
    pl.when(jnp.logical_not(stays))(away.wait)


def up_steps(nz, x_ref, o_ref, lsem, ss, rs):
    z = lax.axis_index("cm")
    mine = pltpu.make_async_copy(x_ref, o_ref.at[z], lsem.at[0])
    mine.start()

    def send(j, src):
        return remote(src, o_ref.at[j], ss.at[j], rs.at[j], {"cm": jnp.minimum(z + 1, nz - 1)})

    @pl.when(z < nz - 1)
    def _():
        send(z, x_ref).start()

    yield
    for i in range(1, nz):

        @pl.when(z >= i)
        def _(i=i):
            j = z - i
            send(j, o_ref.at[j]).wait_recv()

            @pl.when(z < nz - 1)
            def _():
                send(j, o_ref.at[j]).start()

        yield
    for i in range(nz):

        @pl.when(jnp.logical_and(z >= i, z < nz - 1))
        def _(i=i):
            send(z - i, x_ref).wait_send()

    mine.wait()


def pass_steps(src, dst, lsem):
    copy = pltpu.make_async_copy(src, dst, lsem.at[0])
    copy.start()
    yield
    yield
    yield
    copy.wait()


def down_steps(nz, x_ref, o_ref, mine, came, lsem, ss, rs):
    z = lax.axis_index("cm")
    rows = x_ref.shape[1]

    def load(j):
        return pltpu.make_async_copy(x_ref.at[j], mine.at[j], lsem.at[j])

    def send(j):
        return remote(mine.at[j], came.at[j], ss.at[j], rs.at[j], {"cm": jnp.maximum(z - 1, 0)})

    for j in range(nz):
        pl.when(z >= j)(lambda j=j: load(j).start())

    @pl.when(z == nz - 1)
    def _():
        for j in range(nz):
            load(j).wait()
            if j < nz - 1:
                send(j).start()

    yield
    yield
    yield
    for j in range(nz - 1):

        @pl.when(jnp.logical_and(z >= j, z < nz - 1))
        def _(j=j):
            load(j).wait()
            send(j).wait_recv()
            add_rows(mine.at[j], (mine.at[j], came.at[j]), rows)
            pl.when(z > j)(send(j).start)

    yield
    done = pltpu.make_async_copy(mine.at[z], o_ref, lsem.at[nz])
    done.start()
    for j in range(nz):
        pl.when(z > j)(lambda j=j: send(j).wait_send())
    done.wait()


def row_loads(nz, src, dst, sems):
    run = dst.shape[0] // (4 * nz)
    copies = []
    for c in range(4 * nz):
        at = (c % nz * 4 + c // nz) * run
        copies.append(pltpu.make_async_copy(src.at[pl.ds(at, run)], dst.at[pl.ds(c * run, run)], sems.at[c]))
    return copies


def back_steps(nz, r, hid_ref, one_ref, two_ref, wone_ref, wtwo_ref, o_ref, out_ref, *scratch):
    hid, g, w, out, stage, theirs, first, last, gsem, wsem, osem, lsem, cs, cr, ss, rs = scratch
    tiles, _, wide = hid.shape
    run = 2 * r
    per = wide // run
    core = lax.axis_index("core")
    rows, width = theirs.shape[1:]
    loads = [pltpu.make_async_copy(one_ref, g.at[0], gsem.at[0]), pltpu.make_async_copy(two_ref, g.at[1], gsem.at[1])]
    loads += row_loads(nz, wone_ref, w.at[0], wsem.at[0]) + row_loads(nz, wtwo_ref, w.at[1], wsem.at[1])
    later = [
        pltpu.make_async_copy(hid_ref.at[:, pl.ds(i * wide, wide)], hid.at[i], gsem.at[2 + i]) for i in range(tiles)
    ]
    for c in loads + later:
        c.start()
    for c in loads:
        c.wait()

    @pl.loop(0, 8)
    def _(n):
        to = jnp.where(n < 4, 1 - core, core)
        turn = lax.rem(n, 4)
        a, _, cl = places()
        far_a = jnp.where(jnp.logical_or(turn == 0, turn == 1), 1 - a, a)
        far_cl = jnp.where(jnp.logical_or(turn == 0, turn == 2), 1 - cl, cl)
        p = jnp.where(turn == 0, 3, jnp.where(turn == 3, 0, turn))
        first_row = pl.multiple_of(index_of(far_a, to, far_cl) * rows, rows)
        for c in range(0, width, width // 2):
            part = pl.ds(c, width // 2)
            e = dot(g[0, pl.ds(first_row, rows), :], w[0, part, :], 1, 1)
            e += dot(g[1, pl.ds(first_row, rows), :], w[1, part, :], 1, 1)
            stage[n // 4, p, :, part] = e.astype(BF)

        @pl.when(n < 4)
        def _():
            remote(stage.at[0, p], theirs.at[p], cs.at[p], cr.at[p], "core").start()

    out_core = {p: remote(stage.at[0, p], theirs.at[p], cs.at[p], cr.at[p], "core") for p in range(4)}
    for c in later:
        c.wait()

    def store(i, p):
        chunk = i * per + p
        at = (lax.rem(chunk, nz) * 4 + chunk // nz) * run
        return pltpu.make_async_copy(
            out.at[i, pl.ds(p * run, run)], out_ref.at[pl.ds(pl.multiple_of(at, run), run)], osem.at[i, p]
        )

    def products(lo, hi):
        @pl.loop(lo, hi)
        def _(i):
            out[i] = dot(hid[i], g[0], 0, 0).astype(BF)
            for p in range(per):
                store(i, p).start()

    summing = sum_rest(o_ref, stage.at[1], theirs, first, last, lsem, out_core, {}, ss, rs)
    for n in range(4):
        next(summing, None)
        products(n * tiles // 4, (n + 1) * tiles // 4)
    for _ in summing:
        pass

    @pl.loop(0, tiles)
    def _(i):
        for p in range(per):
            store(i, p).wait()

    yield


def forward_steps(nz, x_ref, wone_ref, wtwo_ref, low_ref, all_ref, gate_ref, up_ref, in_ref, *rest):
    g_refs, scratch = rest[:2], rest[2:]
    buf, w, low, inner, stage, out, wsem, asem, gsem, osem, local, ss, rs = scratch
    rows = buf.shape[1]
    loads = row_loads(nz, wone_ref, w.at[0], wsem.at[0]) + row_loads(nz, wtwo_ref, w.at[1], wsem.at[1])
    load_low = pltpu.make_async_copy(low_ref, low, osem.at[0])
    done = []

    def keep(src, dst, sem):
        done.append(pltpu.make_async_copy(src, dst, sem))
        done[-1].start()

    def ready(i):
        n = len(done) // 4
        if n == 0:
            for c in loads:
                c.wait()
        block = buf[i]
        part = pl.ds(pl.multiple_of(i * rows, rows), rows)
        gate = dot(block, w[0])
        up = dot(block, w[1])
        stage[n, 0] = gate
        stage[n, 1] = up
        inner[part, :] = (gate * jax.nn.sigmoid(gate) * up).astype(BF)
        keep(buf.at[i], all_ref.at[i], asem.at[n])
        keep(stage.at[n, 0], gate_ref.at[part], gsem.at[n, 0])
        keep(stage.at[n, 1], up_ref.at[part], gsem.at[n, 1])
        keep(inner.at[part], in_ref.at[part], gsem.at[n, 2])

    first = gather_steps(x_ref, buf, local, ss, rs, ready)
    next(first)
    for c in (*loads, load_low):
        c.start()
    for _ in first:
        pass
    load_low.wait()
    tiles, wide, width = out.shape
    half = width // 2

    def store(t, n):
        return pltpu.make_async_copy(
            out.at[t, :, pl.ds(n * half, half)], g_refs[n].at[pl.ds(t * wide, wide)], osem.at[1 + t * 2 + n]
        )

    for t in range(tiles):
        left = inner[:, t * wide : (t + 1) * wide]
        for n in range(2):
            out[t, :, n * half : (n + 1) * half] = dot(left, low[:, n * half : (n + 1) * half], 0, 0).astype(BF)
            store(t, n).start()
    for t in range(tiles):
        for n in range(2):
            store(t, n).wait()
    for c in done:
        c.wait()
    yield


def product_steps(a_ref, b_ref, o_ref, a, b, out, lsem, osem):
    tiles, rows, _ = out.shape
    loads = [pltpu.make_async_copy(a_ref, a, lsem.at[0]), pltpu.make_async_copy(b_ref, b, lsem.at[1])]
    for c in loads:
        c.start()
    for c in loads:
        c.wait()

    def store(i):
        return pltpu.make_async_copy(out.at[i], o_ref.at[pl.ds(pl.multiple_of(i * rows, rows), rows)], osem.at[i])

    half = b.shape[1] // 2
    for lo, hi in ((0, tiles // 2), (tiles // 2, tiles)):

        @pl.loop(lo, hi)
        def _(i):
            left = a[pl.ds(pl.multiple_of(i * rows, rows), rows), :]
            for c in (0, half):
                out[i, :, c : c + half] = dot(left, b[:, c : c + half]).astype(BF)
            store(i).start()

        yield

    @pl.loop(0, tiles)
    def _(i):
        store(i).wait()


def heads_steps(x_ref, wo_ref, low_ref, heads_ref, g_ref, buf, wo, low, heads, total, g, lsem, local, ss, rs):
    loads = [pltpu.make_async_copy(wo_ref, wo, lsem.at[0]), pltpu.make_async_copy(low_ref, low, lsem.at[1])]
    for c in loads:
        c.start()
    yield from gather_steps(x_ref, buf, local, ss, rs)
    for c in loads:
        c.wait()
    total[...] = jnp.zeros_like(total)
    rows = buf.shape[1]

    @pl.loop(0, 8)
    def _(i):
        block = buf[i]
        part = pl.ds(pl.multiple_of(i * rows, rows), rows)
        heads[part, :] = dot(block, wo[...], 1, 1).astype(BF)
        total[...] += dot(low[part, :], block, 0, 0)

    g[...] = total[...].astype(BF)
    stores = [pltpu.make_async_copy(heads, heads_ref, lsem.at[2]), pltpu.make_async_copy(g, g_ref, lsem.at[3])]
    for c in stores:
        c.start()
    for c in stores:
        c.wait()


def part(kind, *xs, **how):
    nz = lax.axis_size("cm")
    x = xs[0]
    like = lambda *shape: jax.ShapeDtypeStruct(shape, x.dtype)
    vmem = lambda *shape: pltpu.VMEM(shape, x.dtype)
    if kind == "gather":
        rows, cols = x.shape
        return kind, gather_steps, xs, [like(8, rows, cols)], [dma(1), dma(13), dma(13)]
    if kind == "sum":
        rows, cols = x.shape[0] // 8, x.shape[1]
        scratch = [vmem(n, m, cols) for n, m in ((4, rows), (4, rows), (4, rows // 2), (2, rows // 2))]
        scratch += [dma(5), dma(4), dma(4), dma(6), dma(6)]
        return kind, sum_steps, [x.reshape(8, rows, cols)], [like(rows, cols)], scratch
    if kind == "up":
        return kind, functools.partial(up_steps, nz), xs, [like(nz, *x.shape)], [dma(1), dma(nz), dma(nz)]
    if kind == "pass":
        return kind, pass_steps, xs, [like(*x.shape)], [dma(1)]
    if kind == "down":
        scratch = [vmem(*x.shape)] * 2 + [dma(nz + 1), dma(nz), dma(nz)]
        return kind, functools.partial(down_steps, nz), xs, [like(*x.shape[1:])], scratch
    if kind in ("move", "home"):
        return kind, functools.partial(move_steps, nz, kind == "home"), xs, [like(*x.shape)], [dma(1), dma(1), dma(1)]
    if kind == "mlp":
        rows, width = x.shape
        cols = xs[1].shape[1]
        r = width // (8 * nz)
        wide = 256
        tiles = width // wide
        block = rows // 8
        scratch = [vmem(tiles, rows, wide), vmem(2, rows, cols), vmem(2, width, cols), vmem(tiles, wide, cols)]
        scratch += [vmem(2, 4, block, width), vmem(4, block, width), vmem(4, block // 2, width)]
        scratch += [vmem(2, block // 2, width), dma(2 + tiles), dma(2, 4 * nz), dma(tiles, wide // (2 * r))]
        scratch += [dma(5), dma(4), dma(4), dma(6), dma(6)]
        return kind, functools.partial(back_steps, nz, r), xs, [like(block, width), like(width, cols)], scratch
    if kind == "forward":
        rows, width = x.shape
        cols = xs[1].shape[1]
        wide = min(256, cols)
        tiles = cols // wide
        full = [jax.ShapeDtypeStruct((8 * rows, cols), F32)] * 2
        outs = [like(8, rows, width), *full, like(8 * rows, cols), *[like(cols, width // 2)] * 2]
        scratch = [vmem(8, rows, width), vmem(2, width, cols), vmem(8 * rows, width), vmem(8 * rows, cols)]
        scratch += [pltpu.VMEM((8, 2, rows, cols), F32), vmem(tiles, wide, width)]
        scratch += [dma(2, 4 * nz), dma(8), dma(8, 3), dma(1 + 2 * tiles), dma(1), dma(13), dma(13)]
        return kind, functools.partial(forward_steps, nz), xs, outs, scratch
    if kind == "product":
        rows, cols = x.shape[0], xs[1].shape[1]
        scratch = [vmem(*x.shape), vmem(*xs[1].shape), vmem(8, rows // 8, cols), dma(2), dma(8)]
        return kind, product_steps, xs, [like(rows, cols)], scratch
    if kind == "heads":
        rows, cols = x.shape
        wide = xs[1].shape[0]
        scratch = [vmem(8, rows, cols), vmem(wide, cols), vmem(8 * rows, wide), vmem(8 * rows, wide)]
        scratch += [pltpu.VMEM((wide, cols), F32), vmem(wide, cols), dma(4), dma(1), dma(13), dma(13)]
        return kind, heads_steps, xs, [like(8 * rows, wide), like(wide, cols)], scratch
    pieces = how.get("pieces", 1)
    shape = x.shape
    if kind == "cols":
        shape = (8, x.shape[0], x.shape[1] // 8)
    elif kind == "back":
        shape = (x.shape[1], 8 * x.shape[2])
    scratch = [dma(pieces), dma(pieces, 7), dma(pieces, 7)]
    return kind, functools.partial(swap_steps, kind, pieces), xs, [like(*shape)], scratch


def transfer(cid, parts, deps=()):
    nz = lax.axis_size("cm")
    kinds = [p[0] for p in parts]
    operands = [x for p in parts for x in p[2]]
    results = [o for p in parts for o in p[3]]
    moves = [k == "home" for k in kinds if k in ("move", "home")]
    whole = any(k in ("slab", "cols", "back") for k in kinds)
    line = any(k in ("up", "down") for k in kinds)

    def kernel(*refs):
        ins = list(refs[: len(operands)])
        rest = list(refs[len(operands) + len(deps) :])
        outs, scratch = rest[: len(results)], rest[len(results) :]

        def take(refs, n):
            out = refs[:n]
            del refs[:n]
            return out

        greet(whole, line, moves[0] if moves else None, nz)
        running = []
        for _, steps, xs, shapes, own in parts:
            running.append(steps(*take(ins, len(xs)), *take(outs, len(shapes)), *take(scratch, len(own))))
        while running:
            still = []
            for steps in running:
                try:
                    next(steps)
                except StopIteration:
                    continue
                still.append(steps)
            running = still

    return pl.pallas_call(
        kernel,
        out_shape=results,
        in_specs=[ANY] * (len(operands) + len(deps)),
        out_specs=[ANY] * len(results),
        scratch_shapes=[s for p in parts for s in p[4]],
        compiler_params=pltpu.CompilerParams(
            collective_id=cid, has_side_effects=True, vmem_limit_bytes=60 * MIB
        ),
        name="_".join(kinds) + str(cid),
    )(*operands, *deps)


def after(x, deps):
    return pl.pallas_call(
        lambda *refs: None,
        out_shape=jax.ShapeDtypeStruct(x.shape, x.dtype),
        in_specs=[ANY] * (1 + len(deps)),
        out_specs=ANY,
        input_output_aliases={0: 0},
        name="after",
    )(x, *deps)


def sum_planes(g):
    return lax.psum_scatter(g, "cm", scatter_dimension=0, tiled=True)


def gather_planes(x):
    return lax.all_gather(x, "cm", axis=0, tiled=True)


def dot(a, b, left=1, right=0):
    return lax.dot_general(a, b, (((left,), (right,)), ((), ())), preferred_element_type=F32)


def rope(u, cos, sin):
    width = u.shape[-1]
    lane = lax.broadcasted_iota(jnp.int32, u.shape, 1)
    other = jnp.where(lane % HD < HD // 2, pltpu.roll(u, width - HD // 2, 1), pltpu.roll(u, HD // 2, 1))
    return u * cos + other * sin


def tables(positions):
    lane = jnp.arange(2 * HD)
    frequency = 500000.0 ** (-(lane % (HD // 2)).astype(F32) * 2.0 / HD)
    angles = positions.astype(F32)[..., None] * frequency
    return jnp.cos(angles), jnp.where(lane % HD < HD // 2, -1.0, 1.0) * jnp.sin(angles)


def project_kernel(x_ref, gain_ref, w_ref, cos_ref, sin_ref, hid_ref, q_ref, kv_ref):
    x = x_ref[...].astype(F32)
    hid = (x * lax.rsqrt(jnp.mean(x * x, -1, keepdims=True) + EPSILON) * gain_ref[...]).astype(BF)
    hid_ref[...] = hid
    u = dot(hid, w_ref[...])
    times = x.shape[0] // cos_ref.shape[1]
    cos = jnp.concatenate([cos_ref[0]] * times, 0)
    sin = jnp.concatenate([sin_ref[0]] * times, 0)
    wide = q_ref.shape[-1]
    copies = wide // (2 * HD)
    q_ref[...] = rope(u[:, :wide], jnp.concatenate([cos] * copies, 1), jnp.concatenate([sin] * copies, 1)).astype(BF)
    kv = u[:, wide:]
    lane = lax.broadcasted_iota(jnp.int32, kv.shape, 1)
    kv_ref[...] = jnp.where(lane < HD, rope(kv, cos, sin), kv).astype(BF)


def project(x, gain, w, wide, cos, sin):
    rows, width = x.shape
    step = rows // 8
    block = cos.shape[1]
    table = pl.BlockSpec((1, block, 2 * HD), lambda g: (g % 2, 0, 0))
    return pl.pallas_call(
        project_kernel,
        grid=(8,),
        out_shape=[jax.ShapeDtypeStruct((rows, c), BF) for c in (width, wide, 2 * HD)],
        in_specs=[
            pl.BlockSpec((step, width), lambda g: (g, 0)),
            pl.BlockSpec((1, width), lambda g: (0, 0)),
            pl.BlockSpec((width, wide + 2 * HD), lambda g: (0, 0)),
            table,
            table,
        ],
        out_specs=[pl.BlockSpec((step, c), lambda g: (g, 0)) for c in (width, wide, 2 * HD)],
        compiler_params=pltpu.CompilerParams(vmem_limit_bytes=48 * MIB),
        name="project",
    )(x, gain, w, cos, sin)


def project_back_kernel(dq_ref, dkv_ref, hid_ref, w_ref, cos_ref, sin_ref, *rest):
    e_ref, g_ref, total = rest[-3:]
    step = pl.program_id(0)

    @pl.when(step == 0)
    def _():
        total[...] = jnp.zeros_like(total)

    dq = dq_ref[...]
    times = dq.shape[0] // cos_ref.shape[1]
    cos = jnp.concatenate([cos_ref[0]] * times, 0)
    sin = -jnp.concatenate([sin_ref[0]] * times, 0)
    copies = dq.shape[1] // (2 * HD)
    dq = rope(dq, jnp.concatenate([cos] * copies, 1), jnp.concatenate([sin] * copies, 1))
    dkv = dkv_ref[...].astype(F32)
    lane = lax.broadcasted_iota(jnp.int32, dkv.shape, 1)
    dkv = jnp.where(lane < HD, rope(dkv, cos, sin), dkv)
    rows = jnp.concatenate([dq.astype(BF), dkv.astype(BF)], 1)
    e_ref[...] = dot(rows, w_ref[...], 1, 1).astype(BF)
    total[...] += dot(hid_ref[...], rows, 0, 0)

    @pl.when(step == pl.num_programs(0) - 1)
    def _():
        g_ref[...] = total[...].astype(BF)


def project_back(dq, dkv, hid, w, cos, sin, deps):
    rows, width = hid.shape
    step = rows // 8
    shape = (width, dq.shape[1] + 2 * HD)
    block = cos.shape[1]
    table = pl.BlockSpec((1, block, 2 * HD), lambda g: (g % 2, 0, 0))
    return pl.pallas_call(
        project_back_kernel,
        grid=(8,),
        out_shape=[jax.ShapeDtypeStruct((rows, width), BF), jax.ShapeDtypeStruct(shape, BF)],
        in_specs=[
            pl.BlockSpec((step, dq.shape[1]), lambda g: (g, 0)),
            pl.BlockSpec((step, 2 * HD), lambda g: (g, 0)),
            pl.BlockSpec((step, width), lambda g: (g, 0)),
            pl.BlockSpec(shape, lambda g: (0, 0)),
            table,
            table,
        ]
        + [ANY] * len(deps),
        out_specs=[pl.BlockSpec((step, width), lambda g: (g, 0)), pl.BlockSpec(shape, lambda g: (0, 0))],
        scratch_shapes=[pltpu.VMEM(shape, F32)],
        compiler_params=pltpu.CompilerParams(vmem_limit_bytes=48 * MIB),
        name="project_back",
    )(dq, dkv, hid, w, cos, sin, *deps)


def inner_back_kernel(nz, r, low_ref, gate_ref, up_ref, wd_ref, hid_ref, gg_ref, gu_ref, out_ref, hid, gu, sems):
    step = pl.program_id(0)
    tiles, _, wide = hid.shape
    loads = [
        pltpu.make_async_copy(hid_ref.at[:, pl.ds(i * wide, wide)], hid.at[i], sems.at[i]) for i in range(tiles)
    ]

    @pl.when(step == 0)
    def _():
        for c in loads:
            c.start()

    inner = dot(low_ref[...], wd_ref[...], 1, 1).astype(BF).astype(F32)
    gate = gate_ref[...]
    sig = jax.nn.sigmoid(gate)
    act = gate * sig
    gg_ref[...] = (inner * up_ref[...] * (sig * (1.0 + gate * (1.0 - sig)))).astype(BF)
    up = (inner * act).astype(BF)
    gu_ref[...] = up
    rows = up.shape[0]
    gu[pl.ds(pl.multiple_of(step * rows, rows), rows), :] = up

    @pl.when(step == pl.num_programs(0) - 1)
    def _():
        for c in loads:
            c.wait()
        run = 2 * r
        per = wide // run

        @pl.loop(0, tiles)
        def _(i):
            product = dot(hid[i], gu[...], 0, 0).astype(BF)
            for p in range(per):
                chunk = i * per + p
                at = (lax.rem(chunk, nz) * 4 + chunk // nz) * run
                out_ref[pl.ds(pl.multiple_of(at, run), run), :] = product[p * run : (p + 1) * run]


def inner_back(low, gate, up, wd, hid):
    nz = lax.axis_size("cm")
    rows, width = low.shape
    cols = gate.shape[1]
    step = rows // 8
    wide = 256
    tiles = width // wide
    block = lambda c: pl.BlockSpec((step, c), lambda g: (g, 0))
    return pl.pallas_call(
        functools.partial(inner_back_kernel, nz, width // (8 * nz)),
        grid=(8,),
        out_shape=[
            jax.ShapeDtypeStruct((rows, cols), BF),
            jax.ShapeDtypeStruct((rows, cols), BF),
            jax.ShapeDtypeStruct((width, cols), BF),
        ],
        in_specs=[block(width), block(cols), block(cols), pl.BlockSpec(wd.shape, lambda g: (0, 0)), ANY],
        out_specs=[block(cols), block(cols), pl.BlockSpec((width, cols), lambda g: (0, 0))],
        scratch_shapes=[pltpu.VMEM((tiles, rows, wide), BF), pltpu.VMEM((rows, cols), BF), dma(tiles)],
        compiler_params=pltpu.CompilerParams(vmem_limit_bytes=60 * MIB),
        name="inner_back",
    )(low, gate, up, wd, hid)


def flat(ref):
    x = ref[...]
    return x.reshape(x.shape[-4] * x.shape[-2], x.shape[-1])


def heads_of(x):
    return [x[:, h * HD : (h + 1) * HD] for h in range(x.shape[1] // HD)]


def seen(n, j, z, slots):
    col = lax.broadcasted_iota(jnp.int32, (slots, slots), 0) + j * slots
    row = lax.broadcasted_iota(jnp.int32, (slots, slots), 1) + z * slots
    return jnp.logical_and(col <= row, col < n)


def attend_kernel(lens, q_ref, kv_ref, att_ref, low_ref, log_ref, scores, top, sums, acc):
    z = lax.axis_index("cm")
    n = lens[pl.program_id(0) * pl.num_programs(1) + pl.program_id(1)]
    q = flat(q_ref)
    slots = q.shape[0]
    qs = heads_of((q.astype(F32) * HD ** (-0.5)).astype(BF))
    top[...] = jnp.full_like(top, NEGATIVE)
    sums[...] = jnp.zeros_like(sums)
    acc[...] = jnp.zeros_like(acc)

    def score(j, _):
        k = flat(kv_ref.at[j])[:, :HD]
        mask = seen(n, j, z, slots)
        for h, qh in enumerate(qs):
            s = jnp.where(mask, dot(k, qh, 1, 1), NEGATIVE)
            scores[j, h] = s
            top[h : h + 1] = jnp.maximum(top[h : h + 1], jnp.max(s, 0, keepdims=True))
        return 0

    blocks = jnp.minimum(z + 1, (n + slots - 1) // slots)
    lax.fori_loop(0, blocks, score, 0)

    def weigh(j, _):
        v = flat(kv_ref.at[j])[:, HD:]
        for h in range(len(qs)):
            p = jnp.exp(scores[j, h] - top[h : h + 1])
            sums[h : h + 1] += jnp.sum(p, 0, keepdims=True)
            acc[h * HD : (h + 1) * HD] += dot(v, p.astype(BF), 0, 0)
        return 0

    lax.fori_loop(0, blocks, weigh, 0)
    out = jnp.concatenate([acc[h * HD : (h + 1) * HD] / sums[h : h + 1] for h in range(len(qs))], 0)
    att_ref[0, 0] = out
    low_ref[...] = out.T.astype(BF).reshape(low_ref.shape)
    log_ref[0, 0] = top[...] + jnp.log(sums[...])


def attend_back_kernel(lens, q_ref, kv_ref, do_ref, att_ref, log_ref, *rest):
    dq_ref, dkv_ref, acc = rest[-3:]
    z = lax.axis_index("cm")
    n = lens[pl.program_id(0) * pl.num_programs(1) + pl.program_id(1)]
    q = flat(q_ref)
    slots = q.shape[0]
    qs = heads_of((q.astype(F32) * HD ** (-0.5)).astype(BF))
    do = flat(do_ref)
    dos = heads_of(do)
    both = do.astype(F32).T * att_ref[0, 0]
    deltas = [jnp.sum(both[h * HD : (h + 1) * HD], 0, keepdims=True) for h in range(len(qs))]
    acc[...] = jnp.zeros_like(acc)

    def step(j, _):
        kv = flat(kv_ref.at[j])
        k, v = kv[:, :HD], kv[:, HD:]
        mask = seen(n, j, z, slots)
        dk = jnp.zeros((slots, HD), F32)
        dv = jnp.zeros((slots, HD), F32)
        for h, qh in enumerate(qs):
            s = jnp.where(mask, dot(k, qh, 1, 1), NEGATIVE)
            p = jnp.exp(s - log_ref[0, 0, h : h + 1])
            ds = (p * (dot(v, dos[h], 1, 1) - deltas[h])).astype(BF)
            acc[h * HD : (h + 1) * HD] += dot(k, ds, 0, 0)
            dk += dot(ds, qh)
            dv += dot(p.astype(BF), dos[h])
        out = jnp.concatenate([dk, dv], 1).astype(BF)
        dkv_ref[j] = out.reshape(dkv_ref.shape[1:])
        return 0

    live = jnp.where(z * slots < n, z + 1, 0)
    lax.fori_loop(0, live, step, 0)

    def nothing(j, _):
        dkv_ref[j] = jnp.zeros(dkv_ref.shape[1:], BF)
        return 0

    lax.fori_loop(live, z + 1, nothing, 0)
    dq_ref[...] = (acc[...] * HD ** (-0.5)).T.reshape(dq_ref.shape)


def attention_specs(seqs, block, wide, nz):
    own = lambda c: pl.BlockSpec((1, 2, 1, block, c), lambda f, s: (f, 0, s, 0, 0))
    every = pl.BlockSpec((nz, 1, 2, 1, block, 2 * HD), lambda f, s: (0, f, 0, s, 0, 0))
    turned = lambda c: pl.BlockSpec((1, 1, c, 2 * block), lambda f, s: (f, s, 0, 0))
    return own(wide), every, turned(wide), turned(wide // HD)


def attend(lens, q, kv, seqs, block):
    nz, rows, _ = kv.shape
    wide = q.shape[1]
    heads = wide // HD
    own, every, turned, logs = attention_specs(seqs, block, wide, nz)
    view = (4, 2, seqs, block)
    att, low, log = pl.pallas_call(
        attend_kernel,
        grid=(4, seqs),
        out_shape=[
            jax.ShapeDtypeStruct((4, seqs, wide, 2 * block), F32),
            jax.ShapeDtypeStruct((*view, wide), BF),
            jax.ShapeDtypeStruct((4, seqs, heads, 2 * block), F32),
        ],
        in_specs=[pl.BlockSpec(memory_space=pltpu.SMEM), own, every],
        out_specs=[turned, own, logs],
        scratch_shapes=[
            pltpu.VMEM((nz, heads, 2 * block, 2 * block), F32),
            pltpu.VMEM((heads, 2 * block), F32),
            pltpu.VMEM((heads, 2 * block), F32),
            pltpu.VMEM((wide, 2 * block), F32),
        ],
        compiler_params=pltpu.CompilerParams(vmem_limit_bytes=48 * MIB),
        name="attend",
    )(lens, q.reshape(*view, wide), kv.reshape(nz, *view, 2 * HD))
    return att, low.reshape(rows, wide), log


def attend_back(lens, q, kv, do, att, log, seqs, block, deps):
    nz, rows, _ = kv.shape
    wide = q.shape[1]
    own, every, turned, logs = attention_specs(seqs, block, wide, nz)
    view = (4, 2, seqs, block)
    dq, dkv = pl.pallas_call(
        attend_back_kernel,
        grid=(4, seqs),
        out_shape=[
            jax.ShapeDtypeStruct((*view, wide), F32),
            jax.ShapeDtypeStruct((nz, *view, 2 * HD), BF),
        ],
        in_specs=[pl.BlockSpec(memory_space=pltpu.SMEM), own, every, own, turned, logs] + [ANY] * len(deps),
        out_specs=[own, every],
        scratch_shapes=[pltpu.VMEM((wide, 2 * block), F32)],
        compiler_params=pltpu.CompilerParams(vmem_limit_bytes=48 * MIB),
        name="attend_back",
    )(lens, q.reshape(*view, wide), kv.reshape(nz, *view, 2 * HD), do.reshape(*view, wide), att, log, *deps)
    return dq.reshape(rows, wide), dkv.reshape(nz, rows, 2 * HD)


def rms_scale(field):
    return lax.rsqrt(jnp.mean(field * field, -1, keepdims=True) + EPSILON)


def norm_back(grad_normed, normed, scale_rows):
    return scale_rows * (grad_normed - normed * jnp.mean(grad_normed * normed, -1, keepdims=True))


def rows_of(x):
    nz = lax.axis_size("cm")
    _, r, c = x.shape
    x = gather_planes(x)
    return x.reshape(nz, 4, 2, r, c).transpose(1, 0, 2, 3, 4).reshape(nz * 8 * r, c)


def rows_first(g):
    nz = lax.axis_size("cm")
    rows, c = g.shape
    r = rows // (8 * nz)
    return g.astype(BF).reshape(4, nz, 2, r, c).transpose(1, 0, 2, 3, 4).reshape(nz * 8, r, c)


def on_device(
    tokens, lengths, cotangent, attn_gain, w_query, w_key, w_value, w_out, mlp_gain, w_gate, w_up, w_down
):
    seqs, block, width = tokens.shape
    nz = lax.axis_size("cm")
    rows = seqs * block
    r = w_query.shape[0]
    wide = HEADS // 8 * HD
    cm = lax.axis_index("cm")
    cl = lax.axis_index("cl")
    gain_two = mlp_gain.astype(F32)[:, None]
    pieces = nz if w_down.shape[0] % 128 == 0 else 1
    perm = [(c, (c % nz) * 2 + c // nz) for c in range(2 * nz)]
    home = [(t, s) for s, t in perm]

    def gained(w):
        return (w.astype(F32) * gain_two).astype(BF)

    pack = [w.reshape(r, 8, -1) for w in (w_query, w_key, w_value)]
    pack.append(jnp.broadcast_to(attn_gain[:, None, None], (r, 8, 2 * HD)))
    pack = jnp.concatenate(pack, -1).transpose(1, 0, 2)
    lens = jnp.broadcast_to(jnp.pad(lengths, (0, 128 - seqs))[None, None], (8, 8, 128))
    pack, lens = transfer(1, [part("slab", pack), part("slab", lens)])
    lens = lens[::2, 0, :seqs].reshape(-1)
    wg, wo = transfer(2, [part("cols", gained(w_gate), pieces=pieces), part("move", w_out)], (pack,))
    own = tokens.reshape(rows, width)
    tok_all, wu = transfer(3, [part("gather", own), part("cols", gained(w_up), pieces=pieces)], (wg,))
    pack = rows_of(pack)
    gain_row = pack[:, wide + 2 * HD].astype(F32)[None]
    wg = gather_planes(wg).reshape(width, -1)
    wo = gather_planes(wo)

    slot = cm * 2 * block + jnp.arange(2 * block, dtype=jnp.int32).reshape(2, block)
    cos, sin = tables(slot)
    hidden_one, q, kv = project(tok_all.reshape(8 * rows, width), gain_row, pack, wide, cos, sin)
    own_pos = cm * 2 * block + cl * block + jnp.arange(block, dtype=jnp.int32)
    valid = (own_pos[None, :] < lengths[:, None]).astype(F32)
    grad_out = (cotangent.astype(F32) * valid[..., None]).reshape(rows, width)
    grad_low, kv_all = transfer(
        4,
        [
            part("gather", grad_out.astype(BF)),
            part("up", kv),
        ],
    )
    grad_low = grad_low.reshape(8 * rows, width)
    wu = gather_planes(wu).reshape(width, -1)
    att, att_low, log = attend(lens, q, kv_all, seqs, block)

    resid_in = own.astype(F32)
    mid, down = transfer(5, [part("sum", dot(att_low, wo).astype(BF)), part("pass", w_down)], (wg,))
    wd = gather_planes(down if pieces > 1 else lax.ppermute(down, ("cm", "cl"), perm))
    resid_mid = resid_in + mid.astype(F32)
    scale_two = rms_scale(resid_mid)
    normed_two = resid_mid * scale_two
    hidden_two, gate_pre, up_pre, inner, wd_left, wd_right = transfer(
        6, [part("forward", normed_two.astype(BF), wg, wu, grad_low)]
    )
    hidden_two = hidden_two.reshape(8 * rows, width)
    wd = after(wd, (wd_left,))
    grad_gate, grad_up, grad_wu = inner_back(grad_low, gate_pre, up_pre, wd, hidden_two)
    e_two, grad_wg = transfer(7, [part("mlp", hidden_two, grad_gate, grad_up, wg, wu)], (grad_wu,))
    by_owner = lambda g: sum_planes(g.reshape(8 * nz, r, -1))
    wd_left, grad_wu, grad_wg = sum_planes(wd_left), by_owner(grad_wu), by_owner(grad_wg)
    grad_mid = grad_out + norm_back(e_two.astype(F32), normed_two, scale_two)
    grad_heads, grad_wo, out_part = transfer(
        8, [part("heads", grad_mid.astype(BF), wo, att_low), part("product", inner, wd)], (wd_left,)
    )
    dq, dkv = attend_back(lens, q, kv_all, grad_heads, att, log, seqs, block, (grad_wu,))
    dkv, out_sum, grad_wu = transfer(
        9, [part("down", dkv), part("sum", out_part), part("back", grad_wu, pieces=pieces)]
    )
    wd_right = after(wd_right, (dkv,))
    layer_out = (resid_mid + out_sum.astype(F32)).astype(BF)
    e_one, grad_qkv = project_back(dq, dkv, hidden_one, pack, cos, sin, (wd_right,))
    wd_right = sum_planes(wd_right)
    e_one, grad_wg = transfer(10, [part("sum", e_one), part("back", grad_wg, pieces=pieces)])
    grad_wo = sum_planes(grad_wo)
    grad_qkv = sum_planes(rows_first(grad_qkv))
    scale_one = rms_scale(resid_in)
    grad_tokens = grad_mid + norm_back(e_one.astype(F32) * gain_row, resid_in * scale_one, scale_one)
    grad_qkv, grad_wo = transfer(11, [part("slab", grad_qkv), part("home", grad_wo)], (e_one,))
    grad_wd = jnp.concatenate([wd_left, wd_right], 1)
    if pieces == 1:
        grad_wd = lax.ppermute(grad_wd, ("cm", "cl"), home)
    grad_qkv = grad_qkv.transpose(1, 0, 2).astype(F32)
    grad_wq = grad_qkv[..., :wide].reshape(r, 8 * wide)
    grad_wk = grad_qkv[..., wide : wide + HD].reshape(r, 8 * HD)
    grad_wv = grad_qkv[..., wide + HD :].reshape(r, 8 * HD)
    grad_wg, grad_wu = grad_wg.astype(F32), grad_wu.astype(F32)

    def gain_grad(pairs):
        return sum(jnp.sum(w.astype(F32) * g, -1) for w, g in pairs)

    gain_grad_one = gain_grad(((w_query, grad_wq), (w_key, grad_wk), (w_value, grad_wv))) / attn_gain.astype(F32)
    gain_grad_two = gain_grad(((w_gate, grad_wg), (w_up, grad_wu)))
    return (
        layer_out.reshape(seqs, block, width),
        grad_tokens.reshape(seqs, block, width).astype(BF),
        gain_grad_one,
        grad_wq,
        grad_wk,
        grad_wv,
        grad_wo.astype(F32),
        gain_grad_two,
        grad_wg * gain_two,
        grad_wu * gain_two,
        grad_wd.astype(F32),
    )


def solution(mesh):
    fsdp, ctx = mesh.devices.shape
    fine = Mesh(mesh.devices.reshape(fsdp // 2, 2, ctx // 2, 2), ("a", "core", "cm", "cl"))
    token = P(("a", "core"), ("cm", "cl"), None)
    vector = P(("a", "core", "cm", "cl"))
    matrix = P(("a", "core", "cm", "cl"), None)
    return jax.shard_map(
        on_device,
        mesh=fine,
        in_specs=(
            token,
            P(("a", "core")),
            token,
            vector,
            matrix,
            matrix,
            matrix,
            matrix,
            vector,
            matrix,
            matrix,
            matrix,
        ),
        out_specs=(token, token, vector, matrix, matrix, matrix, matrix, vector, matrix, matrix, matrix),
        check_vma=False,
    )
```

```python
import functools

import jax
import jax.numpy as jnp
from jax import lax
from jax.experimental import pallas as pl
from jax.experimental.pallas import tpu as pltpu
from jax.sharding import Mesh
from jax.sharding import PartitionSpec as P

HEADS = 32
KVH = 8
HD = 64
EPSILON = 1e-05
NEGATIVE = -1e30
BF = jnp.bfloat16
F32 = jnp.float32
GROUP = ("a", "core", "cl")
MESH = pl.DeviceIdType.MESH
ANY = pl.BlockSpec(memory_space=pl.ANY)
TILE = 32
MIB = 2**20


def dma(*shape):
    return pltpu.SemaphoreType.DMA(shape)


def places():
    return tuple(lax.axis_index(n) for n in GROUP)


def index_of(a, core, cl):
    return (a * 2 + core) * 2 + cl


def partners():
    a, core, cl = places()
    out = []
    for t in range(1, 8):
        at = (a ^ (t >> 2), core ^ ((t >> 1) & 1), cl ^ (t & 1))
        out.append((dict(zip(GROUP, at)), index_of(*at)))
    return out


def moved_to(c, nz):
    return lax.rem(c, nz), c // nz


def moved_from(c, nz):
    block = lax.rem(c, 2) * nz + c // 2
    return block // 2, lax.rem(block, 2)


def move_pair(nz, back):
    here = lax.axis_index("cm") * 2 + lax.axis_index("cl")
    pair = [dict(zip(("cm", "cl"), f(here, nz))) for f in (moved_to, moved_from)]
    if back:
        pair.reverse()
    return pair, pair[0]["cm"] * 2 + pair[0]["cl"] == here


def greet(whole, line, move, nz):
    barrier = pltpu.get_barrier_semaphore()

    def signal(device):
        pl.semaphore_signal(barrier, inc=1, device_id=device, device_id_type=MESH)

    if whole:
        base = [device for device, _ in partners()]
    else:
        base = [{n: 1 - lax.axis_index(n)} for n in GROUP]
    for device in base:
        signal(device)
    n = len(base)
    if line:
        z = lax.axis_index("cm")
        pl.when(z > 0)(lambda: signal({"cm": z - 1}))
        pl.when(z < nz - 1)(lambda: signal({"cm": z + 1}))
        edge = jnp.logical_or(z == 0, z == nz - 1)
        pl.when(edge)(lambda: pl.semaphore_wait(barrier, n + 1))
        pl.when(jnp.logical_not(edge))(lambda: pl.semaphore_wait(barrier, n + 2))
    elif move is not None:
        pair, stays = move_pair(nz, move)

        @pl.when(jnp.logical_not(stays))
        def _():
            for device in pair:
                signal(device)
            pl.semaphore_wait(barrier, n + 2)

        @pl.when(stays)
        def _():
            pl.semaphore_wait(barrier, n)

    else:
        pl.semaphore_wait(barrier, n)


def remote(src, dst, send, recv, device):
    if isinstance(device, str):
        device = {device: 1 - lax.axis_index(device)}
    return pltpu.make_async_remote_copy(
        src_ref=src, dst_ref=dst, send_sem=send, recv_sem=recv, device_id=device, device_id_type=MESH
    )


def gather_steps(x_ref, o_ref, local, ss, rs, ready=None):
    ready = ready or (lambda i: None)
    a, core, cl = places()
    half = x_ref.shape[0] // 2
    lo, hi, both = pl.ds(0, half), pl.ds(half, half), pl.ds(0, 2 * half)
    me = index_of(a, core, cl)
    sx = index_of(1 - a, core, cl)
    sy = index_of(a, core, 1 - cl)
    sd = index_of(1 - a, core, 1 - cl)
    other = 2 - 4 * core
    mine = pltpu.make_async_copy(x_ref, o_ref.at[me], local.at[0])

    def put(i, slot, part, name, src=None):
        src = o_ref.at[slot, part] if src is None else src
        return remote(src, o_ref.at[slot, part], ss.at[i], rs.at[i], name)

    sent = [
        put(0, me, lo, "a", x_ref.at[lo]),
        put(1, me, hi, "cl", x_ref.at[hi]),
        put(2, me, hi, "a", x_ref.at[hi]),
        put(3, me, lo, "cl", x_ref.at[lo]),
        put(4, me, both, "core", x_ref),
    ]
    for c in sent:
        c.start()
    mine.start()
    yield
    mine.wait()
    ready(me)

    def on(i, slot, part, name):
        c = put(i, slot, part, name)
        c.start()
        sent.append(c)

    put(0, sx, lo, "a").wait_recv()
    on(5, sx, lo, "cl")
    on(6, sx, lo, "core")
    put(1, sy, hi, "cl").wait_recv()
    on(7, sy, hi, "a")
    on(8, sy, hi, "core")
    put(4, me + other, both, "core").wait_recv()
    ready(me + other)
    yield
    put(2, sx, hi, "a").wait_recv()
    on(9, sx, hi, "core")
    put(3, sy, lo, "cl").wait_recv()
    on(10, sy, lo, "core")
    ready(sx)
    ready(sy)
    yield
    for i, slot, part in ((6, sx, lo), (9, sx, hi)):
        put(i, slot + other, part, "core").wait_recv()
    ready(sx + other)
    put(5, sd, lo, "cl").wait_recv()
    on(11, sd, lo, "core")
    put(7, sd, hi, "a").wait_recv()
    on(12, sd, hi, "core")
    yield
    for i, slot, part in ((8, sy, hi), (10, sy, lo)):
        put(i, slot + other, part, "core").wait_recv()
    ready(sy + other)
    ready(sd)
    for i, slot, part in ((11, sd, lo), (12, sd, hi)):
        put(i, slot + other, part, "core").wait_recv()
    ready(sd + other)
    for c in sent:
        c.wait_send()


def add_rows(dst, sources, n):
    @pl.loop(0, n // TILE)
    def _(i):
        part = pl.ds(pl.multiple_of(i * TILE, TILE), TILE)
        total = sources[0][part, :].astype(F32)
        for s in sources[1:]:
            total = total + s[part, :].astype(F32)
        dst[part, :] = total.astype(dst.dtype)


def plane_chips():
    a, _, cl = places()
    return (a, cl), (1 - a, cl), (a, 1 - cl), (1 - a, 1 - cl)


def sum_steps(x_ref, o_ref, mine, theirs, first, last, lsem, cs, cr, ss, rs):
    core = lax.axis_index("core")
    out, loc = {}, {}
    for p in (3, 1, 2, 0):
        ca, cc = plane_chips()[p]
        out[p] = remote(x_ref.at[index_of(ca, 1 - core, cc)], theirs.at[p], cs.at[p], cr.at[p], "core")
        out[p].start()
        loc[p] = pltpu.make_async_copy(x_ref.at[index_of(ca, core, cc)], mine.at[p], lsem.at[p])
        loc[p].start()
    yield
    yield from sum_rest(o_ref, mine, theirs, first, last, lsem, out, loc, ss, rs)


def sum_rest(o_ref, mine, theirs, first, last, lsem, out, loc, ss, rs, make=None):
    rows = mine.shape[1]
    half = rows // 2
    lo, hi = pl.ds(0, half), pl.ds(half, half)

    def chip_sum(p):
        if make is not None:
            make(p)
        out[p].wait_recv()
        if p in loc:
            loc[p].wait()
        add_rows(mine.at[p], (mine.at[p], theirs.at[p]), rows)

    chip_sum(3)
    xd = remote(mine.at[3, lo], first.at[0], ss.at[0], rs.at[0], "a")
    yd = remote(mine.at[3, hi], first.at[1], ss.at[1], rs.at[1], "cl")
    xd.start()
    yd.start()
    chip_sum(1)
    xo = remote(mine.at[1, lo], first.at[2], ss.at[2], rs.at[2], "a")
    xo.start()
    chip_sum(2)
    yo = remote(mine.at[2, hi], first.at[3], ss.at[3], rs.at[3], "cl")
    yo.start()
    chip_sum(0)
    yield
    xd.wait_recv()
    add_rows(mine.at[2, lo], (mine.at[2, lo], first.at[0]), half)
    y2 = remote(mine.at[2, lo], last.at[0], ss.at[4], rs.at[4], "cl")
    y2.start()
    yd.wait_recv()
    add_rows(mine.at[1, hi], (mine.at[1, hi], first.at[1]), half)
    x2 = remote(mine.at[1, hi], last.at[1], ss.at[5], rs.at[5], "a")
    x2.start()
    yield
    xo.wait_recv()
    add_rows(mine.at[0, lo], (mine.at[0, lo], first.at[2]), half)
    yo.wait_recv()
    add_rows(mine.at[0, hi], (mine.at[0, hi], first.at[3]), half)
    yield
    y2.wait_recv()
    add_rows(mine.at[0, lo], (mine.at[0, lo], last.at[0]), half)
    x2.wait_recv()
    add_rows(mine.at[0, hi], (mine.at[0, hi], last.at[1]), half)
    done = pltpu.make_async_copy(mine.at[0], o_ref, lsem.at[4])
    done.start()
    for c in (*out.values(), xd, yd, xo, yo, y2, x2):
        c.wait_send()
    done.wait()


def swap_steps(kind, pieces, src, dst, lsem, ss, rs):
    me = index_of(*places())
    copies = []
    for p in range(pieces):

        def block(f, p=p):
            return ((f // 2) * pieces + p) * 2 + lax.rem(f, 2) if pieces > 1 else f

        width = (dst if kind == "cols" else src).shape[-1] // pieces

        def cut(ref, i, width=width):
            return ref.at[:, pl.ds(pl.multiple_of(i * width, width), width)]

        def part(ref, i, p=p, width=width):
            return ref.at[i] if pieces == 1 else ref.at[i, :, pl.ds(p * width, width)]

        def source(f, block=block, cut=cut, part=part):
            return cut(src, block(f)) if kind == "cols" else part(src, f)

        target = cut(dst, block(me)) if kind == "back" else part(dst, me)
        for t, (device, index) in enumerate(partners()):
            copies.append(remote(source(index), target, ss.at[p, t], rs.at[p, t], device))
            copies[-1].start()
        copies.append(pltpu.make_async_copy(source(me), target, lsem.at[p]))
        copies[-1].start()
    yield
    yield
    yield
    yield
    for copy in copies:
        copy.wait()


def move_steps(nz, back, src, dst, lsem, ss, rs):
    pair, stays = move_pair(nz, back)
    mine = pltpu.make_async_copy(src, dst, lsem.at[0])
    away = remote(src, dst, ss.at[0], rs.at[0], pair[0])
    pl.when(stays)(mine.start)
    pl.when(jnp.logical_not(stays))(away.start)
    yield
    yield
    yield
    yield
    pl.when(stays)(mine.wait)
    pl.when(jnp.logical_not(stays))(away.wait)


def up_steps(nz, x_ref, o_ref, lsem, ss, rs):
    z = lax.axis_index("cm")
    mine = pltpu.make_async_copy(x_ref, o_ref.at[z], lsem.at[0])
    mine.start()

    def send(j, src):
        return remote(src, o_ref.at[j], ss.at[j], rs.at[j], {"cm": jnp.minimum(z + 1, nz - 1)})

    @pl.when(z < nz - 1)
    def _():
        send(z, x_ref).start()

    yield
    for i in range(1, nz):

        @pl.when(z >= i)
        def _(i=i):
            j = z - i
            send(j, o_ref.at[j]).wait_recv()

            @pl.when(z < nz - 1)
            def _():
                send(j, o_ref.at[j]).start()

        yield
    for i in range(nz):

        @pl.when(jnp.logical_and(z >= i, z < nz - 1))
        def _(i=i):
            send(z - i, x_ref).wait_send()

    mine.wait()


def pass_steps(src, dst, lsem):
    copy = pltpu.make_async_copy(src, dst, lsem.at[0])
    copy.start()
    yield
    yield
    yield
    copy.wait()


def down_steps(nz, x_ref, o_ref, mine, came, lsem, ss, rs):
    z = lax.axis_index("cm")
    rows = x_ref.shape[1]

    def load(j):
        return pltpu.make_async_copy(x_ref.at[j], mine.at[j], lsem.at[j])

    def send(j):
        return remote(mine.at[j], came.at[j], ss.at[j], rs.at[j], {"cm": jnp.maximum(z - 1, 0)})

    for j in range(nz):
        pl.when(z >= j)(lambda j=j: load(j).start())

    ends = [0, 1, 2, nz]
    for first, end in zip(ends, ends[1:]):

        @pl.when(z == nz - 1)
        def _(first=first, end=end):
            for j in range(first, end):
                load(j).wait()
                if j < nz - 1:
                    send(j).start()

        yield
    for j in range(nz - 1):

        @pl.when(jnp.logical_and(z >= j, z < nz - 1))
        def _(j=j):
            load(j).wait()
            send(j).wait_recv()
            add_rows(mine.at[j], (mine.at[j], came.at[j]), rows)
            pl.when(z > j)(send(j).start)

    yield
    done = pltpu.make_async_copy(mine.at[z], o_ref, lsem.at[nz])
    done.start()
    for j in range(nz):
        pl.when(z > j)(lambda j=j: send(j).wait_send())
    done.wait()


def row_loads(nz, src, dst, sems):
    run = dst.shape[0] // (4 * nz)
    copies = []
    for c in range(4 * nz):
        at = (c % nz * 4 + c // nz) * run
        copies.append(pltpu.make_async_copy(src.at[pl.ds(at, run)], dst.at[pl.ds(c * run, run)], sems.at[c]))
    return copies


def back_steps(nz, r, hid_ref, one_ref, two_ref, wone_ref, wtwo_ref, o_ref, out_ref, *scratch):
    hid, g, w, out, stage, theirs, first, last, gsem, wsem, osem, lsem, cs, cr, ss, rs = scratch
    tiles, _, wide = hid.shape
    run = 2 * r
    per = wide // run
    core = lax.axis_index("core")
    rows, width = theirs.shape[1:]
    loads = [pltpu.make_async_copy(one_ref, g.at[0], gsem.at[0]), pltpu.make_async_copy(two_ref, g.at[1], gsem.at[1])]
    loads += row_loads(nz, wone_ref, w.at[0], wsem.at[0]) + row_loads(nz, wtwo_ref, w.at[1], wsem.at[1])
    later = [
        pltpu.make_async_copy(hid_ref.at[:, pl.ds(i * wide, wide)], hid.at[i], gsem.at[2 + i]) for i in range(tiles)
    ]
    for c in loads + later:
        c.start()
    for c in loads:
        c.wait()

    def blocks(p):
        ca, cc = plane_chips()[p]

        @pl.loop(0, 2)
        def _(n):
            to = jnp.where(n == 0, 1 - core, core)
            first_row = pl.multiple_of(index_of(ca, to, cc) * rows, rows)
            for c in range(0, width, width // 2):
                part = pl.ds(c, width // 2)
                e = dot(g[0, pl.ds(first_row, rows), :], w[0, part, :], 1, 1)
                e += dot(g[1, pl.ds(first_row, rows), :], w[1, part, :], 1, 1)
                stage[n, p, :, part] = e.astype(BF)

            @pl.when(n == 0)
            def _():
                out_core[p].start()

    out_core = {p: remote(stage.at[0, p], theirs.at[p], cs.at[p], cr.at[p], "core") for p in range(4)}

    def store(i, p):
        chunk = i * per + p
        at = (lax.rem(chunk, nz) * 4 + chunk // nz) * run
        return pltpu.make_async_copy(
            out.at[i, pl.ds(p * run, run)], out_ref.at[pl.ds(pl.multiple_of(at, run), run)], osem.at[i, p]
        )

    def products(lo, hi):
        @pl.loop(lo, hi)
        def _(i):
            out[i] = dot(hid[i], g[0], 0, 0).astype(BF)
            for p in range(per):
                store(i, p).start()

    summing = sum_rest(o_ref, stage.at[1], theirs, first, last, lsem, out_core, {}, ss, rs, blocks)
    for n in range(4):
        next(summing, None)
        if n == 0:
            for c in later:
                c.wait()
        products(n * tiles // 4, (n + 1) * tiles // 4)
    for _ in summing:
        pass

    @pl.loop(0, tiles)
    def _(i):
        for p in range(per):
            store(i, p).wait()

    yield


def forward_steps(nz, x_ref, wone_ref, wtwo_ref, low_ref, all_ref, gate_ref, up_ref, in_ref, *rest):
    g_refs, scratch = rest[:2], rest[2:]
    buf, w, low, inner, stage, out, wsem, asem, gsem, osem, local, ss, rs = scratch
    rows = buf.shape[1]
    loads = row_loads(nz, wone_ref, w.at[0], wsem.at[0]) + row_loads(nz, wtwo_ref, w.at[1], wsem.at[1])
    load_low = pltpu.make_async_copy(low_ref, low, osem.at[0])
    done = []

    def keep(src, dst, sem):
        done.append(pltpu.make_async_copy(src, dst, sem))
        done[-1].start()

    def ready(i):
        n = len(done) // 4
        if n == 0:
            for c in loads:
                c.wait()
        block = buf[i]
        part = pl.ds(pl.multiple_of(i * rows, rows), rows)
        gate = dot(block, w[0])
        up = dot(block, w[1])
        stage[n, 0] = gate
        stage[n, 1] = up
        inner[part, :] = (gate * jax.nn.sigmoid(gate) * up).astype(BF)
        keep(buf.at[i], all_ref.at[i], asem.at[n])
        keep(stage.at[n, 0], gate_ref.at[part], gsem.at[n, 0])
        keep(stage.at[n, 1], up_ref.at[part], gsem.at[n, 1])
        keep(inner.at[part], in_ref.at[part], gsem.at[n, 2])

    first = gather_steps(x_ref, buf, local, ss, rs, ready)
    next(first)
    for c in (*loads, load_low):
        c.start()
    for _ in first:
        pass
    load_low.wait()
    tiles, wide, width = out.shape
    half = width // 2

    def store(t, n):
        return pltpu.make_async_copy(
            out.at[t, :, pl.ds(n * half, half)], g_refs[n].at[pl.ds(t * wide, wide)], osem.at[1 + t * 2 + n]
        )

    for t in range(tiles):
        left = inner[:, t * wide : (t + 1) * wide]
        for n in range(2):
            out[t, :, n * half : (n + 1) * half] = dot(left, low[:, n * half : (n + 1) * half], 0, 0).astype(BF)
            store(t, n).start()
    for t in range(tiles):
        for n in range(2):
            store(t, n).wait()
    for c in done:
        c.wait()
    yield


def product_steps(a_ref, left_ref, right_ref, o_ref, a, b, out, lsem, osem):
    half = b.shape[1] // 2
    tiles, rows, _ = out.shape
    loads = [
        pltpu.make_async_copy(a_ref, a, lsem.at[0]),
        pltpu.make_async_copy(left_ref, b.at[:, pl.ds(0, left_ref.shape[1])], lsem.at[1]),
        pltpu.make_async_copy(right_ref, b.at[:, pl.ds(left_ref.shape[1], right_ref.shape[1])], lsem.at[2]),
    ]
    for c in loads:
        c.start()
    for c in loads:
        c.wait()

    def store(i):
        return pltpu.make_async_copy(out.at[i], o_ref.at[pl.ds(pl.multiple_of(i * rows, rows), rows)], osem.at[i])

    for lo, hi in ((0, tiles // 2), (tiles // 2, tiles)):

        @pl.loop(lo, hi)
        def _(i):
            left = a[pl.ds(pl.multiple_of(i * rows, rows), rows), :]
            for c in (0, half):
                out[i, :, c : c + half] = dot(left, b[:, c : c + half]).astype(BF)
            store(i).start()

        yield

    @pl.loop(0, tiles)
    def _(i):
        store(i).wait()


def heads_steps(x_ref, wo_ref, low_ref, heads_ref, g_ref, buf, wo, low, heads, total, g, lsem, local, ss, rs):
    loads = [pltpu.make_async_copy(wo_ref, wo, lsem.at[0]), pltpu.make_async_copy(low_ref, low, lsem.at[1])]
    for c in loads:
        c.start()
    rows = buf.shape[1]
    seen_blocks = []

    def ready(i):
        if not seen_blocks:
            for c in loads:
                c.wait()
            total[...] = jnp.zeros_like(total)
        seen_blocks.append(i)
        block = buf[i]
        part = pl.ds(pl.multiple_of(i * rows, rows), rows)
        heads[part, :] = dot(block, wo[...], 1, 1).astype(BF)
        total[...] += dot(low[part, :], block, 0, 0)

    yield from gather_steps(x_ref, buf, local, ss, rs, ready)
    g[...] = total[...].astype(BF)
    stores = [pltpu.make_async_copy(heads, heads_ref, lsem.at[2]), pltpu.make_async_copy(g, g_ref, lsem.at[3])]
    for c in stores:
        c.start()
    for c in stores:
        c.wait()


def part(kind, *xs, **how):
    nz = lax.axis_size("cm")
    x = xs[0]
    like = lambda *shape: jax.ShapeDtypeStruct(shape, x.dtype)
    vmem = lambda *shape: pltpu.VMEM(shape, x.dtype)
    if kind == "gather":
        rows, cols = x.shape
        return kind, gather_steps, xs, [like(8, rows, cols)], [dma(1), dma(13), dma(13)]
    if kind == "sum":
        rows, cols = x.shape[0] // 8, x.shape[1]
        scratch = [vmem(n, m, cols) for n, m in ((4, rows), (4, rows), (4, rows // 2), (2, rows // 2))]
        scratch += [dma(5), dma(4), dma(4), dma(6), dma(6)]
        return kind, sum_steps, [x.reshape(8, rows, cols)], [like(rows, cols)], scratch
    if kind == "up":
        return kind, functools.partial(up_steps, nz), xs, [like(nz, *x.shape)], [dma(1), dma(nz), dma(nz)]
    if kind == "pass":
        return kind, pass_steps, xs, [like(*x.shape)], [dma(1)]
    if kind == "down":
        scratch = [vmem(*x.shape)] * 2 + [dma(nz + 1), dma(nz), dma(nz)]
        return kind, functools.partial(down_steps, nz), xs, [like(*x.shape[1:])], scratch
    if kind in ("move", "home"):
        return kind, functools.partial(move_steps, nz, kind == "home"), xs, [like(*x.shape)], [dma(1), dma(1), dma(1)]
    if kind == "mlp":
        rows, width = x.shape
        cols = xs[1].shape[1]
        r = width // (8 * nz)
        wide = 256
        tiles = width // wide
        block = rows // 8
        scratch = [vmem(tiles, rows, wide), vmem(2, rows, cols), vmem(2, width, cols), vmem(tiles, wide, cols)]
        scratch += [vmem(2, 4, block, width), vmem(4, block, width), vmem(4, block // 2, width)]
        scratch += [vmem(2, block // 2, width), dma(2 + tiles), dma(2, 4 * nz), dma(tiles, wide // (2 * r))]
        scratch += [dma(5), dma(4), dma(4), dma(6), dma(6)]
        return kind, functools.partial(back_steps, nz, r), xs, [like(block, width), like(width, cols)], scratch
    if kind == "forward":
        rows, width = x.shape
        cols = xs[1].shape[1]
        wide = min(256, cols)
        tiles = cols // wide
        full = [jax.ShapeDtypeStruct((8 * rows, cols), F32)] * 2
        outs = [like(8, rows, width), *full, like(8 * rows, cols), *[like(cols, width // 2)] * 2]
        scratch = [vmem(8, rows, width), vmem(2, width, cols), vmem(8 * rows, width), vmem(8 * rows, cols)]
        scratch += [pltpu.VMEM((8, 2, rows, cols), F32), vmem(tiles, wide, width)]
        scratch += [dma(2, 4 * nz), dma(8), dma(8, 3), dma(1 + 2 * tiles), dma(1), dma(13), dma(13)]
        return kind, functools.partial(forward_steps, nz), xs, outs, scratch
    if kind == "product":
        rows, cols = x.shape[0], xs[1].shape[1] + xs[2].shape[1]
        scratch = [vmem(*x.shape), vmem(x.shape[1], cols), vmem(8, rows // 8, cols), dma(3), dma(8)]
        return kind, product_steps, xs, [like(rows, cols)], scratch
    if kind == "heads":
        rows, cols = x.shape
        wide = xs[1].shape[0]
        scratch = [vmem(8, rows, cols), vmem(wide, cols), vmem(8 * rows, wide), vmem(8 * rows, wide)]
        scratch += [pltpu.VMEM((wide, cols), F32), vmem(wide, cols), dma(4), dma(1), dma(13), dma(13)]
        return kind, heads_steps, xs, [like(8 * rows, wide), like(wide, cols)], scratch
    pieces = how.get("pieces", 1)
    shape = x.shape
    if kind == "cols":
        shape = (8, x.shape[0], x.shape[1] // 8)
    elif kind == "back":
        shape = (x.shape[1], 8 * x.shape[2])
    scratch = [dma(pieces), dma(pieces, 7), dma(pieces, 7)]
    return kind, functools.partial(swap_steps, kind, pieces), xs, [like(*shape)], scratch


def transfer(cid, parts, deps=()):
    nz = lax.axis_size("cm")
    kinds = [p[0] for p in parts]
    operands = [x for p in parts for x in p[2]]
    results = [o for p in parts for o in p[3]]
    moves = [k == "home" for k in kinds if k in ("move", "home")]
    whole = any(k in ("slab", "cols", "back") for k in kinds)
    line = any(k in ("up", "down") for k in kinds)

    def kernel(*refs):
        ins = list(refs[: len(operands)])
        rest = list(refs[len(operands) + len(deps) :])
        outs, scratch = rest[: len(results)], rest[len(results) :]

        def take(refs, n):
            out = refs[:n]
            del refs[:n]
            return out

        greet(whole, line, moves[0] if moves else None, nz)
        running = []
        for _, steps, xs, shapes, own in parts:
            running.append(steps(*take(ins, len(xs)), *take(outs, len(shapes)), *take(scratch, len(own))))
        while running:
            still = []
            for steps in running:
                try:
                    next(steps)
                except StopIteration:
                    continue
                still.append(steps)
            running = still

    return pl.pallas_call(
        kernel,
        out_shape=results,
        in_specs=[ANY] * (len(operands) + len(deps)),
        out_specs=[ANY] * len(results),
        scratch_shapes=[s for p in parts for s in p[4]],
        compiler_params=pltpu.CompilerParams(
            collective_id=cid, has_side_effects=True, vmem_limit_bytes=60 * MIB
        ),
        name="_".join(kinds) + str(cid),
    )(*operands, *deps)


def after(x, deps):
    return pl.pallas_call(
        lambda *refs: None,
        out_shape=jax.ShapeDtypeStruct(x.shape, x.dtype),
        in_specs=[ANY] * (1 + len(deps)),
        out_specs=ANY,
        input_output_aliases={0: 0},
        name="after",
    )(x, *deps)


def sum_planes(g):
    return lax.psum_scatter(g, "cm", scatter_dimension=0, tiled=True)


def gather_planes(x):
    return lax.all_gather(x, "cm", axis=0, tiled=True)


def dot(a, b, left=1, right=0):
    return lax.dot_general(a, b, (((left,), (right,)), ((), ())), preferred_element_type=F32)


def rope(u, cos, sin):
    width = u.shape[-1]
    lane = lax.broadcasted_iota(jnp.int32, u.shape, 1)
    other = jnp.where(lane % HD < HD // 2, pltpu.roll(u, width - HD // 2, 1), pltpu.roll(u, HD // 2, 1))
    return u * cos + other * sin


def tables(positions):
    lane = jnp.arange(2 * HD)
    frequency = 500000.0 ** (-(lane % (HD // 2)).astype(F32) * 2.0 / HD)
    angles = positions.astype(F32)[..., None] * frequency
    return jnp.cos(angles), jnp.where(lane % HD < HD // 2, -1.0, 1.0) * jnp.sin(angles)


def project_kernel(x_ref, gain_ref, w_ref, cos_ref, sin_ref, hid_ref, q_ref, kv_ref):
    x = x_ref[...].astype(F32)
    hid = (x * lax.rsqrt(jnp.mean(x * x, -1, keepdims=True) + EPSILON) * gain_ref[...]).astype(BF)
    hid_ref[...] = hid
    u = dot(hid, w_ref[...])
    times = x.shape[0] // cos_ref.shape[1]
    cos = jnp.concatenate([cos_ref[0]] * times, 0)
    sin = jnp.concatenate([sin_ref[0]] * times, 0)
    wide = q_ref.shape[-1]
    copies = wide // (2 * HD)
    q_ref[...] = rope(u[:, :wide], jnp.concatenate([cos] * copies, 1), jnp.concatenate([sin] * copies, 1)).astype(BF)
    kv = u[:, wide:]
    lane = lax.broadcasted_iota(jnp.int32, kv.shape, 1)
    kv_ref[...] = jnp.where(lane < HD, rope(kv, cos, sin), kv).astype(BF)


def project(x, gain, w, wide, cos, sin):
    rows, width = x.shape
    step = rows // 8
    block = cos.shape[1]
    table = pl.BlockSpec((1, block, 2 * HD), lambda g: (g % 2, 0, 0))
    return pl.pallas_call(
        project_kernel,
        grid=(8,),
        out_shape=[jax.ShapeDtypeStruct((rows, c), BF) for c in (width, wide, 2 * HD)],
        in_specs=[
            pl.BlockSpec((step, width), lambda g: (g, 0)),
            pl.BlockSpec((1, width), lambda g: (0, 0)),
            pl.BlockSpec((width, wide + 2 * HD), lambda g: (0, 0)),
            table,
            table,
        ],
        out_specs=[pl.BlockSpec((step, c), lambda g: (g, 0)) for c in (width, wide, 2 * HD)],
        compiler_params=pltpu.CompilerParams(vmem_limit_bytes=48 * MIB),
        name="project",
    )(x, gain, w, cos, sin)


def project_back_kernel(dq_ref, dkv_ref, hid_ref, w_ref, cos_ref, sin_ref, *rest):
    e_ref, g_ref, total = rest[-3:]
    step = pl.program_id(0)

    @pl.when(step == 0)
    def _():
        total[...] = jnp.zeros_like(total)

    dq = dq_ref[...]
    times = dq.shape[0] // cos_ref.shape[1]
    cos = jnp.concatenate([cos_ref[0]] * times, 0)
    sin = -jnp.concatenate([sin_ref[0]] * times, 0)
    copies = dq.shape[1] // (2 * HD)
    dq = rope(dq, jnp.concatenate([cos] * copies, 1), jnp.concatenate([sin] * copies, 1))
    dkv = dkv_ref[...].astype(F32)
    lane = lax.broadcasted_iota(jnp.int32, dkv.shape, 1)
    dkv = jnp.where(lane < HD, rope(dkv, cos, sin), dkv)
    rows = jnp.concatenate([dq.astype(BF), dkv.astype(BF)], 1)
    e_ref[...] = dot(rows, w_ref[...], 1, 1).astype(BF)
    total[...] += dot(hid_ref[...], rows, 0, 0)

    @pl.when(step == pl.num_programs(0) - 1)
    def _():
        g_ref[...] = total[...].astype(BF)


def project_back(dq, dkv, hid, w, cos, sin, deps):
    rows, width = hid.shape
    step = rows // 8
    shape = (width, dq.shape[1] + 2 * HD)
    block = cos.shape[1]
    table = pl.BlockSpec((1, block, 2 * HD), lambda g: (g % 2, 0, 0))
    return pl.pallas_call(
        project_back_kernel,
        grid=(8,),
        out_shape=[jax.ShapeDtypeStruct((rows, width), BF), jax.ShapeDtypeStruct(shape, BF)],
        in_specs=[
            pl.BlockSpec((step, dq.shape[1]), lambda g: (g, 0)),
            pl.BlockSpec((step, 2 * HD), lambda g: (g, 0)),
            pl.BlockSpec((step, width), lambda g: (g, 0)),
            pl.BlockSpec(shape, lambda g: (0, 0)),
            table,
            table,
        ]
        + [ANY] * len(deps),
        out_specs=[pl.BlockSpec((step, width), lambda g: (g, 0)), pl.BlockSpec(shape, lambda g: (0, 0))],
        scratch_shapes=[pltpu.VMEM(shape, F32)],
        compiler_params=pltpu.CompilerParams(vmem_limit_bytes=48 * MIB),
        name="project_back",
    )(dq, dkv, hid, w, cos, sin, *deps)


def inner_back_kernel(nz, r, low_ref, gate_ref, up_ref, wl_ref, wr_ref, hid_ref, gg_ref, gu_ref, out_ref, hid, gu, sems):
    step = pl.program_id(0)
    tiles, _, wide = hid.shape
    loads = [
        pltpu.make_async_copy(hid_ref.at[:, pl.ds(i * wide, wide)], hid.at[i], sems.at[i]) for i in range(tiles)
    ]

    @pl.when(step == 0)
    def _():
        for c in loads:
            c.start()

    half = wl_ref.shape[1]
    inner = dot(low_ref[:, :half], wl_ref[...], 1, 1) + dot(low_ref[:, half:], wr_ref[...], 1, 1)
    inner = inner.astype(BF).astype(F32)
    gate = gate_ref[...]
    sig = jax.nn.sigmoid(gate)
    act = gate * sig
    gg_ref[...] = (inner * up_ref[...] * (sig * (1.0 + gate * (1.0 - sig)))).astype(BF)
    up = (inner * act).astype(BF)
    gu_ref[...] = up
    rows = up.shape[0]
    gu[pl.ds(pl.multiple_of(step * rows, rows), rows), :] = up

    @pl.when(step == pl.num_programs(0) - 1)
    def _():
        for c in loads:
            c.wait()
        run = 2 * r
        per = wide // run

        @pl.loop(0, tiles)
        def _(i):
            product = dot(hid[i], gu[...], 0, 0).astype(BF)
            for p in range(per):
                chunk = i * per + p
                at = (lax.rem(chunk, nz) * 4 + chunk // nz) * run
                out_ref[pl.ds(pl.multiple_of(at, run), run), :] = product[p * run : (p + 1) * run]


def inner_back(low, gate, up, wl, wr, hid):
    nz = lax.axis_size("cm")
    rows, width = low.shape
    cols = gate.shape[1]
    step = rows // 8
    wide = 256
    tiles = width // wide
    block = lambda c: pl.BlockSpec((step, c), lambda g: (g, 0))
    return pl.pallas_call(
        functools.partial(inner_back_kernel, nz, width // (8 * nz)),
        grid=(8,),
        out_shape=[
            jax.ShapeDtypeStruct((rows, cols), BF),
            jax.ShapeDtypeStruct((rows, cols), BF),
            jax.ShapeDtypeStruct((width, cols), BF),
        ],
        in_specs=[block(width), block(cols), block(cols)] + [pl.BlockSpec(w.shape, lambda g: (0, 0)) for w in (wl, wr)] + [ANY],
        out_specs=[block(cols), block(cols), pl.BlockSpec((width, cols), lambda g: (0, 0))],
        scratch_shapes=[pltpu.VMEM((tiles, rows, wide), BF), pltpu.VMEM((rows, cols), BF), dma(tiles)],
        compiler_params=pltpu.CompilerParams(vmem_limit_bytes=60 * MIB),
        name="inner_back",
    )(low, gate, up, wl, wr, hid)


def flat(ref):
    x = ref[...]
    return x.reshape(x.shape[-4] * x.shape[-2], x.shape[-1])


def heads_of(x):
    return [x[:, h * HD : (h + 1) * HD] for h in range(x.shape[1] // HD)]


def seen(n, j, z, slots):
    col = lax.broadcasted_iota(jnp.int32, (slots, slots), 0) + j * slots
    row = lax.broadcasted_iota(jnp.int32, (slots, slots), 1) + z * slots
    return jnp.logical_and(col <= row, col < n)


def attend_kernel(lens, q_ref, kv_ref, att_ref, low_ref, log_ref, scores, top, sums, acc):
    z = lax.axis_index("cm")
    n = lens[pl.program_id(0) * pl.num_programs(1) + pl.program_id(1)]
    q = flat(q_ref)
    slots = q.shape[0]
    qs = heads_of((q.astype(F32) * HD ** (-0.5)).astype(BF))
    top[...] = jnp.full_like(top, NEGATIVE)
    sums[...] = jnp.zeros_like(sums)
    acc[...] = jnp.zeros_like(acc)

    def score(j, _):
        k = flat(kv_ref.at[j])[:, :HD]
        mask = seen(n, j, z, slots)
        for h, qh in enumerate(qs):
            s = jnp.where(mask, dot(k, qh, 1, 1), NEGATIVE)
            scores[j, h] = s
            top[h : h + 1] = jnp.maximum(top[h : h + 1], jnp.max(s, 0, keepdims=True))
        return 0

    blocks = jnp.minimum(z + 1, (n + slots - 1) // slots)
    lax.fori_loop(0, blocks, score, 0)

    def weigh(j, _):
        v = flat(kv_ref.at[j])[:, HD:]
        for h in range(len(qs)):
            p = jnp.exp(scores[j, h] - top[h : h + 1])
            sums[h : h + 1] += jnp.sum(p, 0, keepdims=True)
            acc[h * HD : (h + 1) * HD] += dot(v, p.astype(BF), 0, 0)
        return 0

    lax.fori_loop(0, blocks, weigh, 0)
    out = jnp.concatenate([acc[h * HD : (h + 1) * HD] / sums[h : h + 1] for h in range(len(qs))], 0)
    att_ref[0, 0] = out
    low_ref[...] = out.T.astype(BF).reshape(low_ref.shape)
    log_ref[0, 0] = top[...] + jnp.log(sums[...])


def attend_back_kernel(lens, q_ref, kv_ref, do_ref, att_ref, log_ref, *rest):
    dq_ref, dkv_ref, acc = rest[-3:]
    z = lax.axis_index("cm")
    n = lens[pl.program_id(0) * pl.num_programs(1) + pl.program_id(1)]
    q = flat(q_ref)
    slots = q.shape[0]
    qs = heads_of((q.astype(F32) * HD ** (-0.5)).astype(BF))
    do = flat(do_ref)
    dos = heads_of(do)
    both = do.astype(F32).T * att_ref[0, 0]
    deltas = [jnp.sum(both[h * HD : (h + 1) * HD], 0, keepdims=True) for h in range(len(qs))]
    acc[...] = jnp.zeros_like(acc)

    def step(j, _):
        kv = flat(kv_ref.at[j])
        k, v = kv[:, :HD], kv[:, HD:]
        mask = seen(n, j, z, slots)
        dk = jnp.zeros((slots, HD), F32)
        dv = jnp.zeros((slots, HD), F32)
        for h, qh in enumerate(qs):
            s = jnp.where(mask, dot(k, qh, 1, 1), NEGATIVE)
            p = jnp.exp(s - log_ref[0, 0, h : h + 1])
            ds = (p * (dot(v, dos[h], 1, 1) - deltas[h])).astype(BF)
            acc[h * HD : (h + 1) * HD] += dot(k, ds, 0, 0)
            dk += dot(ds, qh)
            dv += dot(p.astype(BF), dos[h])
        out = jnp.concatenate([dk, dv], 1).astype(BF)
        dkv_ref[j] = out.reshape(dkv_ref.shape[1:])
        return 0

    live = jnp.where(z * slots < n, z + 1, 0)
    lax.fori_loop(0, live, step, 0)

    def nothing(j, _):
        dkv_ref[j] = jnp.zeros(dkv_ref.shape[1:], BF)
        return 0

    lax.fori_loop(live, z + 1, nothing, 0)
    dq_ref[...] = (acc[...] * HD ** (-0.5)).T.reshape(dq_ref.shape)


def attention_specs(seqs, block, wide, nz):
    own = lambda c: pl.BlockSpec((1, 2, 1, block, c), lambda f, s: (f, 0, s, 0, 0))
    every = pl.BlockSpec((nz, 1, 2, 1, block, 2 * HD), lambda f, s: (0, f, 0, s, 0, 0))
    turned = lambda c: pl.BlockSpec((1, 1, c, 2 * block), lambda f, s: (f, s, 0, 0))
    return own(wide), every, turned(wide), turned(wide // HD)


def attend(lens, q, kv, seqs, block):
    nz, rows, _ = kv.shape
    wide = q.shape[1]
    heads = wide // HD
    own, every, turned, logs = attention_specs(seqs, block, wide, nz)
    view = (4, 2, seqs, block)
    att, low, log = pl.pallas_call(
        attend_kernel,
        grid=(4, seqs),
        out_shape=[
            jax.ShapeDtypeStruct((4, seqs, wide, 2 * block), F32),
            jax.ShapeDtypeStruct((*view, wide), BF),
            jax.ShapeDtypeStruct((4, seqs, heads, 2 * block), F32),
        ],
        in_specs=[pl.BlockSpec(memory_space=pltpu.SMEM), own, every],
        out_specs=[turned, own, logs],
        scratch_shapes=[
            pltpu.VMEM((nz, heads, 2 * block, 2 * block), F32),
            pltpu.VMEM((heads, 2 * block), F32),
            pltpu.VMEM((heads, 2 * block), F32),
            pltpu.VMEM((wide, 2 * block), F32),
        ],
        compiler_params=pltpu.CompilerParams(vmem_limit_bytes=48 * MIB),
        name="attend",
    )(lens, q.reshape(*view, wide), kv.reshape(nz, *view, 2 * HD))
    return att, low.reshape(rows, wide), log


def attend_back(lens, q, kv, do, att, log, seqs, block, deps):
    nz, rows, _ = kv.shape
    wide = q.shape[1]
    own, every, turned, logs = attention_specs(seqs, block, wide, nz)
    view = (4, 2, seqs, block)
    dq, dkv = pl.pallas_call(
        attend_back_kernel,
        grid=(4, seqs),
        out_shape=[
            jax.ShapeDtypeStruct((*view, wide), F32),
            jax.ShapeDtypeStruct((nz, *view, 2 * HD), BF),
        ],
        in_specs=[pl.BlockSpec(memory_space=pltpu.SMEM), own, every, own, turned, logs] + [ANY] * len(deps),
        out_specs=[own, every],
        scratch_shapes=[pltpu.VMEM((wide, 2 * block), F32)],
        compiler_params=pltpu.CompilerParams(vmem_limit_bytes=48 * MIB),
        name="attend_back",
    )(lens, q.reshape(*view, wide), kv.reshape(nz, *view, 2 * HD), do.reshape(*view, wide), att, log, *deps)
    return dq.reshape(rows, wide), dkv.reshape(nz, rows, 2 * HD)


def rms_scale(field):
    return lax.rsqrt(jnp.mean(field * field, -1, keepdims=True) + EPSILON)


def norm_back(grad_normed, normed, scale_rows):
    return scale_rows * (grad_normed - normed * jnp.mean(grad_normed * normed, -1, keepdims=True))


def rows_first(g):
    nz = lax.axis_size("cm")
    rows, c = g.shape
    r = rows // (8 * nz)
    return g.astype(BF).reshape(4, nz, 2, r, c).transpose(1, 0, 2, 3, 4).reshape(nz * 8, r, c)


def on_device(
    tokens, lengths, cotangent, attn_gain, w_query, w_key, w_value, w_out, mlp_gain, w_gate, w_up, w_down
):
    seqs, block, width = tokens.shape
    nz = lax.axis_size("cm")
    rows = seqs * block
    r = w_query.shape[0]
    wide = HEADS // 8 * HD
    cm = lax.axis_index("cm")
    cl = lax.axis_index("cl")
    gain_two = mlp_gain.astype(F32)[:, None]
    pieces = nz if w_down.shape[0] % 128 == 0 else 1
    perm = [(c, (c % nz) * 2 + c // nz) for c in range(2 * nz)]
    home = [(t, s) for s, t in perm]

    def gained(w):
        return (w.astype(F32) * gain_two).astype(BF)

    down = w_down if pieces > 1 else lax.ppermute(w_down, ("cm", "cl"), perm)
    wd_one = gather_planes(down[:, : width // 4])
    pack = [w.reshape(r, 8, -1) for w in (w_query, w_key, w_value)]
    pack.append(jnp.broadcast_to(attn_gain[:, None, None], (r, 8, 2 * HD)))
    pack = jnp.concatenate(pack, -1).transpose(1, 0, 2)
    lens = jnp.broadcast_to(jnp.pad(lengths, (0, 128 - seqs))[None, None], (8, 8, 128))
    pack, lens = transfer(1, [part("slab", pack), part("slab", lens)])
    lens = lens[::2, 0, :seqs].reshape(-1)
    wg, wo = transfer(2, [part("cols", gained(w_gate), pieces=pieces), part("move", w_out)], (pack,))
    own = tokens.reshape(rows, width)
    tok_all, wu = transfer(
        3, [part("gather", own), part("cols", gained(w_up), pieces=pieces)], (wg, wd_one)
    )
    pack = gather_planes(pack).reshape(nz, 4, 2 * r, -1).transpose(1, 0, 2, 3).reshape(width, -1)
    gain_row = pack[:, wide + 2 * HD].astype(F32)[None]
    wg = gather_planes(wg).reshape(width, -1)
    wo = gather_planes(wo)

    slot = cm * 2 * block + jnp.arange(2 * block, dtype=jnp.int32).reshape(2, block)
    cos, sin = tables(slot)
    hidden_one, q, kv = project(tok_all.reshape(8 * rows, width), gain_row, pack, wide, cos, sin)
    own_pos = cm * 2 * block + cl * block + jnp.arange(block, dtype=jnp.int32)
    valid = (own_pos[None, :] < lengths[:, None]).astype(F32)
    grad_out = (cotangent.astype(F32) * valid[..., None]).reshape(rows, width)
    grad_low, kv_all = transfer(
        4,
        [
            part("gather", grad_out.astype(BF)),
            part("up", kv),
        ],
    )
    grad_low = grad_low.reshape(8 * rows, width)
    wu = gather_planes(wu).reshape(width, -1)
    att, att_low, log = attend(lens, q, kv_all, seqs, block)

    resid_in = own.astype(F32)
    mid, down = transfer(5, [part("sum", dot(att_low, wo).astype(BF)), part("pass", down[:, width // 4 :])], (wg,))
    wd_two = gather_planes(down)
    resid_mid = resid_in + mid.astype(F32)
    scale_two = rms_scale(resid_mid)
    normed_two = resid_mid * scale_two
    hidden_two, gate_pre, up_pre, inner, wd_left, wd_right = transfer(
        6, [part("forward", normed_two.astype(BF), wg, wu, grad_low)]
    )
    hidden_two = hidden_two.reshape(8 * rows, width)
    wd_two = after(wd_two, (wd_left,))
    grad_gate, grad_up, grad_wu = inner_back(grad_low, gate_pre, up_pre, wd_one, wd_two, hidden_two)
    e_two, grad_wg = transfer(7, [part("mlp", hidden_two, grad_gate, grad_up, wg, wu)], (grad_wu,))
    by_owner = lambda g: sum_planes(g.reshape(8 * nz, r, -1))
    wd_left, grad_wu, grad_wg = sum_planes(wd_left), by_owner(grad_wu), by_owner(grad_wg)
    grad_mid = grad_out + norm_back(e_two.astype(F32), normed_two, scale_two)
    grad_heads, grad_wo, out_part = transfer(
        8, [part("heads", grad_mid.astype(BF), wo, att_low), part("product", inner, wd_one, wd_two)], (wd_left,)
    )
    dq, dkv = attend_back(lens, q, kv_all, grad_heads, att, log, seqs, block, (grad_wu,))
    dkv, out_sum, grad_wu = transfer(
        9, [part("down", dkv), part("sum", out_part), part("back", grad_wu, pieces=pieces)]
    )
    wd_right = after(wd_right, (dkv,))
    layer_out = (resid_mid + out_sum.astype(F32)).astype(BF)
    e_one, grad_qkv = project_back(dq, dkv, hidden_one, pack, cos, sin, (wd_right,))
    wd_right = sum_planes(wd_right)
    e_one, grad_wg = transfer(10, [part("sum", e_one), part("back", grad_wg, pieces=pieces)])
    grad_wo = sum_planes(grad_wo)
    grad_qkv = sum_planes(rows_first(grad_qkv))
    scale_one = rms_scale(resid_in)
    grad_tokens = grad_mid + norm_back(e_one.astype(F32) * gain_row, resid_in * scale_one, scale_one)
    grad_qkv, grad_wo = transfer(11, [part("slab", grad_qkv), part("home", grad_wo)], (e_one,))
    grad_wd = jnp.concatenate([wd_left, wd_right], 1)
    if pieces == 1:
        grad_wd = lax.ppermute(grad_wd, ("cm", "cl"), home)
    grad_qkv = grad_qkv.transpose(1, 0, 2).astype(F32)
    grad_wq = grad_qkv[..., :wide].reshape(r, 8 * wide)
    grad_wk = grad_qkv[..., wide : wide + HD].reshape(r, 8 * HD)
    grad_wv = grad_qkv[..., wide + HD :].reshape(r, 8 * HD)
    grad_wg, grad_wu = grad_wg.astype(F32), grad_wu.astype(F32)

    def gain_grad(pairs):
        return sum(jnp.sum(w.astype(F32) * g, -1) for w, g in pairs)

    gain_grad_one = gain_grad(((w_query, grad_wq), (w_key, grad_wk), (w_value, grad_wv))) / attn_gain.astype(F32)
    gain_grad_two = gain_grad(((w_gate, grad_wg), (w_up, grad_wu)))
    return (
        layer_out.reshape(seqs, block, width),
        grad_tokens.reshape(seqs, block, width).astype(BF),
        gain_grad_one,
        grad_wq,
        grad_wk,
        grad_wv,
        grad_wo.astype(F32),
        gain_grad_two,
        grad_wg * gain_two,
        grad_wu * gain_two,
        grad_wd.astype(F32),
    )


def solution(mesh):
    fsdp, ctx = mesh.devices.shape
    fine = Mesh(mesh.devices.reshape(fsdp // 2, 2, ctx // 2, 2), ("a", "core", "cm", "cl"))
    token = P(("a", "core"), ("cm", "cl"), None)
    vector = P(("a", "core", "cm", "cl"))
    matrix = P(("a", "core", "cm", "cl"), None)
    return jax.shard_map(
        on_device,
        mesh=fine,
        in_specs=(
            token,
            P(("a", "core")),
            token,
            vector,
            matrix,
            matrix,
            matrix,
            matrix,
            vector,
            matrix,
            matrix,
            matrix,
        ),
        out_specs=(token, token, vector, matrix, matrix, matrix, matrix, vector, matrix, matrix, matrix),
        check_vma=False,
    )
```

```python
import functools

import jax
import jax.numpy as jnp
from jax import lax
from jax.experimental import pallas as pl
from jax.experimental.pallas import tpu as pltpu
from jax.sharding import Mesh
from jax.sharding import PartitionSpec as P

HEADS = 32
KVH = 8
HD = 64
EPSILON = 1e-05
NEGATIVE = -1e30
BF = jnp.bfloat16
F32 = jnp.float32
GROUP = ("a", "core", "cl")
MESH = pl.DeviceIdType.MESH
ANY = pl.BlockSpec(memory_space=pl.ANY)
TILE = 32
MIB = 2**20


def dma(*shape):
    return pltpu.SemaphoreType.DMA(shape)


def places():
    return tuple(lax.axis_index(n) for n in GROUP)


def index_of(a, core, cl):
    return (a * 2 + core) * 2 + cl


def partners():
    a, core, cl = places()
    out = []
    for t in range(1, 8):
        at = (a ^ (t >> 2), core ^ ((t >> 1) & 1), cl ^ (t & 1))
        out.append((dict(zip(GROUP, at)), index_of(*at)))
    return out


def moved_to(c, nz):
    return lax.rem(c, nz), c // nz


def moved_from(c, nz):
    block = lax.rem(c, 2) * nz + c // 2
    return block // 2, lax.rem(block, 2)


def move_pair(nz, back):
    here = lax.axis_index("cm") * 2 + lax.axis_index("cl")
    pair = [dict(zip(("cm", "cl"), f(here, nz))) for f in (moved_to, moved_from)]
    if back:
        pair.reverse()
    return pair, pair[0]["cm"] * 2 + pair[0]["cl"] == here


def greet(whole, line, move, nz):
    barrier = pltpu.get_barrier_semaphore()

    def signal(device):
        pl.semaphore_signal(barrier, inc=1, device_id=device, device_id_type=MESH)

    if whole:
        base = [device for device, _ in partners()]
    else:
        base = [{n: 1 - lax.axis_index(n)} for n in GROUP]
    for device in base:
        signal(device)
    n = len(base)
    if line:
        z = lax.axis_index("cm")
        pl.when(z > 0)(lambda: signal({"cm": z - 1}))
        pl.when(z < nz - 1)(lambda: signal({"cm": z + 1}))
        edge = jnp.logical_or(z == 0, z == nz - 1)
        pl.when(edge)(lambda: pl.semaphore_wait(barrier, n + 1))
        pl.when(jnp.logical_not(edge))(lambda: pl.semaphore_wait(barrier, n + 2))
    elif move is not None:
        pair, stays = move_pair(nz, move)

        @pl.when(jnp.logical_not(stays))
        def _():
            for device in pair:
                signal(device)
            pl.semaphore_wait(barrier, n + 2)

        @pl.when(stays)
        def _():
            pl.semaphore_wait(barrier, n)

    else:
        pl.semaphore_wait(barrier, n)


def remote(src, dst, send, recv, device):
    if isinstance(device, str):
        device = {device: 1 - lax.axis_index(device)}
    return pltpu.make_async_remote_copy(
        src_ref=src, dst_ref=dst, send_sem=send, recv_sem=recv, device_id=device, device_id_type=MESH
    )


def gather_steps(x_ref, o_ref, local, ss, rs, ready=None):
    ready = ready or (lambda i: None)
    a, core, cl = places()
    half = x_ref.shape[0] // 2
    lo, hi, both = pl.ds(0, half), pl.ds(half, half), pl.ds(0, 2 * half)
    me = index_of(a, core, cl)
    sx = index_of(1 - a, core, cl)
    sy = index_of(a, core, 1 - cl)
    sd = index_of(1 - a, core, 1 - cl)
    other = 2 - 4 * core
    mine = pltpu.make_async_copy(x_ref, o_ref.at[me], local.at[0])

    def put(i, slot, part, name, src=None):
        src = o_ref.at[slot, part] if src is None else src
        return remote(src, o_ref.at[slot, part], ss.at[i], rs.at[i], name)

    sent = [
        put(0, me, lo, "a", x_ref.at[lo]),
        put(1, me, hi, "cl", x_ref.at[hi]),
        put(2, me, hi, "a", x_ref.at[hi]),
        put(3, me, lo, "cl", x_ref.at[lo]),
        put(4, me, both, "core", x_ref),
    ]
    for c in sent:
        c.start()
    mine.start()
    yield
    mine.wait()
    ready(me)

    def on(i, slot, part, name):
        c = put(i, slot, part, name)
        c.start()
        sent.append(c)

    put(0, sx, lo, "a").wait_recv()
    on(5, sx, lo, "cl")
    on(6, sx, lo, "core")
    put(1, sy, hi, "cl").wait_recv()
    on(7, sy, hi, "a")
    on(8, sy, hi, "core")
    put(4, me + other, both, "core").wait_recv()
    ready(me + other)
    yield
    put(2, sx, hi, "a").wait_recv()
    on(9, sx, hi, "core")
    put(3, sy, lo, "cl").wait_recv()
    on(10, sy, lo, "core")
    ready(sx)
    ready(sy)
    yield
    for i, slot, part in ((6, sx, lo), (9, sx, hi)):
        put(i, slot + other, part, "core").wait_recv()
    ready(sx + other)
    put(5, sd, lo, "cl").wait_recv()
    on(11, sd, lo, "core")
    put(7, sd, hi, "a").wait_recv()
    on(12, sd, hi, "core")
    yield
    for i, slot, part in ((8, sy, hi), (10, sy, lo)):
        put(i, slot + other, part, "core").wait_recv()
    ready(sy + other)
    ready(sd)
    for i, slot, part in ((11, sd, lo), (12, sd, hi)):
        put(i, slot + other, part, "core").wait_recv()
    ready(sd + other)
    for c in sent:
        c.wait_send()


def add_rows(dst, sources, n):
    @pl.loop(0, n // TILE)
    def _(i):
        part = pl.ds(pl.multiple_of(i * TILE, TILE), TILE)
        total = sources[0][part, :].astype(F32)
        for s in sources[1:]:
            total = total + s[part, :].astype(F32)
        dst[part, :] = total.astype(dst.dtype)


def plane_chips():
    a, _, cl = places()
    return (a, cl), (1 - a, cl), (a, 1 - cl), (1 - a, 1 - cl)


def sum_steps(x_ref, o_ref, mine, theirs, first, last, lsem, cs, cr, ss, rs):
    core = lax.axis_index("core")
    out, loc = {}, {}
    for p in (3, 1, 2, 0):
        ca, cc = plane_chips()[p]
        out[p] = remote(x_ref.at[index_of(ca, 1 - core, cc)], theirs.at[p], cs.at[p], cr.at[p], "core")
        out[p].start()
        loc[p] = pltpu.make_async_copy(x_ref.at[index_of(ca, core, cc)], mine.at[p], lsem.at[p])
        loc[p].start()
    yield
    yield from sum_rest(o_ref, mine, theirs, first, last, lsem, out, loc, ss, rs)


def sum_rest(o_ref, mine, theirs, first, last, lsem, out, loc, ss, rs, make=None):
    rows = mine.shape[1]
    half = rows // 2
    lo, hi = pl.ds(0, half), pl.ds(half, half)

    def chip_sum(p):
        if make is not None:
            make(p)
        out[p].wait_recv()
        if p in loc:
            loc[p].wait()
        add_rows(mine.at[p], (mine.at[p], theirs.at[p]), rows)

    chip_sum(3)
    xd = remote(mine.at[3, lo], first.at[0], ss.at[0], rs.at[0], "a")
    yd = remote(mine.at[3, hi], first.at[1], ss.at[1], rs.at[1], "cl")
    xd.start()
    yd.start()
    chip_sum(1)
    xo = remote(mine.at[1, lo], first.at[2], ss.at[2], rs.at[2], "a")
    xo.start()
    chip_sum(2)
    yo = remote(mine.at[2, hi], first.at[3], ss.at[3], rs.at[3], "cl")
    yo.start()
    chip_sum(0)
    yield
    xd.wait_recv()
    add_rows(mine.at[2, lo], (mine.at[2, lo], first.at[0]), half)
    y2 = remote(mine.at[2, lo], last.at[0], ss.at[4], rs.at[4], "cl")
    y2.start()
    yd.wait_recv()
    add_rows(mine.at[1, hi], (mine.at[1, hi], first.at[1]), half)
    x2 = remote(mine.at[1, hi], last.at[1], ss.at[5], rs.at[5], "a")
    x2.start()
    yield
    xo.wait_recv()
    add_rows(mine.at[0, lo], (mine.at[0, lo], first.at[2]), half)
    yo.wait_recv()
    add_rows(mine.at[0, hi], (mine.at[0, hi], first.at[3]), half)
    yield
    y2.wait_recv()
    add_rows(mine.at[0, lo], (mine.at[0, lo], last.at[0]), half)
    x2.wait_recv()
    add_rows(mine.at[0, hi], (mine.at[0, hi], last.at[1]), half)
    done = pltpu.make_async_copy(mine.at[0], o_ref, lsem.at[4])
    done.start()
    for c in (*out.values(), xd, yd, xo, yo, y2, x2):
        c.wait_send()
    done.wait()


def swap_steps(kind, pieces, src, dst, lsem, ss, rs):
    me = index_of(*places())
    copies = []
    for p in range(pieces):

        def block(f, p=p):
            return ((f // 2) * pieces + p) * 2 + lax.rem(f, 2) if pieces > 1 else f

        width = (dst if kind == "cols" else src).shape[-1] // pieces

        def cut(ref, i, width=width):
            return ref.at[:, pl.ds(pl.multiple_of(i * width, width), width)]

        def part(ref, i, p=p, width=width):
            return ref.at[i] if pieces == 1 else ref.at[i, :, pl.ds(p * width, width)]

        def source(f, block=block, cut=cut, part=part):
            return cut(src, block(f)) if kind == "cols" else part(src, f)

        target = cut(dst, block(me)) if kind == "back" else part(dst, me)
        for t, (device, index) in enumerate(partners()):
            copies.append(remote(source(index), target, ss.at[p, t], rs.at[p, t], device))
            copies[-1].start()
        copies.append(pltpu.make_async_copy(source(me), target, lsem.at[p]))
        copies[-1].start()
    yield
    yield
    yield
    yield
    for copy in copies:
        copy.wait()


def move_steps(nz, back, src, dst, lsem, ss, rs):
    pair, stays = move_pair(nz, back)
    mine = pltpu.make_async_copy(src, dst, lsem.at[0])
    away = remote(src, dst, ss.at[0], rs.at[0], pair[0])
    pl.when(stays)(mine.start)
    pl.when(jnp.logical_not(stays))(away.start)
    yield
    yield
    yield
    yield
    pl.when(stays)(mine.wait)
    pl.when(jnp.logical_not(stays))(away.wait)


def up_steps(nz, x_ref, o_ref, lsem, ss, rs):
    z = lax.axis_index("cm")
    mine = pltpu.make_async_copy(x_ref, o_ref.at[z], lsem.at[0])
    mine.start()

    def send(j, src):
        return remote(src, o_ref.at[j], ss.at[j], rs.at[j], {"cm": jnp.minimum(z + 1, nz - 1)})

    @pl.when(z < nz - 1)
    def _():
        send(z, x_ref).start()

    yield
    for i in range(1, nz):

        @pl.when(z >= i)
        def _(i=i):
            j = z - i
            send(j, o_ref.at[j]).wait_recv()

            @pl.when(z < nz - 1)
            def _():
                send(j, o_ref.at[j]).start()

        yield
    for i in range(nz):

        @pl.when(jnp.logical_and(z >= i, z < nz - 1))
        def _(i=i):
            send(z - i, x_ref).wait_send()

    mine.wait()


def pass_steps(src, dst, lsem):
    copy = pltpu.make_async_copy(src, dst, lsem.at[0])
    copy.start()
    yield
    yield
    yield
    copy.wait()


def down_steps(nz, x_ref, o_ref, mine, came, lsem, ss, rs):
    z = lax.axis_index("cm")
    rows = x_ref.shape[1]

    def load(j):
        return pltpu.make_async_copy(x_ref.at[j], mine.at[j], lsem.at[j])

    def send(j):
        return remote(mine.at[j], came.at[j], ss.at[j], rs.at[j], {"cm": jnp.maximum(z - 1, 0)})

    for j in range(nz):
        pl.when(z >= j)(lambda j=j: load(j).start())

    ends = [0, 1, 2, nz]
    for first, end in zip(ends, ends[1:]):

        @pl.when(z == nz - 1)
        def _(first=first, end=end):
            for j in range(first, end):
                load(j).wait()
                if j < nz - 1:
                    send(j).start()

        yield
    for j in range(nz - 1):

        @pl.when(jnp.logical_and(z >= j, z < nz - 1))
        def _(j=j):
            load(j).wait()
            send(j).wait_recv()
            add_rows(mine.at[j], (mine.at[j], came.at[j]), rows)
            pl.when(z > j)(send(j).start)

    yield
    done = pltpu.make_async_copy(mine.at[z], o_ref, lsem.at[nz])
    done.start()
    for j in range(nz):
        pl.when(z > j)(lambda j=j: send(j).wait_send())
    done.wait()


def reduce_steps(nz, x_ref, o_ref, mine, above, below, lsem, us, ur, ds, dr):
    z = lax.axis_index("cm")
    rows = x_ref.shape[1]

    def load(j):
        return pltpu.make_async_copy(x_ref.at[j], mine.at[j], lsem.at[j])

    def down(j):
        return remote(mine.at[j], above.at[j], ds.at[j], dr.at[j], {"cm": jnp.maximum(z - 1, 0)})

    def up(j):
        return remote(mine.at[j], below.at[j], us.at[j], ur.at[j], {"cm": jnp.minimum(z + 1, nz - 1)})

    for j in range(nz):
        load(j).start()
    for j in range(nz):
        load(j).wait()

    @pl.when(z == nz - 1)
    def _():
        for j in range(nz - 1):
            down(j).start()

    @pl.when(z == 0)
    def _():
        for j in range(nz - 1, 0, -1):
            up(j).start()

    yield
    yield

    def pass_down():
        for j in range(nz - 1):

            @pl.when(jnp.logical_and(z > j, z < nz - 1))
            def _(j=j):
                down(j).wait_recv()
                add_rows(mine.at[j], (mine.at[j], above.at[j]), rows)
                down(j).start()

    def pass_up():
        for j in range(nz - 1, 0, -1):

            @pl.when(jnp.logical_and(z < j, z > 0))
            def _(j=j):
                up(j).wait_recv()
                add_rows(mine.at[j], (mine.at[j], below.at[j]), rows)
                up(j).start()

    low = 2 * z < nz - 1
    pl.when(low)(pass_up)
    pl.when(jnp.logical_not(low))(pass_down)
    yield
    pl.when(low)(pass_down)
    pl.when(jnp.logical_not(low))(pass_up)
    yield
    for j in range(nz):

        @pl.when(z == j)
        def _(j=j):
            if j < nz - 1:
                down(j).wait_recv()
                add_rows(mine.at[j], (mine.at[j], above.at[j]), rows)
            if j > 0:
                up(j).wait_recv()
                add_rows(mine.at[j], (mine.at[j], below.at[j]), rows)
            done = pltpu.make_async_copy(mine.at[j], o_ref, lsem.at[nz])
            done.start()
            done.wait()

    for j in range(nz):
        pl.when(z > j)(lambda j=j: down(j).wait_send())
        pl.when(z < j)(lambda j=j: up(j).wait_send())


def row_loads(nz, src, dst, sems):
    run = dst.shape[0] // (4 * nz)
    copies = []
    for c in range(4 * nz):
        at = c % nz * (src.shape[0] // nz) + c // nz * run
        copies.append(pltpu.make_async_copy(src.at[pl.ds(at, run)], dst.at[pl.ds(c * run, run)], sems.at[c]))
    return copies


def back_steps(nz, r, hid_ref, one_ref, two_ref, wone_ref, wtwo_ref, o_ref, out_ref, *scratch):
    hid, g, w, out, stage, theirs, first, last, gsem, wsem, osem, lsem, cs, cr, ss, rs = scratch
    tiles, _, wide = hid.shape
    run = 2 * r
    per = wide // run
    core = lax.axis_index("core")
    rows, width = theirs.shape[1:]
    loads = [pltpu.make_async_copy(one_ref, g.at[0], gsem.at[0]), pltpu.make_async_copy(two_ref, g.at[1], gsem.at[1])]
    loads += row_loads(nz, wone_ref, w.at[0], wsem.at[0]) + row_loads(nz, wtwo_ref, w.at[1], wsem.at[1])
    later = [
        pltpu.make_async_copy(hid_ref.at[:, pl.ds(i * wide, wide)], hid.at[i], gsem.at[2 + i]) for i in range(tiles)
    ]
    for c in loads + later:
        c.start()
    for c in loads:
        c.wait()

    def blocks(p):
        ca, cc = plane_chips()[p]

        @pl.loop(0, 2)
        def _(n):
            to = jnp.where(n == 0, 1 - core, core)
            first_row = pl.multiple_of(index_of(ca, to, cc) * rows, rows)
            for c in range(0, width, width // 2):
                part = pl.ds(c, width // 2)
                e = dot(g[0, pl.ds(first_row, rows), :], w[0, part, :], 1, 1)
                e += dot(g[1, pl.ds(first_row, rows), :], w[1, part, :], 1, 1)
                stage[n, p, :, part] = e.astype(BF)

            @pl.when(n == 0)
            def _():
                out_core[p].start()

    out_core = {p: remote(stage.at[0, p], theirs.at[p], cs.at[p], cr.at[p], "core") for p in range(4)}

    def store(i, p):
        chunk = i * per + p
        at = (lax.rem(chunk, nz) * 4 + chunk // nz) * run
        return pltpu.make_async_copy(
            out.at[i, pl.ds(p * run, run)], out_ref.at[pl.ds(pl.multiple_of(at, run), run)], osem.at[i, p]
        )

    def products(lo, hi):
        @pl.loop(lo, hi)
        def _(i):
            out[i] = dot(hid[i], g[0], 0, 0).astype(BF)
            for p in range(per):
                store(i, p).start()

    summing = sum_rest(o_ref, stage.at[1], theirs, first, last, lsem, out_core, {}, ss, rs, blocks)
    for n in range(4):
        next(summing, None)
        if n == 0:
            for c in later:
                c.wait()
        products(n * tiles // 4, (n + 1) * tiles // 4)
    for _ in summing:
        pass

    @pl.loop(0, tiles)
    def _(i):
        for p in range(per):
            store(i, p).wait()

    yield


def forward_steps(nz, x_ref, wone_ref, wtwo_ref, low_ref, all_ref, gate_ref, up_ref, in_ref, *rest):
    g_refs, scratch = rest[:2], rest[2:]
    buf, w, low, inner, stage, out, wsem, asem, gsem, osem, local, ss, rs = scratch
    rows = buf.shape[1]
    loads = row_loads(nz, wone_ref, w.at[0], wsem.at[0]) + row_loads(nz, wtwo_ref, w.at[1], wsem.at[1])
    load_low = pltpu.make_async_copy(low_ref, low, osem.at[0])
    done = []

    def keep(src, dst, sem):
        done.append(pltpu.make_async_copy(src, dst, sem))
        done[-1].start()

    def ready(i):
        n = len(done) // 4
        if n == 0:
            for c in loads:
                c.wait()
        block = buf[i]
        part = pl.ds(pl.multiple_of(i * rows, rows), rows)
        gate = dot(block, w[0])
        up = dot(block, w[1])
        stage[n, 0] = gate
        stage[n, 1] = up
        inner[part, :] = (gate * jax.nn.sigmoid(gate) * up).astype(BF)
        keep(buf.at[i], all_ref.at[i], asem.at[n])
        keep(stage.at[n, 0], gate_ref.at[part], gsem.at[n, 0])
        keep(stage.at[n, 1], up_ref.at[part], gsem.at[n, 1])
        keep(inner.at[part], in_ref.at[part], gsem.at[n, 2])

    first = gather_steps(x_ref, buf, local, ss, rs, ready)
    next(first)
    for c in (*loads, load_low):
        c.start()
    for _ in first:
        pass
    load_low.wait()
    tiles, wide, width = out.shape
    half = width // 2

    def store(t, n):
        return pltpu.make_async_copy(
            out.at[t, :, pl.ds(n * half, half)], g_refs[n].at[pl.ds(t * wide, wide)], osem.at[1 + t * 2 + n]
        )

    for t in range(tiles):
        left = inner[:, t * wide : (t + 1) * wide]
        for n in range(2):
            out[t, :, n * half : (n + 1) * half] = dot(left, low[:, n * half : (n + 1) * half], 0, 0).astype(BF)
            store(t, n).start()
    for t in range(tiles):
        for n in range(2):
            store(t, n).wait()
    for c in done:
        c.wait()
    yield


def product_steps(a_ref, left_ref, right_ref, o_ref, a, b, out, lsem, osem):
    half = b.shape[1] // 2
    tiles, rows, _ = out.shape
    loads = [
        pltpu.make_async_copy(a_ref, a, lsem.at[0]),
        pltpu.make_async_copy(left_ref, b.at[:, pl.ds(0, left_ref.shape[1])], lsem.at[1]),
        pltpu.make_async_copy(right_ref, b.at[:, pl.ds(left_ref.shape[1], right_ref.shape[1])], lsem.at[2]),
    ]
    for c in loads:
        c.start()
    for c in loads:
        c.wait()

    def store(i):
        return pltpu.make_async_copy(out.at[i], o_ref.at[pl.ds(pl.multiple_of(i * rows, rows), rows)], osem.at[i])

    for lo, hi in ((0, tiles // 2), (tiles // 2, tiles)):

        @pl.loop(lo, hi)
        def _(i):
            left = a[pl.ds(pl.multiple_of(i * rows, rows), rows), :]
            for c in (0, half):
                out[i, :, c : c + half] = dot(left, b[:, c : c + half]).astype(BF)
            store(i).start()

        yield

    @pl.loop(0, tiles)
    def _(i):
        store(i).wait()


def heads_steps(x_ref, wo_ref, low_ref, heads_ref, g_ref, buf, wo, low, heads, total, g, lsem, local, ss, rs):
    loads = [pltpu.make_async_copy(wo_ref, wo, lsem.at[0]), pltpu.make_async_copy(low_ref, low, lsem.at[1])]
    for c in loads:
        c.start()
    rows = buf.shape[1]
    seen_blocks = []

    def ready(i):
        if not seen_blocks:
            for c in loads:
                c.wait()
            total[...] = jnp.zeros_like(total)
        seen_blocks.append(i)
        block = buf[i]
        part = pl.ds(pl.multiple_of(i * rows, rows), rows)
        heads[part, :] = dot(block, wo[...], 1, 1).astype(BF)
        total[...] += dot(low[part, :], block, 0, 0)

    yield from gather_steps(x_ref, buf, local, ss, rs, ready)
    g[...] = total[...].astype(BF)
    stores = [pltpu.make_async_copy(heads, heads_ref, lsem.at[2]), pltpu.make_async_copy(g, g_ref, lsem.at[3])]
    for c in stores:
        c.start()
    for c in stores:
        c.wait()


def part(kind, *xs, **how):
    nz = lax.axis_size("cm")
    x = xs[0]
    like = lambda *shape: jax.ShapeDtypeStruct(shape, x.dtype)
    vmem = lambda *shape: pltpu.VMEM(shape, x.dtype)
    if kind == "gather":
        rows, cols = x.shape
        return kind, gather_steps, xs, [like(8, rows, cols)], [dma(1), dma(13), dma(13)]
    if kind == "sum":
        rows, cols = x.shape[0] // 8, x.shape[1]
        scratch = [vmem(n, m, cols) for n, m in ((4, rows), (4, rows), (4, rows // 2), (2, rows // 2))]
        scratch += [dma(5), dma(4), dma(4), dma(6), dma(6)]
        return kind, sum_steps, [x.reshape(8, rows, cols)], [like(rows, cols)], scratch
    if kind == "up":
        return kind, functools.partial(up_steps, nz), xs, [like(nz, *x.shape)], [dma(1), dma(nz), dma(nz)]
    if kind == "pass":
        return kind, pass_steps, xs, [like(*x.shape)], [dma(1)]
    if kind == "down":
        scratch = [vmem(*x.shape)] * 2 + [dma(nz + 1), dma(nz), dma(nz)]
        return kind, functools.partial(down_steps, nz), xs, [like(*x.shape[1:])], scratch
    if kind == "reduce":
        scratch = [vmem(*x.shape)] * 3 + [dma(nz + 1)] + [dma(nz)] * 4
        return kind, functools.partial(reduce_steps, nz), xs, [like(*x.shape[1:])], scratch
    if kind in ("move", "home"):
        return kind, functools.partial(move_steps, nz, kind == "home"), xs, [like(*x.shape)], [dma(1), dma(1), dma(1)]
    if kind == "mlp":
        rows, width = x.shape
        cols = xs[1].shape[1]
        r = width // (8 * nz)
        wide = 256
        tiles = width // wide
        block = rows // 8
        scratch = [vmem(tiles, rows, wide), vmem(2, rows, cols), vmem(2, width, cols), vmem(tiles, wide, cols)]
        scratch += [vmem(2, 4, block, width), vmem(4, block, width), vmem(4, block // 2, width)]
        scratch += [vmem(2, block // 2, width), dma(2 + tiles), dma(2, 4 * nz), dma(tiles, wide // (2 * r))]
        scratch += [dma(5), dma(4), dma(4), dma(6), dma(6)]
        return kind, functools.partial(back_steps, nz, r), xs, [like(block, width), like(width, cols)], scratch
    if kind == "forward":
        rows, width = x.shape
        cols = xs[1].shape[1]
        wide = min(256, cols)
        tiles = cols // wide
        full = [jax.ShapeDtypeStruct((8 * rows, cols), F32)] * 2
        outs = [like(8, rows, width), *full, like(8 * rows, cols), *[like(cols, width // 2)] * 2]
        scratch = [vmem(8, rows, width), vmem(2, width, cols), vmem(8 * rows, width), vmem(8 * rows, cols)]
        scratch += [pltpu.VMEM((8, 2, rows, cols), F32), vmem(tiles, wide, width)]
        scratch += [dma(2, 4 * nz), dma(8), dma(8, 3), dma(1 + 2 * tiles), dma(1), dma(13), dma(13)]
        return kind, functools.partial(forward_steps, nz), xs, outs, scratch
    if kind == "product":
        rows, cols = x.shape[0], xs[1].shape[1] + xs[2].shape[1]
        scratch = [vmem(*x.shape), vmem(x.shape[1], cols), vmem(8, rows // 8, cols), dma(3), dma(8)]
        return kind, product_steps, xs, [like(rows, cols)], scratch
    if kind == "heads":
        rows, cols = x.shape
        wide = xs[1].shape[0]
        scratch = [vmem(8, rows, cols), vmem(wide, cols), vmem(8 * rows, wide), vmem(8 * rows, wide)]
        scratch += [pltpu.VMEM((wide, cols), F32), vmem(wide, cols), dma(4), dma(1), dma(13), dma(13)]
        return kind, heads_steps, xs, [like(8 * rows, wide), like(wide, cols)], scratch
    pieces = how.get("pieces", 1)
    shape = x.shape
    if kind == "cols":
        shape = (8, x.shape[0], x.shape[1] // 8)
    elif kind == "back":
        shape = (x.shape[1], 8 * x.shape[2])
    scratch = [dma(pieces), dma(pieces, 7), dma(pieces, 7)]
    return kind, functools.partial(swap_steps, kind, pieces), xs, [like(*shape)], scratch


def transfer(cid, parts, deps=()):
    nz = lax.axis_size("cm")
    kinds = [p[0] for p in parts]
    operands = [x for p in parts for x in p[2]]
    results = [o for p in parts for o in p[3]]
    moves = [k == "home" for k in kinds if k in ("move", "home")]
    whole = any(k in ("slab", "cols", "back") for k in kinds)
    line = any(k in ("up", "down", "reduce") for k in kinds)

    def kernel(*refs):
        ins = list(refs[: len(operands)])
        rest = list(refs[len(operands) + len(deps) :])
        outs, scratch = rest[: len(results)], rest[len(results) :]

        def take(refs, n):
            out = refs[:n]
            del refs[:n]
            return out

        greet(whole, line, moves[0] if moves else None, nz)
        running = []
        for _, steps, xs, shapes, own in parts:
            running.append(steps(*take(ins, len(xs)), *take(outs, len(shapes)), *take(scratch, len(own))))
        while running:
            still = []
            for steps in running:
                try:
                    next(steps)
                except StopIteration:
                    continue
                still.append(steps)
            running = still

    return pl.pallas_call(
        kernel,
        out_shape=results,
        in_specs=[ANY] * (len(operands) + len(deps)),
        out_specs=[ANY] * len(results),
        scratch_shapes=[s for p in parts for s in p[4]],
        compiler_params=pltpu.CompilerParams(
            collective_id=cid, has_side_effects=True, vmem_limit_bytes=60 * MIB
        ),
        name="_".join(kinds) + str(cid),
    )(*operands, *deps)


def after(x, deps):
    return pl.pallas_call(
        lambda *refs: None,
        out_shape=jax.ShapeDtypeStruct(x.shape, x.dtype),
        in_specs=[ANY] * (1 + len(deps)),
        out_specs=ANY,
        input_output_aliases={0: 0},
        name="after",
    )(x, *deps)


def sum_planes(g):
    return lax.psum_scatter(g, "cm", scatter_dimension=0, tiled=True)


def gather_planes(x):
    return lax.all_gather(x, "cm", axis=0, tiled=True)


def dot(a, b, left=1, right=0):
    return lax.dot_general(a, b, (((left,), (right,)), ((), ())), preferred_element_type=F32)


def rope(u, cos, sin):
    width = u.shape[-1]
    lane = lax.broadcasted_iota(jnp.int32, u.shape, 1)
    other = jnp.where(lane % HD < HD // 2, pltpu.roll(u, width - HD // 2, 1), pltpu.roll(u, HD // 2, 1))
    return u * cos + other * sin


def tables(positions):
    lane = jnp.arange(2 * HD)
    frequency = 500000.0 ** (-(lane % (HD // 2)).astype(F32) * 2.0 / HD)
    angles = positions.astype(F32)[..., None] * frequency
    return jnp.cos(angles), jnp.where(lane % HD < HD // 2, -1.0, 1.0) * jnp.sin(angles)


def project_kernel(x_ref, gain_ref, w_ref, cos_ref, sin_ref, hid_ref, q_ref, kv_ref):
    x = x_ref[...].astype(F32)
    hid = (x * lax.rsqrt(jnp.mean(x * x, -1, keepdims=True) + EPSILON) * gain_ref[...]).astype(BF)
    hid_ref[...] = hid
    u = dot(hid, w_ref[...])
    times = x.shape[0] // cos_ref.shape[1]
    cos = jnp.concatenate([cos_ref[0]] * times, 0)
    sin = jnp.concatenate([sin_ref[0]] * times, 0)
    wide = q_ref.shape[-1]
    copies = wide // (2 * HD)
    q_ref[...] = rope(u[:, :wide], jnp.concatenate([cos] * copies, 1), jnp.concatenate([sin] * copies, 1)).astype(BF)
    kv = u[:, wide:]
    lane = lax.broadcasted_iota(jnp.int32, kv.shape, 1)
    kv_ref[...] = jnp.where(lane < HD, rope(kv, cos, sin), kv).astype(BF)


def project(x, gain, w, wide, cos, sin):
    rows, width = x.shape
    step = rows // 8
    block = cos.shape[1]
    table = pl.BlockSpec((1, block, 2 * HD), lambda g: (g % 2, 0, 0))
    return pl.pallas_call(
        project_kernel,
        grid=(8,),
        out_shape=[jax.ShapeDtypeStruct((rows, c), BF) for c in (width, wide, 2 * HD)],
        in_specs=[
            pl.BlockSpec((step, width), lambda g: (g, 0)),
            pl.BlockSpec((1, width), lambda g: (0, 0)),
            pl.BlockSpec((width, wide + 2 * HD), lambda g: (0, 0)),
            table,
            table,
        ],
        out_specs=[pl.BlockSpec((step, c), lambda g: (g, 0)) for c in (width, wide, 2 * HD)],
        compiler_params=pltpu.CompilerParams(vmem_limit_bytes=48 * MIB),
        name="project",
    )(x, gain, w, cos, sin)


def project_back_kernel(dq_ref, dkv_ref, hid_ref, w_ref, cos_ref, sin_ref, *rest):
    e_ref, g_ref, total = rest[-3:]
    step = pl.program_id(0)

    @pl.when(step == 0)
    def _():
        total[...] = jnp.zeros_like(total)

    dq = dq_ref[...]
    times = dq.shape[0] // cos_ref.shape[1]
    cos = jnp.concatenate([cos_ref[0]] * times, 0)
    sin = -jnp.concatenate([sin_ref[0]] * times, 0)
    copies = dq.shape[1] // (2 * HD)
    dq = rope(dq, jnp.concatenate([cos] * copies, 1), jnp.concatenate([sin] * copies, 1))
    dkv = dkv_ref[...].astype(F32)
    lane = lax.broadcasted_iota(jnp.int32, dkv.shape, 1)
    dkv = jnp.where(lane < HD, rope(dkv, cos, sin), dkv)
    rows = jnp.concatenate([dq.astype(BF), dkv.astype(BF)], 1)
    e_ref[...] = dot(rows, w_ref[...], 1, 1).astype(BF)
    total[...] += dot(hid_ref[...], rows, 0, 0)

    @pl.when(step == pl.num_programs(0) - 1)
    def _():
        g_ref[...] = total[...].astype(BF)


def project_back(dq, dkv, hid, w, cos, sin, deps):
    rows, width = hid.shape
    step = rows // 8
    shape = (width, dq.shape[1] + 2 * HD)
    block = cos.shape[1]
    table = pl.BlockSpec((1, block, 2 * HD), lambda g: (g % 2, 0, 0))
    return pl.pallas_call(
        project_back_kernel,
        grid=(8,),
        out_shape=[jax.ShapeDtypeStruct((rows, width), BF), jax.ShapeDtypeStruct(shape, BF)],
        in_specs=[
            pl.BlockSpec((step, dq.shape[1]), lambda g: (g, 0)),
            pl.BlockSpec((step, 2 * HD), lambda g: (g, 0)),
            pl.BlockSpec((step, width), lambda g: (g, 0)),
            pl.BlockSpec(shape, lambda g: (0, 0)),
            table,
            table,
        ]
        + [ANY] * len(deps),
        out_specs=[pl.BlockSpec((step, width), lambda g: (g, 0)), pl.BlockSpec(shape, lambda g: (0, 0))],
        scratch_shapes=[pltpu.VMEM(shape, F32)],
        compiler_params=pltpu.CompilerParams(vmem_limit_bytes=48 * MIB),
        name="project_back",
    )(dq, dkv, hid, w, cos, sin, *deps)


def inner_back_kernel(nz, r, low_ref, gate_ref, up_ref, wl_ref, wr_ref, hid_ref, gg_ref, gu_ref, out_ref, hid, gu, sems):
    step = pl.program_id(0)
    tiles, _, wide = hid.shape
    loads = [
        pltpu.make_async_copy(hid_ref.at[:, pl.ds(i * wide, wide)], hid.at[i], sems.at[i]) for i in range(tiles)
    ]

    @pl.when(step == 0)
    def _():
        for c in loads:
            c.start()

    half = wl_ref.shape[1]
    inner = dot(low_ref[:, :half], wl_ref[...], 1, 1) + dot(low_ref[:, half:], wr_ref[...], 1, 1)
    inner = inner.astype(BF).astype(F32)
    gate = gate_ref[...]
    sig = jax.nn.sigmoid(gate)
    act = gate * sig
    gg_ref[...] = (inner * up_ref[...] * (sig * (1.0 + gate * (1.0 - sig)))).astype(BF)
    up = (inner * act).astype(BF)
    gu_ref[...] = up
    rows = up.shape[0]
    gu[pl.ds(pl.multiple_of(step * rows, rows), rows), :] = up

    @pl.when(step == pl.num_programs(0) - 1)
    def _():
        for c in loads:
            c.wait()
        run = 2 * r
        per = wide // run

        @pl.loop(0, tiles)
        def _(i):
            product = dot(hid[i], gu[...], 0, 0).astype(BF)
            for p in range(per):
                chunk = i * per + p
                at = (lax.rem(chunk, nz) * 4 + chunk // nz) * run
                out_ref[pl.ds(pl.multiple_of(at, run), run), :] = product[p * run : (p + 1) * run]


def inner_back(low, gate, up, wl, wr, hid):
    nz = lax.axis_size("cm")
    rows, width = low.shape
    cols = gate.shape[1]
    step = rows // 8
    wide = 256
    tiles = width // wide
    block = lambda c: pl.BlockSpec((step, c), lambda g: (g, 0))
    return pl.pallas_call(
        functools.partial(inner_back_kernel, nz, width // (8 * nz)),
        grid=(8,),
        out_shape=[
            jax.ShapeDtypeStruct((rows, cols), BF),
            jax.ShapeDtypeStruct((rows, cols), BF),
            jax.ShapeDtypeStruct((width, cols), BF),
        ],
        in_specs=[block(width), block(cols), block(cols)] + [pl.BlockSpec(w.shape, lambda g: (0, 0)) for w in (wl, wr)] + [ANY],
        out_specs=[block(cols), block(cols), pl.BlockSpec((width, cols), lambda g: (0, 0))],
        scratch_shapes=[pltpu.VMEM((tiles, rows, wide), BF), pltpu.VMEM((rows, cols), BF), dma(tiles)],
        compiler_params=pltpu.CompilerParams(vmem_limit_bytes=60 * MIB),
        name="inner_back",
    )(low, gate, up, wl, wr, hid)


def flat(ref):
    x = ref[...]
    return x.reshape(x.shape[-4] * x.shape[-2], x.shape[-1])


def heads_of(x):
    return [x[:, h * HD : (h + 1) * HD] for h in range(x.shape[1] // HD)]


def seen(n, j, z, slots):
    col = lax.broadcasted_iota(jnp.int32, (slots, slots), 0) + j * slots
    row = lax.broadcasted_iota(jnp.int32, (slots, slots), 1) + z * slots
    return jnp.logical_and(col <= row, col < n)


def attend_kernel(lens, q_ref, kv_ref, att_ref, low_ref, log_ref, scores, top, sums, acc):
    z = lax.axis_index("cm")
    n = lens[pl.program_id(0) * pl.num_programs(1) + pl.program_id(1)]
    q = flat(q_ref)
    slots = q.shape[0]
    qs = heads_of((q.astype(F32) * HD ** (-0.5)).astype(BF))
    top[...] = jnp.full_like(top, NEGATIVE)
    sums[...] = jnp.zeros_like(sums)
    acc[...] = jnp.zeros_like(acc)

    def score(j, _):
        k = flat(kv_ref.at[j])[:, :HD]
        mask = seen(n, j, z, slots)
        for h, qh in enumerate(qs):
            s = jnp.where(mask, dot(k, qh, 1, 1), NEGATIVE)
            scores[j, h] = s
            top[h : h + 1] = jnp.maximum(top[h : h + 1], jnp.max(s, 0, keepdims=True))
        return 0

    blocks = jnp.minimum(z + 1, (n + slots - 1) // slots)
    lax.fori_loop(0, blocks, score, 0)

    def weigh(j, _):
        v = flat(kv_ref.at[j])[:, HD:]
        for h in range(len(qs)):
            p = jnp.exp(scores[j, h] - top[h : h + 1])
            sums[h : h + 1] += jnp.sum(p, 0, keepdims=True)
            acc[h * HD : (h + 1) * HD] += dot(v, p.astype(BF), 0, 0)
        return 0

    lax.fori_loop(0, blocks, weigh, 0)
    out = jnp.concatenate([acc[h * HD : (h + 1) * HD] / sums[h : h + 1] for h in range(len(qs))], 0)
    att_ref[0, 0] = out
    low_ref[...] = out.T.astype(BF).reshape(low_ref.shape)
    log_ref[0, 0] = top[...] + jnp.log(sums[...])


def attend_back_kernel(lens, q_ref, kv_ref, do_ref, att_ref, log_ref, *rest):
    dq_ref, dkv_ref, acc = rest[-3:]
    z = lax.axis_index("cm")
    n = lens[pl.program_id(0) * pl.num_programs(1) + pl.program_id(1)]
    q = flat(q_ref)
    slots = q.shape[0]
    qs = heads_of((q.astype(F32) * HD ** (-0.5)).astype(BF))
    do = flat(do_ref)
    dos = heads_of(do)
    both = do.astype(F32).T * att_ref[0, 0]
    deltas = [jnp.sum(both[h * HD : (h + 1) * HD], 0, keepdims=True) for h in range(len(qs))]
    acc[...] = jnp.zeros_like(acc)

    def step(j, _):
        kv = flat(kv_ref.at[j])
        k, v = kv[:, :HD], kv[:, HD:]
        mask = seen(n, j, z, slots)
        dk = jnp.zeros((slots, HD), F32)
        dv = jnp.zeros((slots, HD), F32)
        for h, qh in enumerate(qs):
            s = jnp.where(mask, dot(k, qh, 1, 1), NEGATIVE)
            p = jnp.exp(s - log_ref[0, 0, h : h + 1])
            ds = (p * (dot(v, dos[h], 1, 1) - deltas[h])).astype(BF)
            acc[h * HD : (h + 1) * HD] += dot(k, ds, 0, 0)
            dk += dot(ds, qh)
            dv += dot(p.astype(BF), dos[h])
        out = jnp.concatenate([dk, dv], 1).astype(BF)
        dkv_ref[j] = out.reshape(dkv_ref.shape[1:])
        return 0

    live = jnp.where(z * slots < n, z + 1, 0)
    lax.fori_loop(0, live, step, 0)

    def nothing(j, _):
        dkv_ref[j] = jnp.zeros(dkv_ref.shape[1:], BF)
        return 0

    lax.fori_loop(live, z + 1, nothing, 0)
    dq_ref[...] = (acc[...] * HD ** (-0.5)).T.reshape(dq_ref.shape)


def attention_specs(seqs, block, wide, nz):
    own = lambda c: pl.BlockSpec((1, 2, 1, block, c), lambda f, s: (f, 0, s, 0, 0))
    every = pl.BlockSpec((nz, 1, 2, 1, block, 2 * HD), lambda f, s: (0, f, 0, s, 0, 0))
    turned = lambda c: pl.BlockSpec((1, 1, c, 2 * block), lambda f, s: (f, s, 0, 0))
    return own(wide), every, turned(wide), turned(wide // HD)


def attend(lens, q, kv, seqs, block):
    nz, rows, _ = kv.shape
    wide = q.shape[1]
    heads = wide // HD
    own, every, turned, logs = attention_specs(seqs, block, wide, nz)
    view = (4, 2, seqs, block)
    att, low, log = pl.pallas_call(
        attend_kernel,
        grid=(4, seqs),
        out_shape=[
            jax.ShapeDtypeStruct((4, seqs, wide, 2 * block), F32),
            jax.ShapeDtypeStruct((*view, wide), BF),
            jax.ShapeDtypeStruct((4, seqs, heads, 2 * block), F32),
        ],
        in_specs=[pl.BlockSpec(memory_space=pltpu.SMEM), own, every],
        out_specs=[turned, own, logs],
        scratch_shapes=[
            pltpu.VMEM((nz, heads, 2 * block, 2 * block), F32),
            pltpu.VMEM((heads, 2 * block), F32),
            pltpu.VMEM((heads, 2 * block), F32),
            pltpu.VMEM((wide, 2 * block), F32),
        ],
        compiler_params=pltpu.CompilerParams(vmem_limit_bytes=48 * MIB),
        name="attend",
    )(lens, q.reshape(*view, wide), kv.reshape(nz, *view, 2 * HD))
    return att, low.reshape(rows, wide), log


def attend_back(lens, q, kv, do, att, log, seqs, block, deps):
    nz, rows, _ = kv.shape
    wide = q.shape[1]
    own, every, turned, logs = attention_specs(seqs, block, wide, nz)
    view = (4, 2, seqs, block)
    dq, dkv = pl.pallas_call(
        attend_back_kernel,
        grid=(4, seqs),
        out_shape=[
            jax.ShapeDtypeStruct((*view, wide), F32),
            jax.ShapeDtypeStruct((nz, *view, 2 * HD), BF),
        ],
        in_specs=[pl.BlockSpec(memory_space=pltpu.SMEM), own, every, own, turned, logs] + [ANY] * len(deps),
        out_specs=[own, every],
        scratch_shapes=[pltpu.VMEM((wide, 2 * block), F32)],
        compiler_params=pltpu.CompilerParams(vmem_limit_bytes=48 * MIB),
        name="attend_back",
    )(lens, q.reshape(*view, wide), kv.reshape(nz, *view, 2 * HD), do.reshape(*view, wide), att, log, *deps)
    return dq.reshape(rows, wide), dkv.reshape(nz, rows, 2 * HD)


def rms_scale(field):
    return lax.rsqrt(jnp.mean(field * field, -1, keepdims=True) + EPSILON)


def norm_back(grad_normed, normed, scale_rows):
    return scale_rows * (grad_normed - normed * jnp.mean(grad_normed * normed, -1, keepdims=True))


def rows_first(g):
    nz = lax.axis_size("cm")
    rows, c = g.shape
    r = rows // (8 * nz)
    return g.astype(BF).reshape(4, nz, 2, r, c).transpose(1, 0, 2, 3, 4).reshape(nz * 8, r, c)


def on_device(
    tokens, lengths, cotangent, attn_gain, w_query, w_key, w_value, w_out, mlp_gain, w_gate, w_up, w_down
):
    seqs, block, width = tokens.shape
    nz = lax.axis_size("cm")
    rows = seqs * block
    r = w_query.shape[0]
    wide = HEADS // 8 * HD
    cm = lax.axis_index("cm")
    cl = lax.axis_index("cl")
    gain_two = mlp_gain.astype(F32)[:, None]
    pieces = nz if w_down.shape[0] % 128 == 0 else 1
    perm = [(c, (c % nz) * 2 + c // nz) for c in range(2 * nz)]
    home = [(t, s) for s, t in perm]

    def gained(w):
        return (w.astype(F32) * gain_two).astype(BF)

    down = w_down if pieces > 1 else lax.ppermute(w_down, ("cm", "cl"), perm)
    wd_one = gather_planes(down[:, : width // 4])
    pack = [w.reshape(r, 8, -1) for w in (w_query, w_key, w_value)]
    pack.append(jnp.broadcast_to(attn_gain[:, None, None], (r, 8, 2 * HD)))
    pack = jnp.concatenate(pack, -1).transpose(1, 0, 2)
    lens = jnp.broadcast_to(jnp.pad(lengths, (0, 128 - seqs))[None, None], (8, 8, 128))
    pack, lens = transfer(1, [part("slab", pack), part("slab", lens)])
    lens = lens[::2, 0, :seqs].reshape(-1)
    wg, wo = transfer(2, [part("cols", gained(w_gate), pieces=pieces), part("move", w_out)], (pack,))
    ff = wg.shape[2]
    wg = jnp.concatenate([wg.reshape(8 * r, ff), wo.reshape(-1, ff)], 0)
    own = tokens.reshape(rows, width)
    tok_all, wu = transfer(
        3, [part("gather", own), part("cols", gained(w_up), pieces=pieces)], (wg, wd_one)
    )
    pack = gather_planes(pack).reshape(nz, 4, 2 * r, -1).transpose(1, 0, 2, 3).reshape(width, -1)
    gain_row = pack[:, wide + 2 * HD].astype(F32)[None]
    wg = gather_planes(wg)
    wo = wg.reshape(nz, -1, ff)[:, 8 * r :].reshape(-1, width)

    slot = cm * 2 * block + jnp.arange(2 * block, dtype=jnp.int32).reshape(2, block)
    cos, sin = tables(slot)
    hidden_one, q, kv = project(tok_all.reshape(8 * rows, width), gain_row, pack, wide, cos, sin)
    own_pos = cm * 2 * block + cl * block + jnp.arange(block, dtype=jnp.int32)
    valid = (own_pos[None, :] < lengths[:, None]).astype(F32)
    grad_out = (cotangent.astype(F32) * valid[..., None]).reshape(rows, width)
    grad_low, kv_all = transfer(
        4,
        [
            part("gather", grad_out.astype(BF)),
            part("up", kv),
        ],
    )
    grad_low = grad_low.reshape(8 * rows, width)
    wu = gather_planes(wu).reshape(width, -1)
    att, att_low, log = attend(lens, q, kv_all, seqs, block)

    resid_in = own.astype(F32)
    mid, down = transfer(5, [part("sum", dot(att_low, wo).astype(BF)), part("pass", down[:, width // 4 :])], (wg,))
    wd_two = gather_planes(down)
    resid_mid = resid_in + mid.astype(F32)
    scale_two = rms_scale(resid_mid)
    normed_two = resid_mid * scale_two
    hidden_two, gate_pre, up_pre, inner, wd_left, wd_right = transfer(
        6, [part("forward", normed_two.astype(BF), wg, wu, grad_low)]
    )
    hidden_two = hidden_two.reshape(8 * rows, width)
    wd_two = after(wd_two, (wd_left,))
    grad_gate, grad_up, grad_wu = inner_back(grad_low, gate_pre, up_pre, wd_one, wd_two, hidden_two)
    e_two, grad_wg = transfer(7, [part("mlp", hidden_two, grad_gate, grad_up, wg, wu)], (grad_wu,))
    by_owner = lambda g: sum_planes(g.reshape(8 * nz, r, -1))
    wd_left, grad_wu, grad_wg = sum_planes(wd_left), by_owner(grad_wu), by_owner(grad_wg)
    grad_mid = grad_out + norm_back(e_two.astype(F32), normed_two, scale_two)
    grad_heads, grad_wo, out_part = transfer(
        8, [part("heads", grad_mid.astype(BF), wo, att_low), part("product", inner, wd_one, wd_two)], (wd_left,)
    )
    dq, dkv = attend_back(lens, q, kv_all, grad_heads, att, log, seqs, block, (grad_wu,))
    dkv, out_sum, grad_wu = transfer(
        9, [part("down", dkv), part("sum", out_part), part("back", grad_wu, pieces=pieces)]
    )
    wd_right = after(wd_right, (dkv,))
    layer_out = (resid_mid + out_sum.astype(F32)).astype(BF)
    e_one, grad_qkv = project_back(dq, dkv, hidden_one, pack, cos, sin, (wd_right,))
    wd_right = sum_planes(wd_right)
    grad_qkv, e_one, grad_wg = transfer(
        10,
        [
            part("reduce", rows_first(grad_qkv).reshape(nz, 8 * r, -1)),
            part("sum", e_one),
            part("back", grad_wg, pieces=pieces),
        ],
    )
    grad_wo = sum_planes(grad_wo)
    grad_qkv = grad_qkv.reshape(8, r, -1)
    scale_one = rms_scale(resid_in)
    grad_tokens = grad_mid + norm_back(e_one.astype(F32) * gain_row, resid_in * scale_one, scale_one)
    grad_qkv, grad_wo = transfer(11, [part("slab", grad_qkv), part("home", grad_wo)], (e_one,))
    grad_wd = jnp.concatenate([wd_left, wd_right], 1)
    if pieces == 1:
        grad_wd = lax.ppermute(grad_wd, ("cm", "cl"), home)
    grad_qkv = grad_qkv.transpose(1, 0, 2).astype(F32)
    grad_wq = grad_qkv[..., :wide].reshape(r, 8 * wide)
    grad_wk = grad_qkv[..., wide : wide + HD].reshape(r, 8 * HD)
    grad_wv = grad_qkv[..., wide + HD :].reshape(r, 8 * HD)
    grad_wg, grad_wu = grad_wg.astype(F32), grad_wu.astype(F32)

    def gain_grad(pairs):
        return sum(jnp.sum(w.astype(F32) * g, -1) for w, g in pairs)

    gain_grad_one = gain_grad(((w_query, grad_wq), (w_key, grad_wk), (w_value, grad_wv))) / attn_gain.astype(F32)
    gain_grad_two = gain_grad(((w_gate, grad_wg), (w_up, grad_wu)))
    return (
        layer_out.reshape(seqs, block, width),
        grad_tokens.reshape(seqs, block, width).astype(BF),
        gain_grad_one,
        grad_wq,
        grad_wk,
        grad_wv,
        grad_wo.astype(F32),
        gain_grad_two,
        grad_wg * gain_two,
        grad_wu * gain_two,
        grad_wd.astype(F32),
    )


def solution(mesh):
    fsdp, ctx = mesh.devices.shape
    fine = Mesh(mesh.devices.reshape(fsdp // 2, 2, ctx // 2, 2), ("a", "core", "cm", "cl"))
    token = P(("a", "core"), ("cm", "cl"), None)
    vector = P(("a", "core", "cm", "cl"))
    matrix = P(("a", "core", "cm", "cl"), None)
    return jax.shard_map(
        on_device,
        mesh=fine,
        in_specs=(
            token,
            P(("a", "core")),
            token,
            vector,
            matrix,
            matrix,
            matrix,
            matrix,
            vector,
            matrix,
            matrix,
            matrix,
        ),
        out_specs=(token, token, vector, matrix, matrix, matrix, matrix, vector, matrix, matrix, matrix),
        check_vma=False,
    )
```

```python
import functools

import jax
import jax.numpy as jnp
from jax import lax
from jax.experimental import pallas as pl
from jax.experimental.pallas import tpu as pltpu
from jax.sharding import Mesh
from jax.sharding import PartitionSpec as P

HEADS = 32
KVH = 8
HD = 64
EPSILON = 1e-05
NEGATIVE = -1e30
BF = jnp.bfloat16
F32 = jnp.float32
GROUP = ("a", "core", "cl")
MESH = pl.DeviceIdType.MESH
ANY = pl.BlockSpec(memory_space=pl.ANY)
TILE = 32
MIB = 2**20


def dma(*shape):
    return pltpu.SemaphoreType.DMA(shape)


def places():
    return tuple(lax.axis_index(n) for n in GROUP)


def index_of(a, core, cl):
    return (a * 2 + core) * 2 + cl


def partners():
    a, core, cl = places()
    out = []
    for t in range(1, 8):
        at = (a ^ (t >> 2), core ^ ((t >> 1) & 1), cl ^ (t & 1))
        out.append((dict(zip(GROUP, at)), index_of(*at)))
    return out


def moved_to(c, nz):
    return lax.rem(c, nz), c // nz


def moved_from(c, nz):
    block = lax.rem(c, 2) * nz + c // 2
    return block // 2, lax.rem(block, 2)


def move_pair(nz, back):
    here = lax.axis_index("cm") * 2 + lax.axis_index("cl")
    pair = [dict(zip(("cm", "cl"), f(here, nz))) for f in (moved_to, moved_from)]
    if back:
        pair.reverse()
    return pair, pair[0]["cm"] * 2 + pair[0]["cl"] == here


def greet(whole, line, move, nz):
    barrier = pltpu.get_barrier_semaphore()

    def signal(device):
        pl.semaphore_signal(barrier, inc=1, device_id=device, device_id_type=MESH)

    if whole:
        base = [device for device, _ in partners()]
    else:
        base = [{n: 1 - lax.axis_index(n)} for n in GROUP]
    for device in base:
        signal(device)
    n = len(base)
    if line:
        z = lax.axis_index("cm")
        pl.when(z > 0)(lambda: signal({"cm": z - 1}))
        pl.when(z < nz - 1)(lambda: signal({"cm": z + 1}))
        edge = jnp.logical_or(z == 0, z == nz - 1)
        pl.when(edge)(lambda: pl.semaphore_wait(barrier, n + 1))
        pl.when(jnp.logical_not(edge))(lambda: pl.semaphore_wait(barrier, n + 2))
    elif move is not None:
        pair, stays = move_pair(nz, move)

        @pl.when(jnp.logical_not(stays))
        def _():
            for device in pair:
                signal(device)
            pl.semaphore_wait(barrier, n + 2)

        @pl.when(stays)
        def _():
            pl.semaphore_wait(barrier, n)

    else:
        pl.semaphore_wait(barrier, n)


def remote(src, dst, send, recv, device):
    if isinstance(device, str):
        device = {device: 1 - lax.axis_index(device)}
    return pltpu.make_async_remote_copy(
        src_ref=src, dst_ref=dst, send_sem=send, recv_sem=recv, device_id=device, device_id_type=MESH
    )


def gather_steps(x_ref, o_ref, local, ss, rs, ready=None):
    ready = ready or (lambda i: None)
    a, core, cl = places()
    half = x_ref.shape[0] // 2
    lo, hi, both = pl.ds(0, half), pl.ds(half, half), pl.ds(0, 2 * half)
    me = index_of(a, core, cl)
    sx = index_of(1 - a, core, cl)
    sy = index_of(a, core, 1 - cl)
    sd = index_of(1 - a, core, 1 - cl)
    other = 2 - 4 * core
    mine = pltpu.make_async_copy(x_ref, o_ref.at[me], local.at[0])

    def put(i, slot, part, name, src=None):
        src = o_ref.at[slot, part] if src is None else src
        return remote(src, o_ref.at[slot, part], ss.at[i], rs.at[i], name)

    sent = [
        put(0, me, lo, "a", x_ref.at[lo]),
        put(1, me, hi, "cl", x_ref.at[hi]),
        put(2, me, hi, "a", x_ref.at[hi]),
        put(3, me, lo, "cl", x_ref.at[lo]),
        put(4, me, both, "core", x_ref),
    ]
    for c in sent:
        c.start()
    mine.start()
    yield
    mine.wait()
    ready(me)

    def on(i, slot, part, name):
        c = put(i, slot, part, name)
        c.start()
        sent.append(c)

    put(0, sx, lo, "a").wait_recv()
    on(5, sx, lo, "cl")
    on(6, sx, lo, "core")
    put(1, sy, hi, "cl").wait_recv()
    on(7, sy, hi, "a")
    on(8, sy, hi, "core")
    put(4, me + other, both, "core").wait_recv()
    ready(me + other)
    yield
    put(2, sx, hi, "a").wait_recv()
    on(9, sx, hi, "core")
    put(3, sy, lo, "cl").wait_recv()
    on(10, sy, lo, "core")
    ready(sx)
    ready(sy)
    yield
    for i, slot, part in ((6, sx, lo), (9, sx, hi)):
        put(i, slot + other, part, "core").wait_recv()
    ready(sx + other)
    put(5, sd, lo, "cl").wait_recv()
    on(11, sd, lo, "core")
    put(7, sd, hi, "a").wait_recv()
    on(12, sd, hi, "core")
    yield
    for i, slot, part in ((8, sy, hi), (10, sy, lo)):
        put(i, slot + other, part, "core").wait_recv()
    ready(sy + other)
    ready(sd)
    for i, slot, part in ((11, sd, lo), (12, sd, hi)):
        put(i, slot + other, part, "core").wait_recv()
    ready(sd + other)
    for c in sent:
        c.wait_send()


def add_rows(dst, sources, n):
    @pl.loop(0, n // TILE)
    def _(i):
        part = pl.ds(pl.multiple_of(i * TILE, TILE), TILE)
        total = sources[0][part, :].astype(F32)
        for s in sources[1:]:
            total = total + s[part, :].astype(F32)
        dst[part, :] = total.astype(dst.dtype)


def plane_chips():
    a, _, cl = places()
    return (a, cl), (1 - a, cl), (a, 1 - cl), (1 - a, 1 - cl)


def sum_steps(x_ref, o_ref, mine, theirs, first, last, lsem, cs, cr, ss, rs):
    core = lax.axis_index("core")
    out, loc = {}, {}
    for p in (3, 1, 2, 0):
        ca, cc = plane_chips()[p]
        out[p] = remote(x_ref.at[index_of(ca, 1 - core, cc)], theirs.at[p], cs.at[p], cr.at[p], "core")
        out[p].start()
        loc[p] = pltpu.make_async_copy(x_ref.at[index_of(ca, core, cc)], mine.at[p], lsem.at[p])
        loc[p].start()
    yield
    yield from sum_rest(o_ref, mine, theirs, first, last, lsem, out, loc, ss, rs)


def sum_rest(o_ref, mine, theirs, first, last, lsem, out, loc, ss, rs, make=None):
    rows = mine.shape[1]
    half = rows // 2
    lo, hi = pl.ds(0, half), pl.ds(half, half)

    def chip_sum(p):
        if make is not None:
            make(p)
        out[p].wait_recv()
        if p in loc:
            loc[p].wait()
        add_rows(mine.at[p], (mine.at[p], theirs.at[p]), rows)

    chip_sum(3)
    xd = remote(mine.at[3, lo], first.at[0], ss.at[0], rs.at[0], "a")
    yd = remote(mine.at[3, hi], first.at[1], ss.at[1], rs.at[1], "cl")
    xd.start()
    yd.start()
    chip_sum(1)
    xo = remote(mine.at[1, lo], first.at[2], ss.at[2], rs.at[2], "a")
    xo.start()
    chip_sum(2)
    yo = remote(mine.at[2, hi], first.at[3], ss.at[3], rs.at[3], "cl")
    yo.start()
    chip_sum(0)
    yield
    xd.wait_recv()
    add_rows(mine.at[2, lo], (mine.at[2, lo], first.at[0]), half)
    y2 = remote(mine.at[2, lo], last.at[0], ss.at[4], rs.at[4], "cl")
    y2.start()
    yd.wait_recv()
    add_rows(mine.at[1, hi], (mine.at[1, hi], first.at[1]), half)
    x2 = remote(mine.at[1, hi], last.at[1], ss.at[5], rs.at[5], "a")
    x2.start()
    yield
    xo.wait_recv()
    add_rows(mine.at[0, lo], (mine.at[0, lo], first.at[2]), half)
    yo.wait_recv()
    add_rows(mine.at[0, hi], (mine.at[0, hi], first.at[3]), half)
    yield
    y2.wait_recv()
    add_rows(mine.at[0, lo], (mine.at[0, lo], last.at[0]), half)
    x2.wait_recv()
    add_rows(mine.at[0, hi], (mine.at[0, hi], last.at[1]), half)
    done = pltpu.make_async_copy(mine.at[0], o_ref, lsem.at[4])
    done.start()
    for c in (*out.values(), xd, yd, xo, yo, y2, x2):
        c.wait_send()
    done.wait()


def swap_steps(kind, pieces, src, dst, lsem, ss, rs):
    me = index_of(*places())
    copies = []
    for p in range(pieces):

        def block(f, p=p):
            return ((f // 2) * pieces + p) * 2 + lax.rem(f, 2) if pieces > 1 else f

        width = (dst if kind == "cols" else src).shape[-1] // pieces

        def cut(ref, i, width=width):
            return ref.at[:, pl.ds(pl.multiple_of(i * width, width), width)]

        def part(ref, i, p=p, width=width):
            return ref.at[i] if pieces == 1 else ref.at[i, :, pl.ds(p * width, width)]

        def source(f, block=block, cut=cut, part=part):
            return cut(src, block(f)) if kind == "cols" else part(src, f)

        target = cut(dst, block(me)) if kind == "back" else part(dst, me)
        for t, (device, index) in enumerate(partners()):
            copies.append(remote(source(index), target, ss.at[p, t], rs.at[p, t], device))
            copies[-1].start()
        copies.append(pltpu.make_async_copy(source(me), target, lsem.at[p]))
        copies[-1].start()
    yield
    yield
    yield
    yield
    for copy in copies:
        copy.wait()


def move_steps(nz, back, src, dst, lsem, ss, rs):
    pair, stays = move_pair(nz, back)
    mine = pltpu.make_async_copy(src, dst, lsem.at[0])
    away = remote(src, dst, ss.at[0], rs.at[0], pair[0])
    pl.when(stays)(mine.start)
    pl.when(jnp.logical_not(stays))(away.start)
    yield
    yield
    yield
    yield
    pl.when(stays)(mine.wait)
    pl.when(jnp.logical_not(stays))(away.wait)


def up_steps(nz, x_ref, o_ref, lsem, ss, rs):
    z = lax.axis_index("cm")
    mine = pltpu.make_async_copy(x_ref, o_ref.at[z], lsem.at[0])
    mine.start()

    def send(j, src):
        return remote(src, o_ref.at[j], ss.at[j], rs.at[j], {"cm": jnp.minimum(z + 1, nz - 1)})

    @pl.when(z < nz - 1)
    def _():
        send(z, x_ref).start()

    yield
    for i in range(1, nz):

        @pl.when(z >= i)
        def _(i=i):
            j = z - i
            send(j, o_ref.at[j]).wait_recv()

            @pl.when(z < nz - 1)
            def _():
                send(j, o_ref.at[j]).start()

        yield
    for i in range(nz):

        @pl.when(jnp.logical_and(z >= i, z < nz - 1))
        def _(i=i):
            send(z - i, x_ref).wait_send()

    mine.wait()


def pass_steps(src, dst, lsem):
    copy = pltpu.make_async_copy(src, dst, lsem.at[0])
    copy.start()
    yield
    yield
    yield
    copy.wait()


def down_steps(nz, x_ref, o_ref, mine, came, lsem, ss, rs):
    z = lax.axis_index("cm")
    rows = x_ref.shape[1]

    def load(j):
        return pltpu.make_async_copy(x_ref.at[j], mine.at[j], lsem.at[j])

    def send(j):
        return remote(mine.at[j], came.at[j], ss.at[j], rs.at[j], {"cm": jnp.maximum(z - 1, 0)})

    for j in range(nz):
        pl.when(z >= j)(lambda j=j: load(j).start())

    ends = [0, 1, 2, nz]
    for first, end in zip(ends, ends[1:]):

        @pl.when(z == nz - 1)
        def _(first=first, end=end):
            for j in range(first, end):
                load(j).wait()
                if j < nz - 1:
                    send(j).start()

        yield
    for j in range(nz - 1):

        @pl.when(jnp.logical_and(z >= j, z < nz - 1))
        def _(j=j):
            load(j).wait()
            send(j).wait_recv()
            add_rows(mine.at[j], (mine.at[j], came.at[j]), rows)
            pl.when(z > j)(send(j).start)

    yield
    done = pltpu.make_async_copy(mine.at[z], o_ref, lsem.at[nz])
    done.start()
    for j in range(nz):
        pl.when(z > j)(lambda j=j: send(j).wait_send())
    done.wait()


def reduce_steps(nz, x_ref, o_ref, mine, above, below, lsem, us, ur, ds, dr):
    z = lax.axis_index("cm")
    rows = x_ref.shape[1]

    def load(j):
        return pltpu.make_async_copy(x_ref.at[j], mine.at[j], lsem.at[j])

    def down(j):
        return remote(mine.at[j], above.at[j], ds.at[j], dr.at[j], {"cm": jnp.maximum(z - 1, 0)})

    def up(j):
        return remote(mine.at[j], below.at[j], us.at[j], ur.at[j], {"cm": jnp.minimum(z + 1, nz - 1)})

    for j in range(nz):
        load(j).start()
    for j in range(nz):
        load(j).wait()

    @pl.when(z == nz - 1)
    def _():
        for j in range(nz - 1):
            down(j).start()

    @pl.when(z == 0)
    def _():
        for j in range(nz - 1, 0, -1):
            up(j).start()

    yield
    yield

    def pass_down():
        for j in range(nz - 1):

            @pl.when(jnp.logical_and(z > j, z < nz - 1))
            def _(j=j):
                down(j).wait_recv()
                add_rows(mine.at[j], (mine.at[j], above.at[j]), rows)
                down(j).start()

    def pass_up():
        for j in range(nz - 1, 0, -1):

            @pl.when(jnp.logical_and(z < j, z > 0))
            def _(j=j):
                up(j).wait_recv()
                add_rows(mine.at[j], (mine.at[j], below.at[j]), rows)
                up(j).start()

    low = 2 * z < nz - 1
    pl.when(low)(pass_up)
    pl.when(jnp.logical_not(low))(pass_down)
    yield
    pl.when(low)(pass_down)
    pl.when(jnp.logical_not(low))(pass_up)
    yield
    for j in range(nz):

        @pl.when(z == j)
        def _(j=j):
            if j < nz - 1:
                down(j).wait_recv()
                add_rows(mine.at[j], (mine.at[j], above.at[j]), rows)
            if j > 0:
                up(j).wait_recv()
                add_rows(mine.at[j], (mine.at[j], below.at[j]), rows)
            done = pltpu.make_async_copy(mine.at[j], o_ref, lsem.at[nz])
            done.start()
            done.wait()

    for j in range(nz):
        pl.when(z > j)(lambda j=j: down(j).wait_send())
        pl.when(z < j)(lambda j=j: up(j).wait_send())


def row_loads(nz, src, dst, sems):
    run = dst.shape[0] // (4 * nz)
    copies = []
    for c in range(4 * nz):
        at = c % nz * (src.shape[0] // nz) + c // nz * run
        copies.append(pltpu.make_async_copy(src.at[pl.ds(at, run)], dst.at[pl.ds(c * run, run)], sems.at[c]))
    return copies


def back_steps(nz, r, hid_ref, one_ref, two_ref, wone_ref, wtwo_ref, o_ref, out_ref, *scratch):
    hid, g, w, out, stage, theirs, first, last, gsem, wsem, osem, lsem, cs, cr, ss, rs = scratch
    tiles, _, wide = hid.shape
    run = 2 * r
    per = wide // run
    core = lax.axis_index("core")
    rows, width = theirs.shape[1:]
    loads = [pltpu.make_async_copy(one_ref, g.at[0], gsem.at[0]), pltpu.make_async_copy(two_ref, g.at[1], gsem.at[1])]
    loads += row_loads(nz, wone_ref, w.at[0], wsem.at[0]) + row_loads(nz, wtwo_ref, w.at[1], wsem.at[1])
    later = [
        pltpu.make_async_copy(hid_ref.at[:, pl.ds(i * wide, wide)], hid.at[i], gsem.at[2 + i]) for i in range(tiles)
    ]
    for c in loads + later:
        c.start()
    for c in loads:
        c.wait()

    def blocks(p):
        ca, cc = plane_chips()[p]

        @pl.loop(0, 2)
        def _(n):
            to = jnp.where(n == 0, 1 - core, core)
            first_row = pl.multiple_of(index_of(ca, to, cc) * rows, rows)
            for c in range(0, width, width // 2):
                part = pl.ds(c, width // 2)
                e = dot(g[0, pl.ds(first_row, rows), :], w[0, part, :], 1, 1)
                e += dot(g[1, pl.ds(first_row, rows), :], w[1, part, :], 1, 1)
                stage[n, p, :, part] = e.astype(BF)

            @pl.when(n == 0)
            def _():
                out_core[p].start()

    out_core = {p: remote(stage.at[0, p], theirs.at[p], cs.at[p], cr.at[p], "core") for p in range(4)}

    def store(i, p):
        chunk = i * per + p
        at = (lax.rem(chunk, nz) * 4 + chunk // nz) * run
        return pltpu.make_async_copy(
            out.at[i, pl.ds(p * run, run)], out_ref.at[pl.ds(pl.multiple_of(at, run), run)], osem.at[i, p]
        )

    def products(lo, hi):
        @pl.loop(lo, hi)
        def _(i):
            out[i] = dot(hid[i], g[0], 0, 0).astype(BF)
            for p in range(per):
                store(i, p).start()

    summing = sum_rest(o_ref, stage.at[1], theirs, first, last, lsem, out_core, {}, ss, rs, blocks)
    for n in range(4):
        next(summing, None)
        if n == 0:
            for c in later:
                c.wait()
        products(n * tiles // 4, (n + 1) * tiles // 4)
    for _ in summing:
        pass

    @pl.loop(0, tiles)
    def _(i):
        for p in range(per):
            store(i, p).wait()

    yield


def forward_steps(nz, x_ref, wone_ref, wtwo_ref, low_ref, all_ref, gate_ref, up_ref, in_ref, *rest):
    g_refs, scratch = rest[:2], rest[2:]
    buf, w, low, inner, stage, out, wsem, asem, gsem, osem, local, ss, rs = scratch
    rows = buf.shape[1]
    loads = row_loads(nz, wone_ref, w.at[0], wsem.at[0]) + row_loads(nz, wtwo_ref, w.at[1], wsem.at[1])
    load_low = pltpu.make_async_copy(low_ref, low, osem.at[0])
    done = []

    def keep(src, dst, sem):
        done.append(pltpu.make_async_copy(src, dst, sem))
        done[-1].start()

    def ready(i):
        n = len(done) // 4
        if n == 0:
            for c in loads:
                c.wait()
        block = buf[i]
        part = pl.ds(pl.multiple_of(i * rows, rows), rows)
        gate = dot(block, w[0])
        up = dot(block, w[1])
        stage[n, 0] = gate
        stage[n, 1] = up
        inner[part, :] = (gate * jax.nn.sigmoid(gate) * up).astype(BF)
        keep(buf.at[i], all_ref.at[i], asem.at[n])
        keep(stage.at[n, 0], gate_ref.at[part], gsem.at[n, 0])
        keep(stage.at[n, 1], up_ref.at[part], gsem.at[n, 1])
        keep(inner.at[part], in_ref.at[part], gsem.at[n, 2])

    first = gather_steps(x_ref, buf, local, ss, rs, ready)
    next(first)
    for c in (*loads, load_low):
        c.start()
    for _ in first:
        pass
    load_low.wait()
    tiles, wide, width = out.shape
    half = width // 2

    def store(t, n):
        return pltpu.make_async_copy(
            out.at[t, :, pl.ds(n * half, half)], g_refs[n].at[pl.ds(t * wide, wide)], osem.at[1 + t * 2 + n]
        )

    for t in range(tiles):
        left = inner[:, t * wide : (t + 1) * wide]
        for n in range(2):
            out[t, :, n * half : (n + 1) * half] = dot(left, low[:, n * half : (n + 1) * half], 0, 0).astype(BF)
            store(t, n).start()
    for t in range(tiles):
        for n in range(2):
            store(t, n).wait()
    for c in done:
        c.wait()
    yield


def product_steps(a_ref, left_ref, right_ref, o_ref, a, b, out, lsem, osem):
    half = b.shape[1] // 2
    tiles, rows, _ = out.shape
    loads = [
        pltpu.make_async_copy(a_ref, a, lsem.at[0]),
        pltpu.make_async_copy(left_ref, b.at[:, pl.ds(0, left_ref.shape[1])], lsem.at[1]),
        pltpu.make_async_copy(right_ref, b.at[:, pl.ds(left_ref.shape[1], right_ref.shape[1])], lsem.at[2]),
    ]
    for c in loads:
        c.start()
    for c in loads:
        c.wait()

    def store(i):
        return pltpu.make_async_copy(out.at[i], o_ref.at[pl.ds(pl.multiple_of(i * rows, rows), rows)], osem.at[i])

    for lo, hi in ((0, tiles // 2), (tiles // 2, tiles)):

        @pl.loop(lo, hi)
        def _(i):
            left = a[pl.ds(pl.multiple_of(i * rows, rows), rows), :]
            for c in (0, half):
                out[i, :, c : c + half] = dot(left, b[:, c : c + half]).astype(BF)
            store(i).start()

        yield

    @pl.loop(0, tiles)
    def _(i):
        store(i).wait()


def heads_steps(x_ref, wo_ref, low_ref, heads_ref, g_ref, buf, wo, low, heads, total, g, lsem, local, ss, rs):
    loads = [pltpu.make_async_copy(wo_ref, wo, lsem.at[0]), pltpu.make_async_copy(low_ref, low, lsem.at[1])]
    for c in loads:
        c.start()
    rows = buf.shape[1]
    seen_blocks = []

    def ready(i):
        if not seen_blocks:
            for c in loads:
                c.wait()
            total[...] = jnp.zeros_like(total)
        seen_blocks.append(i)
        block = buf[i]
        part = pl.ds(pl.multiple_of(i * rows, rows), rows)
        heads[part, :] = dot(block, wo[...], 1, 1).astype(BF)
        total[...] += dot(low[part, :], block, 0, 0)

    yield from gather_steps(x_ref, buf, local, ss, rs, ready)
    g[...] = total[...].astype(BF)
    stores = [pltpu.make_async_copy(heads, heads_ref, lsem.at[2]), pltpu.make_async_copy(g, g_ref, lsem.at[3])]
    for c in stores:
        c.start()
    for c in stores:
        c.wait()


def part(kind, *xs, **how):
    nz = lax.axis_size("cm")
    x = xs[0]
    like = lambda *shape: jax.ShapeDtypeStruct(shape, x.dtype)
    vmem = lambda *shape: pltpu.VMEM(shape, x.dtype)
    if kind == "gather":
        rows, cols = x.shape
        return kind, gather_steps, xs, [like(8, rows, cols)], [dma(1), dma(13), dma(13)]
    if kind == "sum":
        rows, cols = x.shape[0] // 8, x.shape[1]
        scratch = [vmem(n, m, cols) for n, m in ((4, rows), (4, rows), (4, rows // 2), (2, rows // 2))]
        scratch += [dma(5), dma(4), dma(4), dma(6), dma(6)]
        return kind, sum_steps, [x.reshape(8, rows, cols)], [like(rows, cols)], scratch
    if kind == "up":
        return kind, functools.partial(up_steps, nz), xs, [like(nz, *x.shape)], [dma(1), dma(nz), dma(nz)]
    if kind == "pass":
        return kind, pass_steps, xs, [like(*x.shape)], [dma(1)]
    if kind == "down":
        scratch = [vmem(*x.shape)] * 2 + [dma(nz + 1), dma(nz), dma(nz)]
        return kind, functools.partial(down_steps, nz), xs, [like(*x.shape[1:])], scratch
    if kind == "reduce":
        scratch = [vmem(*x.shape)] * 3 + [dma(nz + 1)] + [dma(nz)] * 4
        return kind, functools.partial(reduce_steps, nz), xs, [like(*x.shape[1:])], scratch
    if kind in ("move", "home"):
        return kind, functools.partial(move_steps, nz, kind == "home"), xs, [like(*x.shape)], [dma(1), dma(1), dma(1)]
    if kind == "mlp":
        rows, width = x.shape
        cols = xs[1].shape[1]
        r = width // (8 * nz)
        wide = 256
        tiles = width // wide
        block = rows // 8
        scratch = [vmem(tiles, rows, wide), vmem(2, rows, cols), vmem(2, width, cols), vmem(tiles, wide, cols)]
        scratch += [vmem(2, 4, block, width), vmem(4, block, width), vmem(4, block // 2, width)]
        scratch += [vmem(2, block // 2, width), dma(2 + tiles), dma(2, 4 * nz), dma(tiles, wide // (2 * r))]
        scratch += [dma(5), dma(4), dma(4), dma(6), dma(6)]
        return kind, functools.partial(back_steps, nz, r), xs, [like(block, width), like(width, cols)], scratch
    if kind == "forward":
        rows, width = x.shape
        cols = xs[1].shape[1]
        wide = min(256, cols)
        tiles = cols // wide
        full = [jax.ShapeDtypeStruct((8 * rows, cols), F32)] * 2
        outs = [like(8, rows, width), *full, like(8 * rows, cols), *[like(cols, width // 2)] * 2]
        scratch = [vmem(8, rows, width), vmem(2, width, cols), vmem(8 * rows, width), vmem(8 * rows, cols)]
        scratch += [pltpu.VMEM((8, 2, rows, cols), F32), vmem(tiles, wide, width)]
        scratch += [dma(2, 4 * nz), dma(8), dma(8, 3), dma(1 + 2 * tiles), dma(1), dma(13), dma(13)]
        return kind, functools.partial(forward_steps, nz), xs, outs, scratch
    if kind == "product":
        rows, cols = x.shape[0], xs[1].shape[1] + xs[2].shape[1]
        scratch = [vmem(*x.shape), vmem(x.shape[1], cols), vmem(8, rows // 8, cols), dma(3), dma(8)]
        return kind, product_steps, xs, [like(rows, cols)], scratch
    if kind == "heads":
        rows, cols = x.shape
        wide = xs[1].shape[0]
        scratch = [vmem(8, rows, cols), vmem(wide, cols), vmem(8 * rows, wide), vmem(8 * rows, wide)]
        scratch += [pltpu.VMEM((wide, cols), F32), vmem(wide, cols), dma(4), dma(1), dma(13), dma(13)]
        return kind, heads_steps, xs, [like(8 * rows, wide), like(wide, cols)], scratch
    pieces = how.get("pieces", 1)
    shape = x.shape
    if kind == "cols":
        shape = (8, x.shape[0], x.shape[1] // 8)
    elif kind == "back":
        shape = (x.shape[1], 8 * x.shape[2])
    scratch = [dma(pieces), dma(pieces, 7), dma(pieces, 7)]
    return kind, functools.partial(swap_steps, kind, pieces), xs, [like(*shape)], scratch


def transfer(cid, parts, deps=()):
    nz = lax.axis_size("cm")
    kinds = [p[0] for p in parts]
    operands = [x for p in parts for x in p[2]]
    results = [o for p in parts for o in p[3]]
    moves = [k == "home" for k in kinds if k in ("move", "home")]
    whole = any(k in ("slab", "cols", "back") for k in kinds)
    line = any(k in ("up", "down", "reduce") for k in kinds)

    def kernel(*refs):
        ins = list(refs[: len(operands)])
        rest = list(refs[len(operands) + len(deps) :])
        outs, scratch = rest[: len(results)], rest[len(results) :]

        def take(refs, n):
            out = refs[:n]
            del refs[:n]
            return out

        greet(whole, line, moves[0] if moves else None, nz)
        running = []
        for _, steps, xs, shapes, own in parts:
            running.append(steps(*take(ins, len(xs)), *take(outs, len(shapes)), *take(scratch, len(own))))
        while running:
            still = []
            for steps in running:
                try:
                    next(steps)
                except StopIteration:
                    continue
                still.append(steps)
            running = still

    return pl.pallas_call(
        kernel,
        out_shape=results,
        in_specs=[ANY] * (len(operands) + len(deps)),
        out_specs=[ANY] * len(results),
        scratch_shapes=[s for p in parts for s in p[4]],
        compiler_params=pltpu.CompilerParams(
            collective_id=cid, has_side_effects=True, vmem_limit_bytes=60 * MIB
        ),
        name="_".join(kinds) + str(cid),
    )(*operands, *deps)


def after(x, deps):
    return pl.pallas_call(
        lambda *refs: None,
        out_shape=jax.ShapeDtypeStruct(x.shape, x.dtype),
        in_specs=[ANY] * (1 + len(deps)),
        out_specs=ANY,
        input_output_aliases={0: 0},
        name="after",
    )(x, *deps)


def sum_planes(g):
    return lax.psum_scatter(g, "cm", scatter_dimension=0, tiled=True)


def gather_planes(x):
    return lax.all_gather(x, "cm", axis=0, tiled=True)


def dot(a, b, left=1, right=0):
    return lax.dot_general(a, b, (((left,), (right,)), ((), ())), preferred_element_type=F32)


def rope(u, cos, sin):
    width = u.shape[-1]
    lane = lax.broadcasted_iota(jnp.int32, u.shape, 1)
    other = jnp.where(lane % HD < HD // 2, pltpu.roll(u, width - HD // 2, 1), pltpu.roll(u, HD // 2, 1))
    return u * cos + other * sin


def tables(positions):
    lane = jnp.arange(2 * HD)
    frequency = 500000.0 ** (-(lane % (HD // 2)).astype(F32) * 2.0 / HD)
    angles = positions.astype(F32)[..., None] * frequency
    return jnp.cos(angles), jnp.where(lane % HD < HD // 2, -1.0, 1.0) * jnp.sin(angles)


def project_kernel(x_ref, gain_ref, w_ref, cos_ref, sin_ref, hid_ref, q_ref, kv_ref):
    x = x_ref[...].astype(F32)
    hid = (x * lax.rsqrt(jnp.mean(x * x, -1, keepdims=True) + EPSILON) * gain_ref[...]).astype(BF)
    hid_ref[...] = hid
    u = dot(hid, w_ref[...])
    times = x.shape[0] // cos_ref.shape[1]
    cos = jnp.concatenate([cos_ref[0]] * times, 0)
    sin = jnp.concatenate([sin_ref[0]] * times, 0)
    wide = q_ref.shape[-1]
    copies = wide // (2 * HD)
    q_ref[...] = rope(u[:, :wide], jnp.concatenate([cos] * copies, 1), jnp.concatenate([sin] * copies, 1)).astype(BF)
    kv = u[:, wide:]
    lane = lax.broadcasted_iota(jnp.int32, kv.shape, 1)
    kv_ref[...] = jnp.where(lane < HD, rope(kv, cos, sin), kv).astype(BF)


def project(x, gain, w, wide, cos, sin):
    rows, width = x.shape
    step = rows // 8
    block = cos.shape[1]
    table = pl.BlockSpec((1, block, 2 * HD), lambda g: (g % 2, 0, 0))
    return pl.pallas_call(
        project_kernel,
        grid=(8,),
        out_shape=[jax.ShapeDtypeStruct((rows, c), BF) for c in (width, wide, 2 * HD)],
        in_specs=[
            pl.BlockSpec((step, width), lambda g: (g, 0)),
            pl.BlockSpec((1, width), lambda g: (0, 0)),
            pl.BlockSpec((width, wide + 2 * HD), lambda g: (0, 0)),
            table,
            table,
        ],
        out_specs=[pl.BlockSpec((step, c), lambda g: (g, 0)) for c in (width, wide, 2 * HD)],
        compiler_params=pltpu.CompilerParams(vmem_limit_bytes=48 * MIB),
        name="project",
    )(x, gain, w, cos, sin)


def project_back_kernel(dq_ref, dkv_ref, hid_ref, w_ref, cos_ref, sin_ref, *rest):
    e_ref, g_ref, total = rest[-3:]
    step = pl.program_id(0)

    @pl.when(step == 0)
    def _():
        total[...] = jnp.zeros_like(total)

    dq = dq_ref[...]
    times = dq.shape[0] // cos_ref.shape[1]
    cos = jnp.concatenate([cos_ref[0]] * times, 0)
    sin = -jnp.concatenate([sin_ref[0]] * times, 0)
    copies = dq.shape[1] // (2 * HD)
    dq = rope(dq, jnp.concatenate([cos] * copies, 1), jnp.concatenate([sin] * copies, 1))
    dkv = dkv_ref[...].astype(F32)
    lane = lax.broadcasted_iota(jnp.int32, dkv.shape, 1)
    dkv = jnp.where(lane < HD, rope(dkv, cos, sin), dkv)
    rows = jnp.concatenate([dq.astype(BF), dkv.astype(BF)], 1)
    e_ref[...] = dot(rows, w_ref[...], 1, 1).astype(BF)
    total[...] += dot(hid_ref[...], rows, 0, 0)

    @pl.when(step == pl.num_programs(0) - 1)
    def _():
        g_ref[...] = total[...].astype(BF)


def project_back(dq, dkv, hid, w, cos, sin, deps):
    rows, width = hid.shape
    step = rows // 8
    shape = (width, dq.shape[1] + 2 * HD)
    block = cos.shape[1]
    table = pl.BlockSpec((1, block, 2 * HD), lambda g: (g % 2, 0, 0))
    return pl.pallas_call(
        project_back_kernel,
        grid=(8,),
        out_shape=[jax.ShapeDtypeStruct((rows, width), BF), jax.ShapeDtypeStruct(shape, BF)],
        in_specs=[
            pl.BlockSpec((step, dq.shape[1]), lambda g: (g, 0)),
            pl.BlockSpec((step, 2 * HD), lambda g: (g, 0)),
            pl.BlockSpec((step, width), lambda g: (g, 0)),
            pl.BlockSpec(shape, lambda g: (0, 0)),
            table,
            table,
        ]
        + [ANY] * len(deps),
        out_specs=[pl.BlockSpec((step, width), lambda g: (g, 0)), pl.BlockSpec(shape, lambda g: (0, 0))],
        scratch_shapes=[pltpu.VMEM(shape, F32)],
        compiler_params=pltpu.CompilerParams(vmem_limit_bytes=48 * MIB),
        name="project_back",
    )(dq, dkv, hid, w, cos, sin, *deps)


def inner_back_kernel(nz, r, low_ref, gate_ref, up_ref, wl_ref, wr_ref, hid_ref, gg_ref, gu_ref, out_ref, hid, gu, sems):
    step = pl.program_id(0)
    tiles, _, wide = hid.shape
    loads = [
        pltpu.make_async_copy(hid_ref.at[:, pl.ds(i * wide, wide)], hid.at[i], sems.at[i]) for i in range(tiles)
    ]

    @pl.when(step == 0)
    def _():
        for c in loads:
            c.start()

    half = wl_ref.shape[1]
    inner = dot(low_ref[:, :half], wl_ref[...], 1, 1) + dot(low_ref[:, half:], wr_ref[...], 1, 1)
    inner = inner.astype(BF).astype(F32)
    gate = gate_ref[...]
    sig = jax.nn.sigmoid(gate)
    act = gate * sig
    gg_ref[...] = (inner * up_ref[...] * (sig * (1.0 + gate * (1.0 - sig)))).astype(BF)
    up = (inner * act).astype(BF)
    gu_ref[...] = up
    rows = up.shape[0]
    gu[pl.ds(pl.multiple_of(step * rows, rows), rows), :] = up

    @pl.when(step == pl.num_programs(0) - 1)
    def _():
        for c in loads:
            c.wait()
        run = 2 * r
        per = wide // run

        @pl.loop(0, tiles)
        def _(i):
            product = dot(hid[i], gu[...], 0, 0).astype(BF)
            for p in range(per):
                chunk = i * per + p
                at = (lax.rem(chunk, nz) * 4 + chunk // nz) * run
                out_ref[pl.ds(pl.multiple_of(at, run), run), :] = product[p * run : (p + 1) * run]


def inner_back(low, gate, up, wl, wr, hid):
    nz = lax.axis_size("cm")
    rows, width = low.shape
    cols = gate.shape[1]
    step = rows // 8
    wide = 256
    tiles = width // wide
    block = lambda c: pl.BlockSpec((step, c), lambda g: (g, 0))
    return pl.pallas_call(
        functools.partial(inner_back_kernel, nz, width // (8 * nz)),
        grid=(8,),
        out_shape=[
            jax.ShapeDtypeStruct((rows, cols), BF),
            jax.ShapeDtypeStruct((rows, cols), BF),
            jax.ShapeDtypeStruct((width, cols), BF),
        ],
        in_specs=[block(width), block(cols), block(cols)] + [pl.BlockSpec(w.shape, lambda g: (0, 0)) for w in (wl, wr)] + [ANY],
        out_specs=[block(cols), block(cols), pl.BlockSpec((width, cols), lambda g: (0, 0))],
        scratch_shapes=[pltpu.VMEM((tiles, rows, wide), BF), pltpu.VMEM((rows, cols), BF), dma(tiles)],
        compiler_params=pltpu.CompilerParams(vmem_limit_bytes=60 * MIB),
        name="inner_back",
    )(low, gate, up, wl, wr, hid)


def flat(ref):
    x = ref[...]
    return x.reshape(x.shape[-4] * x.shape[-2], x.shape[-1])


def heads_of(x):
    return [x[:, h * HD : (h + 1) * HD] for h in range(x.shape[1] // HD)]


def seen(n, j, z, slots):
    col = lax.broadcasted_iota(jnp.int32, (slots, slots), 0) + j * slots
    row = lax.broadcasted_iota(jnp.int32, (slots, slots), 1) + z * slots
    return jnp.logical_and(col <= row, col < n)


def attend_kernel(lens, q_ref, kv_ref, att_ref, low_ref, log_ref, scores, top, sums, acc):
    z = lax.axis_index("cm")
    n = lens[pl.program_id(0) * pl.num_programs(1) + pl.program_id(1)]
    q = flat(q_ref)
    slots = q.shape[0]
    qs = heads_of((q.astype(F32) * HD ** (-0.5)).astype(BF))
    top[...] = jnp.full_like(top, NEGATIVE)
    sums[...] = jnp.zeros_like(sums)
    acc[...] = jnp.zeros_like(acc)

    def score(j, _):
        k = flat(kv_ref.at[j])[:, :HD]
        mask = seen(n, j, z, slots)
        for h, qh in enumerate(qs):
            s = jnp.where(mask, dot(k, qh, 1, 1), NEGATIVE)
            scores[j, h] = s
            top[h : h + 1] = jnp.maximum(top[h : h + 1], jnp.max(s, 0, keepdims=True))
        return 0

    blocks = jnp.minimum(z + 1, (n + slots - 1) // slots)
    lax.fori_loop(0, blocks, score, 0)

    def weigh(j, _):
        v = flat(kv_ref.at[j])[:, HD:]
        for h in range(len(qs)):
            p = jnp.exp(scores[j, h] - top[h : h + 1])
            sums[h : h + 1] += jnp.sum(p, 0, keepdims=True)
            acc[h * HD : (h + 1) * HD] += dot(v, p.astype(BF), 0, 0)
        return 0

    lax.fori_loop(0, blocks, weigh, 0)
    out = jnp.concatenate([acc[h * HD : (h + 1) * HD] / sums[h : h + 1] for h in range(len(qs))], 0)
    att_ref[0, 0] = out
    low_ref[...] = out.T.astype(BF).reshape(low_ref.shape)
    log_ref[0, 0] = top[...] + jnp.log(sums[...])


def attend_back_kernel(lens, q_ref, kv_ref, do_ref, att_ref, log_ref, *rest):
    dq_ref, dkv_ref, acc = rest[-3:]
    z = lax.axis_index("cm")
    n = lens[pl.program_id(0) * pl.num_programs(1) + pl.program_id(1)]
    q = flat(q_ref)
    slots = q.shape[0]
    qs = heads_of((q.astype(F32) * HD ** (-0.5)).astype(BF))
    do = flat(do_ref)
    dos = heads_of(do)
    both = do.astype(F32).T * att_ref[0, 0]
    deltas = [jnp.sum(both[h * HD : (h + 1) * HD], 0, keepdims=True) for h in range(len(qs))]
    acc[...] = jnp.zeros_like(acc)

    def step(j, _):
        kv = flat(kv_ref.at[j])
        k, v = kv[:, :HD], kv[:, HD:]
        mask = seen(n, j, z, slots)
        dk = jnp.zeros((slots, HD), F32)
        dv = jnp.zeros((slots, HD), F32)
        for h, qh in enumerate(qs):
            s = jnp.where(mask, dot(k, qh, 1, 1), NEGATIVE)
            p = jnp.exp(s - log_ref[0, 0, h : h + 1])
            ds = (p * (dot(v, dos[h], 1, 1) - deltas[h])).astype(BF)
            acc[h * HD : (h + 1) * HD] += dot(k, ds, 0, 0)
            dk += dot(ds, qh)
            dv += dot(p.astype(BF), dos[h])
        out = jnp.concatenate([dk, dv], 1).astype(BF)
        dkv_ref[j] = out.reshape(dkv_ref.shape[1:])
        return 0

    live = jnp.where(z * slots < n, z + 1, 0)
    lax.fori_loop(0, live, step, 0)

    def nothing(j, _):
        dkv_ref[j] = jnp.zeros(dkv_ref.shape[1:], BF)
        return 0

    lax.fori_loop(live, z + 1, nothing, 0)
    dq_ref[...] = (acc[...] * HD ** (-0.5)).T.reshape(dq_ref.shape)


def attention_specs(seqs, block, wide, nz):
    own = lambda c: pl.BlockSpec((1, 2, 1, block, c), lambda f, s: (f, 0, s, 0, 0))
    every = pl.BlockSpec((nz, 1, 2, 1, block, 2 * HD), lambda f, s: (0, f, 0, s, 0, 0))
    turned = lambda c: pl.BlockSpec((1, 1, c, 2 * block), lambda f, s: (f, s, 0, 0))
    return own(wide), every, turned(wide), turned(wide // HD)


def attend(lens, q, kv, seqs, block):
    nz, rows, _ = kv.shape
    wide = q.shape[1]
    heads = wide // HD
    own, every, turned, logs = attention_specs(seqs, block, wide, nz)
    view = (4, 2, seqs, block)
    att, low, log = pl.pallas_call(
        attend_kernel,
        grid=(4, seqs),
        out_shape=[
            jax.ShapeDtypeStruct((4, seqs, wide, 2 * block), F32),
            jax.ShapeDtypeStruct((*view, wide), BF),
            jax.ShapeDtypeStruct((4, seqs, heads, 2 * block), F32),
        ],
        in_specs=[pl.BlockSpec(memory_space=pltpu.SMEM), own, every],
        out_specs=[turned, own, logs],
        scratch_shapes=[
            pltpu.VMEM((nz, heads, 2 * block, 2 * block), F32),
            pltpu.VMEM((heads, 2 * block), F32),
            pltpu.VMEM((heads, 2 * block), F32),
            pltpu.VMEM((wide, 2 * block), F32),
        ],
        compiler_params=pltpu.CompilerParams(vmem_limit_bytes=48 * MIB),
        name="attend",
    )(lens, q.reshape(*view, wide), kv.reshape(nz, *view, 2 * HD))
    return att, low.reshape(rows, wide), log


def attend_back(lens, q, kv, do, att, log, seqs, block, deps):
    nz, rows, _ = kv.shape
    wide = q.shape[1]
    own, every, turned, logs = attention_specs(seqs, block, wide, nz)
    view = (4, 2, seqs, block)
    dq, dkv = pl.pallas_call(
        attend_back_kernel,
        grid=(4, seqs),
        out_shape=[
            jax.ShapeDtypeStruct((*view, wide), F32),
            jax.ShapeDtypeStruct((nz, *view, 2 * HD), BF),
        ],
        in_specs=[pl.BlockSpec(memory_space=pltpu.SMEM), own, every, own, turned, logs] + [ANY] * len(deps),
        out_specs=[own, every],
        scratch_shapes=[pltpu.VMEM((wide, 2 * block), F32)],
        compiler_params=pltpu.CompilerParams(vmem_limit_bytes=48 * MIB),
        name="attend_back",
    )(lens, q.reshape(*view, wide), kv.reshape(nz, *view, 2 * HD), do.reshape(*view, wide), att, log, *deps)
    return dq.reshape(rows, wide), dkv.reshape(nz, rows, 2 * HD)


def rms_scale(field):
    return lax.rsqrt(jnp.mean(field * field, -1, keepdims=True) + EPSILON)


def norm_back(grad_normed, normed, scale_rows):
    return scale_rows * (grad_normed - normed * jnp.mean(grad_normed * normed, -1, keepdims=True))


def rows_first(g):
    nz = lax.axis_size("cm")
    rows, c = g.shape
    r = rows // (8 * nz)
    return g.astype(BF).reshape(4, nz, 2, r, c).transpose(1, 0, 2, 3, 4).reshape(nz * 8, r, c)


def on_device(
    tokens, lengths, cotangent, attn_gain, w_query, w_key, w_value, w_out, mlp_gain, w_gate, w_up, w_down
):
    seqs, block, width = tokens.shape
    nz = lax.axis_size("cm")
    rows = seqs * block
    r = w_query.shape[0]
    wide = HEADS // 8 * HD
    cm = lax.axis_index("cm")
    cl = lax.axis_index("cl")
    gain_two = mlp_gain.astype(F32)[:, None]
    pieces = nz if w_down.shape[0] % 128 == 0 else 1
    perm = [(c, (c % nz) * 2 + c // nz) for c in range(2 * nz)]
    home = [(t, s) for s, t in perm]

    def gained(w):
        return (w.astype(F32) * gain_two).astype(BF)

    down = w_down if pieces > 1 else lax.ppermute(w_down, ("cm", "cl"), perm)
    fb = down.shape[0]
    gains = jnp.pad(attn_gain[None], ((0, 15), (0, width // 4 - r)))
    wd_one = gather_planes(jnp.concatenate([down[:, : width // 4], gains], 0)).reshape(nz, fb + 16, -1)
    gains = jnp.pad(wd_one[:, fb, :r].reshape(-1, 2 * HD), ((0, 32 - nz * r // (2 * HD)), (0, 0)))
    wd_one = wd_one[:, :fb].reshape(nz * fb, -1)
    pack = [w.reshape(r, 8, -1) for w in (w_query, w_key, w_value)]
    pack = jnp.concatenate(pack, -1).transpose(1, 0, 2)
    lens = jnp.broadcast_to(jnp.pad(lengths, (0, 128 - seqs))[None, None], (8, 8, 128))
    pack, lens = transfer(1, [part("slab", pack), part("slab", lens)])
    lens = lens[::2, 0, :seqs].reshape(-1)
    wg, wo = transfer(2, [part("cols", gained(w_gate), pieces=pieces), part("move", w_out)], (pack,))
    ff = wg.shape[2]
    wg = jnp.concatenate([wg.reshape(8 * r, ff), wo.reshape(-1, ff)], 0)
    own = tokens.reshape(rows, width)
    tok_all, wu, gains = transfer(
        3, [part("gather", own), part("cols", gained(w_up), pieces=pieces), part("gather", gains)], (wg,)
    )
    pack = gather_planes(pack).reshape(nz, 4, 2 * r, -1).transpose(1, 0, 2, 3).reshape(width, -1)
    gains = gains[:, : nz * r // (2 * HD)].reshape(4, 2, nz, r).transpose(0, 2, 1, 3)
    gain_row = gains.reshape(1, width).astype(F32)
    wg = gather_planes(wg)
    wo = wg.reshape(nz, -1, ff)[:, 8 * r :].reshape(-1, width)

    slot = cm * 2 * block + jnp.arange(2 * block, dtype=jnp.int32).reshape(2, block)
    cos, sin = tables(slot)
    hidden_one, q, kv = project(tok_all.reshape(8 * rows, width), gain_row, pack, wide, cos, sin)
    own_pos = cm * 2 * block + cl * block + jnp.arange(block, dtype=jnp.int32)
    valid = (own_pos[None, :] < lengths[:, None]).astype(F32)
    grad_out = (cotangent.astype(F32) * valid[..., None]).reshape(rows, width)
    grad_low, kv_all = transfer(
        4,
        [
            part("gather", grad_out.astype(BF)),
            part("up", kv),
        ],
    )
    grad_low = grad_low.reshape(8 * rows, width)
    wu = gather_planes(wu).reshape(width, -1)
    att, att_low, log = attend(lens, q, kv_all, seqs, block)

    resid_in = own.astype(F32)
    mid, down = transfer(5, [part("sum", dot(att_low, wo).astype(BF)), part("pass", down[:, width // 4 :])], (wg,))
    wd_two = gather_planes(down)
    resid_mid = resid_in + mid.astype(F32)
    scale_two = rms_scale(resid_mid)
    normed_two = resid_mid * scale_two
    hidden_two, gate_pre, up_pre, inner, wd_left, wd_right = transfer(
        6, [part("forward", normed_two.astype(BF), wg, wu, grad_low)]
    )
    hidden_two = hidden_two.reshape(8 * rows, width)
    wd_two = after(wd_two, (wd_left,))
    grad_gate, grad_up, grad_wu = inner_back(grad_low, gate_pre, up_pre, wd_one, wd_two, hidden_two)
    e_two, grad_wg = transfer(7, [part("mlp", hidden_two, grad_gate, grad_up, wg, wu)], (grad_wu,))
    by_owner = lambda g: sum_planes(g.reshape(8 * nz, r, -1))
    wd_left, grad_wu, grad_wg = sum_planes(wd_left), by_owner(grad_wu), by_owner(grad_wg)
    grad_mid = grad_out + norm_back(e_two.astype(F32), normed_two, scale_two)
    grad_heads, grad_wo, out_part = transfer(
        8, [part("heads", grad_mid.astype(BF), wo, att_low), part("product", inner, wd_one, wd_two)], (wd_left,)
    )
    dq, dkv = attend_back(lens, q, kv_all, grad_heads, att, log, seqs, block, (grad_wu,))
    dkv, out_sum, grad_wu = transfer(
        9, [part("down", dkv), part("sum", out_part), part("back", grad_wu, pieces=pieces)]
    )
    wd_right = after(wd_right, (dkv,))
    layer_out = (resid_mid + out_sum.astype(F32)).astype(BF)
    e_one, grad_qkv = project_back(dq, dkv, hidden_one, pack, cos, sin, (wd_right,))
    wd_right = sum_planes(wd_right)
    grad_qkv, e_one, grad_wg = transfer(
        10,
        [
            part("reduce", rows_first(grad_qkv).reshape(nz, 8 * r, -1)),
            part("sum", e_one),
            part("back", grad_wg, pieces=pieces),
        ],
    )
    grad_wo = sum_planes(grad_wo)
    grad_qkv = grad_qkv.reshape(8, r, -1)
    scale_one = rms_scale(resid_in)
    grad_tokens = grad_mid + norm_back(e_one.astype(F32) * gain_row, resid_in * scale_one, scale_one)
    grad_qkv, grad_wo = transfer(11, [part("slab", grad_qkv), part("home", grad_wo)], (e_one,))
    grad_wd = jnp.concatenate([wd_left, wd_right], 1)
    if pieces == 1:
        grad_wd = lax.ppermute(grad_wd, ("cm", "cl"), home)
    grad_qkv = grad_qkv.transpose(1, 0, 2).astype(F32)
    grad_wq = grad_qkv[..., :wide].reshape(r, 8 * wide)
    grad_wk = grad_qkv[..., wide : wide + HD].reshape(r, 8 * HD)
    grad_wv = grad_qkv[..., wide + HD :].reshape(r, 8 * HD)
    grad_wg, grad_wu = grad_wg.astype(F32), grad_wu.astype(F32)

    def gain_grad(pairs):
        return sum(jnp.sum(w.astype(F32) * g, -1) for w, g in pairs)

    gain_grad_one = gain_grad(((w_query, grad_wq), (w_key, grad_wk), (w_value, grad_wv))) / attn_gain.astype(F32)
    gain_grad_two = gain_grad(((w_gate, grad_wg), (w_up, grad_wu)))
    return (
        layer_out.reshape(seqs, block, width),
        grad_tokens.reshape(seqs, block, width).astype(BF),
        gain_grad_one,
        grad_wq,
        grad_wk,
        grad_wv,
        grad_wo.astype(F32),
        gain_grad_two,
        grad_wg * gain_two,
        grad_wu * gain_two,
        grad_wd.astype(F32),
    )


def solution(mesh):
    fsdp, ctx = mesh.devices.shape
    fine = Mesh(mesh.devices.reshape(fsdp // 2, 2, ctx // 2, 2), ("a", "core", "cm", "cl"))
    token = P(("a", "core"), ("cm", "cl"), None)
    vector = P(("a", "core", "cm", "cl"))
    matrix = P(("a", "core", "cm", "cl"), None)
    return jax.shard_map(
        on_device,
        mesh=fine,
        in_specs=(
            token,
            P(("a", "core")),
            token,
            vector,
            matrix,
            matrix,
            matrix,
            matrix,
            vector,
            matrix,
            matrix,
            matrix,
        ),
        out_specs=(token, token, vector, matrix, matrix, matrix, matrix, vector, matrix, matrix, matrix),
        check_vma=False,
    )
```
